32 devices in a mesh: group: 2 (over y), train: 16 (over z, x, core), layer: 1.
Axes of the slice: x: 2, y: 2, z: 4, core: 2. Of those that a mesh axis runs over, the one named last changes fastest.
Arguments:
- train_grads: bfloat16 [16384, 2, 4096], P(('group', 'train'), 'layer'), parts along dimension 0, may hold values from -6 to 6
- query_grads: bfloat16 [256, 2, 4096], P('train', 'layer'), may hold values from -0.0625 to 0.0625
- basis_in: float32 [2, 64, 64], P('layer'), may hold values from -0.75 to 0.75
- basis_out: float32 [2, 64, 64], P('layer'), may hold values from -0.75 to 0.75
- eigvals: float32 [2, 4096], P('layer'), may hold values from 0.2 to 5
Outputs:
- scores: float32 [16384, 256], P(('group', 'train'), 'layer'), parts along dimension 0
The draws below stay inside these ranges and needn't reach their ends.
There are 2 independent parts, one for each index of `group`. The reference program is written for one: setup_inputs(seed, part) draws one part's arguments, and reference() takes and returns one part's arrays. A program takes and returns all parts, laid end to end along the dimension named above; an argument that names none is the same for every part. Nothing has to cross between parts.
All inputs are finite; a program needn't handle non-finite values.
Results may differ from the reference program's by a relative error of at most 0.0029.
Values may be sent and summed in bfloat16 or wider, within the bound.
No kernel may reach another device: no remote copies, remote signals or barrier semaphores. Data moves between devices by JAX's collectives and lax.ppermute only.
A program may use at most 128 MiB of HBM per device.

```python
import math
import jax
import jax.numpy as jnp
from jax import lax

P_IN = 64
P_OUT = 64
GDIM = 4096
LAYERS = 2
TRAIN = 8192
QUERIES = 256


def steps_of(own_key, dims, cuts, least, top_value):
    gain, own = 1.0, jax.random.fold_in(own_key, 6)
    for axis_at, parts in cuts:
        draws = jnp.exp(jax.random.uniform(jax.random.fold_in(own, axis_at), (parts,), jnp.float32, least / len(cuts), top_value / len(cuts)))
        gain = gain * jnp.repeat(draws, dims[axis_at] // parts).reshape([-1 if axis == axis_at else 1 for axis in range(len(dims))])
    return gain


def bell_draw(rng, extent, width, most, cuts=(), held_as=jnp.bfloat16):
    drawn = width * jax.random.normal(rng, extent, jnp.float32)
    if cuts:
        drawn = drawn * steps_of(rng, extent, cuts, -0.22, 0.18)
    return jnp.clip(drawn, -most, most).astype(held_as)


def setup_inputs(seed: int = 0, part: int = 0) -> dict:
    splits = jax.random.split(jax.random.key(seed), 6)
    part_keys = jax.random.split(jax.random.fold_in(splits[5], part), 6)
    train_grads = bell_draw(part_keys[0], (TRAIN, LAYERS, GDIM), 1.0, 6.0, ((0, 16),))
    query_grads = bell_draw(splits[1], (QUERIES, LAYERS, GDIM), (LAYERS * GDIM) ** -0.5, 0.0625, ((0, 16),))
    basis_in = bell_draw(splits[2], (LAYERS, P_IN, P_IN), P_IN ** -0.5, 0.75, (), jnp.float32)
    basis_out = bell_draw(splits[3], (LAYERS, P_OUT, P_OUT), P_OUT ** -0.5, 0.75, (), jnp.float32)
    eigvals = jnp.clip(jnp.exp(jax.random.uniform(splits[4], (LAYERS, GDIM), jnp.float32, math.log(0.2), math.log(5.0))), 0.2, 5.0)
    return {"train_grads": train_grads, "query_grads": query_grads, "basis_in": basis_in, "basis_out": basis_out, "eigvals": eigvals}


def precondition(query_layer, basis_a, basis_b, values):
    p_in = basis_a.shape[0]
    p_out = basis_b.shape[0]
    grads = query_layer.astype(jnp.float32).reshape(query_layer.shape[0], p_in, p_out)
    hp = lax.Precision.HIGHEST
    rotated = jnp.einsum("ai,qab,bj->qij", basis_a, grads, basis_b, precision=hp)
    damping = 0.1 * jnp.mean(values)
    scaled = rotated / (values.reshape(p_in, p_out) + damping)
    back = jnp.einsum("ia,qab,jb->qij", basis_a, scaled, basis_b, precision=hp)
    return back.reshape(query_layer.shape[0], p_in * p_out).astype(jnp.bfloat16)


def reference(train_grads, query_grads, basis_in, basis_out, eigvals):
    total = jnp.zeros((train_grads.shape[0], query_grads.shape[0]), jnp.float32)
    for layer_id in range(LAYERS):
        precond = precondition(query_grads[:, layer_id, :], basis_in[layer_id], basis_out[layer_id], eigvals[layer_id])
        total = total + jnp.dot(train_grads[:, layer_id, :], precond.T, preferred_element_type=jnp.float32)
    return total
```

```python
import functools

import jax
import jax.numpy as jnp
from jax import lax
from jax.experimental import pallas as pl
from jax.experimental.pallas import tpu as pltpu
from jax.sharding import PartitionSpec as P

CORES = 2
XS = 2
GROUPS = 2
ROWS = 128


def precondition(query_grads, basis_in, basis_out, eigvals):
    q_rows, layers_here = query_grads.shape[:2]
    p_in = basis_in.shape[1]
    p_out = basis_out.shape[1]
    highest = lax.Precision.HIGHEST
    grads = query_grads.astype(jnp.float32).reshape(q_rows, layers_here, p_in, p_out)
    rotated = jnp.einsum("lai,qlab,lbj->qlij", basis_in, grads, basis_out, precision=highest)
    damping = 0.1 * jnp.mean(eigvals, axis=1)
    scaled = rotated / (eigvals.reshape(layers_here, p_in, p_out) + damping[:, None, None])
    back = jnp.einsum("lia,qlab,ljb->qlij", basis_in, scaled, basis_out, precision=highest)
    return back.reshape(q_rows, layers_here * p_in * p_out).astype(jnp.bfloat16)


def place(n_train):
    t = lax.axis_index("train")
    return t // (XS * CORES), (t // CORES) % XS, t % CORES, lax.axis_index("group")


def hop(array, n_train, dz=0, dx=0, dc=0, dg=0):
    zs = n_train // (XS * CORES)
    perm = []
    for g in range(GROUPS):
        for t in range(n_train):
            z, x, c = t // (XS * CORES), (t // CORES) % XS, t % CORES
            to = (((z + dz) % zs) * XS + (x ^ dx)) * CORES + (c ^ dc)
            perm.append((g * n_train + t, (g ^ dg) * n_train + to))
    return lax.ppermute(array, ("group", "train"), perm)


def score_kernel(ids, n_train, t_ref, *refs):
    pieces, (out_ref, all_ref, sems) = refs[: len(ids)], refs[len(ids) :]
    zs = n_train // (XS * CORES)
    q_rows, width = pieces[0].shape
    z, x, c, g = place(n_train)

    @pl.when(pl.program_id(0) == 0)
    def _():
        copies = []
        for at, (dz, dx, dg, dc) in enumerate(ids):
            block = (lax.rem(z - dz + zs, zs) * XS + (x + dx) % XS) * CORES + (c + dc) % CORES
            part = (g + dg) % GROUPS
            rows = pl.ds(pl.multiple_of(block * q_rows, q_rows), q_rows)
            columns = pl.ds(pl.multiple_of(part * width, width), width)
            copies.append(pltpu.make_async_copy(pieces[at], all_ref.at[rows, columns], sems.at[at]))
        for copy in copies:
            copy.start()
        for copy in copies:
            copy.wait()

    out_ref[...] = lax.dot_general(
        t_ref[...], all_ref[...], (((1,), (1,)), ((), ())), preferred_element_type=jnp.float32
    )


def per_device(n_train, train_grads, query_grads, basis_in, basis_out, eigvals):
    tr_rows = train_grads.shape[0]
    zs = n_train // (XS * CORES)
    precond = precondition(query_grads, basis_in, basis_out, eigvals)
    q_rows, depth = precond.shape
    width = depth // GROUPS
    g = lax.axis_index("group")
    mine = lax.dynamic_slice(precond, (0, g * width), (q_rows, width))
    twin = lax.dynamic_slice(precond, (0, (1 - g) * width), (q_rows, width))
    flat_train = train_grads.reshape(tr_rows, depth)

    ids, pieces = [], []

    def keep(array, dz, dx, dg):
        ids.append((dz, dx, dg, 0))
        pieces.append(array)
        ids.append((dz, dx, dg, 1))
        pieces.append(hop(array, n_train, dc=1))

    for dz in range(zs):
        own = hop(mine, n_train, dz=dz) if dz else mine
        over_x = hop(own, n_train, dx=1)
        over_g = hop(own, n_train, dg=1) if dz else twin
        corner = hop(over_g, n_train, dx=1) if dz % 2 else hop(over_x, n_train, dg=1)
        keep(own, dz, 0, 0)
        keep(over_x, dz, 1, 0)
        keep(over_g, dz, 0, 1)
        keep(corner, dz, 1, 1)

    n_query = n_train * q_rows
    partial_scores = pl.pallas_call(
        functools.partial(score_kernel, tuple(ids), n_train),
        grid=(tr_rows // ROWS,),
        out_shape=jax.ShapeDtypeStruct((tr_rows, n_query), jnp.float32),
        in_specs=[pl.BlockSpec((ROWS, depth), lambda i: (i, 0))]
        + [pl.BlockSpec(memory_space=pl.ANY)] * len(ids),
        out_specs=pl.BlockSpec((ROWS, n_query), lambda i: (i, 0)),
        scratch_shapes=[
            pltpu.VMEM((n_query, depth), jnp.bfloat16),
            pltpu.SemaphoreType.DMA((len(ids),)),
        ],
        compiler_params=pltpu.CompilerParams(vmem_limit_bytes=48 * 1024 * 1024),
        cost_estimate=pl.CostEstimate(
            flops=2 * tr_rows * n_query * depth, bytes_accessed=2 * depth * (tr_rows + n_query), transcendentals=0
        ),
        name="scores",
    )(flat_train, *pieces)
    return lax.psum_scatter(partial_scores, "layer", scatter_dimension=1, tiled=True)


def solution(mesh):
    return jax.shard_map(
        functools.partial(per_device, mesh.shape["train"]),
        mesh=mesh,
        in_specs=(
            P(("group", "train"), "layer", None),
            P("train", "layer", None),
            P("layer", None, None),
            P("layer", None, None),
            P("layer", None),
        ),
        out_specs=P(("group", "train"), "layer"),
        check_vma=False,
    )
```

```python
import functools

import jax
import jax.numpy as jnp
from jax import lax
from jax.experimental import pallas as pl
from jax.experimental.pallas import tpu as pltpu
from jax.sharding import PartitionSpec as P

CORES = 2
XS = 2
GROUPS = 2
LANES = 128
MIB = 1024 * 1024
VMEM = pl.BlockSpec(memory_space=pltpu.VMEM)
NN = (((1,), (0,)), ((), ()))
NT = (((1,), (1,)), ((), ()))
TN = (((0,), (0,)), ((), ()))


def mxu(a, b, dims=NN):
    return lax.dot_general(a, b, dims, preferred_element_type=jnp.float32)


def halves(a):
    high = a.astype(jnp.bfloat16)
    return high, (a - high.astype(jnp.float32)).astype(jnp.bfloat16)


def place():
    t = lax.axis_index("train")
    return t // (XS * CORES), (t // CORES) % XS, t % CORES, lax.axis_index("group")


def hop(array, n_train, dz=0, dx=0, dc=0, dg=0):
    zs = n_train // (XS * CORES)
    perm = []
    for g in range(GROUPS):
        for t in range(n_train):
            z, x, c = t // (XS * CORES), (t // CORES) % XS, t % CORES
            to = (((z + dz) % zs) * XS + (x ^ dx)) * CORES + (c ^ dc)
            perm.append((g * n_train + t, (g ^ dg) * n_train + to))
    return lax.ppermute(array, ("group", "train"), perm)


def precond_kernel(slot, q_ref, in_ref, out_ref, eig_ref, piece_ref, wide_ref, tall_ref, even_ref):
    layer = (lax.axis_index("group") + slot) % GROUPS
    q_rows, width = piece_ref.shape
    rows = width // LANES
    p_in, p_out = in_ref.shape[1:]
    left = lax.broadcasted_iota(jnp.int32, (1, LANES), 1) < p_out

    eig = eig_ref[pl.ds(layer, 1), :]
    damping = 0.1 / width * jnp.sum(eig, axis=1, keepdims=True)
    for j in range(rows):
        pair = eig[:, j * LANES : (j + 1) * LANES]
        turned = pltpu.roll(pair, p_out, 1)
        even_ref[2 * j : 2 * j + 1, :] = jnp.where(left, pair, turned)
        even_ref[2 * j + 1 : 2 * j + 2, :] = jnp.where(left, turned, pair)
    scale = 1.0 / (even_ref[...] + damping)

    by_row = [in_ref[layer, pl.ds(p, rows, stride=2), :] for p in range(2)]
    back_left = jnp.concatenate(by_row, axis=0)
    fore_left = jnp.concatenate(by_row, axis=1)
    back_high, back_low = halves(back_left)
    fore_high, fore_low = halves(fore_left)
    fore = jnp.concatenate([fore_high, fore_high, fore_low], axis=0)
    back = jnp.concatenate([back_high, back_high, back_low], axis=1)

    basis = out_ref[layer]
    empty = jnp.zeros((p_out, p_out), jnp.bfloat16)

    def twice(a):
        return jnp.concatenate(
            [jnp.concatenate([a, empty], axis=1), jnp.concatenate([empty, a], axis=1)], axis=0
        )

    right_high, right_low = halves(basis)
    turned_high, turned_low = halves(basis.T)
    fore_right = jnp.concatenate([twice(right_high), twice(right_low)], axis=1)
    back_high, back_low = twice(turned_high), twice(turned_low)
    back_right = jnp.concatenate(
        [
            jnp.concatenate([back_high, back_low], axis=1),
            jnp.concatenate([back_high, jnp.zeros_like(back_low)], axis=1),
        ],
        axis=0,
    )

    flat = jnp.where(layer == 0, q_ref[:, 0, :].astype(jnp.float32), q_ref[:, 1, :].astype(jnp.float32))
    flat = flat.astype(jnp.bfloat16)
    stacked = jnp.concatenate([flat[:, j * LANES : (j + 1) * LANES] for j in range(rows)], axis=0)
    both = mxu(stacked, fore_right)
    wide_ref[...] = both[:, :LANES] + both[:, LANES:]
    by_query = jnp.concatenate([wide_ref[pl.ds(q, rows, stride=q_rows), :] for q in range(q_rows)], axis=1)
    high, low = halves(by_query)
    both = mxu(fore, jnp.concatenate([high, low, high], axis=0), TN)
    every = jnp.concatenate([left] * q_rows, axis=1)
    rotated = jnp.where(every, both[:p_in], both[p_in:])
    rotated = jnp.concatenate(
        [
            part + pltpu.roll(part, p_out, 1)
            for part in (rotated[:, q * LANES : (q + 1) * LANES] for q in range(q_rows))
        ],
        axis=1,
    )
    scaled = rotated * jnp.concatenate([scale] * q_rows, axis=1)
    high, low = halves(scaled)
    both = mxu(back, jnp.concatenate([high, low, high], axis=0))
    mixed = jnp.where(every, both[:rows], both[rows:])
    stacked = jnp.concatenate([mixed[:, q * LANES : (q + 1) * LANES] for q in range(q_rows)], axis=0)
    both = mxu(jnp.concatenate(halves(stacked), axis=1), back_right)
    tall_ref[...] = both[:, :LANES] + both[:, LANES:]
    for j in range(rows):
        block = tall_ref[pl.ds(j, q_rows, stride=rows), :]
        piece_ref[:, j * LANES : (j + 1) * LANES] = block.astype(jnp.bfloat16)


def precondition(slot, query_grads, basis_in, basis_out, eigvals):
    q_rows, _, width = query_grads.shape
    return pl.pallas_call(
        functools.partial(precond_kernel, slot),
        out_shape=jax.ShapeDtypeStruct((q_rows, width), jnp.bfloat16),
        in_specs=[VMEM] * 4,
        out_specs=VMEM,
        scratch_shapes=[
            pltpu.VMEM((q_rows * width // LANES, LANES), jnp.float32),
            pltpu.VMEM((q_rows * width // LANES, LANES), jnp.float32),
            pltpu.VMEM((2 * width // LANES, LANES), jnp.float32),
        ],
        compiler_params=pltpu.CompilerParams(vmem_limit_bytes=12 * MIB),
        cost_estimate=pl.CostEstimate(flops=10**9, bytes_accessed=4 * MIB, transcendentals=0),
        name="precond",
    )(query_grads, basis_in, basis_out, eigvals)


def split_kernel(t_ref, flat_ref):
    rows = 32
    width = t_ref.shape[2]

    @pl.loop(0, t_ref.shape[0] // rows)
    def _(i):
        at = pl.ds(pl.multiple_of(i * rows, rows), rows)
        for layer in range(t_ref.shape[1]):
            flat_ref[at, layer * width : (layer + 1) * width] = t_ref[at, layer, :]


def split_layers(train_grads):
    tr_rows, layers, width = train_grads.shape
    return pl.pallas_call(
        split_kernel,
        out_shape=jax.ShapeDtypeStruct((tr_rows, layers * width), jnp.bfloat16),
        in_specs=[VMEM],
        out_specs=VMEM,
        compiler_params=pltpu.CompilerParams(vmem_limit_bytes=20 * MIB),
        cost_estimate=pl.CostEstimate(flops=10**9, bytes_accessed=16 * MIB, transcendentals=0),
        name="split",
    )(train_grads)


def score_kernel(n_train, t_ref, *refs):
    pieces, out_ref = refs[:-1], refs[-1]
    zs = n_train // (XS * CORES)
    q_rows, width = pieces[0].shape
    n_query = n_train * q_rows
    z, x, c, g = place()
    depth = min(width, 1024)
    total = None
    for part in range(GROUPS):
        mine = pieces[part * n_train : (part + 1) * n_train]
        for at in range(0, width, depth):
            columns = pl.ds(pl.multiple_of((g + part) % GROUPS * width + at, depth), depth)
            block = jnp.concatenate([piece[:, at : at + depth] for piece in mine], axis=0)
            term = mxu(t_ref[:, columns], block, NT)
            total = term if total is None else total + term

    came = lax.broadcasted_iota(jnp.int32, (n_query, n_query), 0)
    query = lax.broadcasted_iota(jnp.int32, (n_query, n_query), 1)
    block = came // q_rows
    to_z = (z - block // (XS * CORES) + zs) % zs
    to_x = (x + block // CORES) % XS
    to_c = (c + block) % CORES
    goes = ((to_z * XS + to_x) * CORES + to_c) * q_rows + came % q_rows
    order = jnp.where(goes == query, 1.0, 0.0).astype(jnp.bfloat16)
    high, low = halves(total)
    lowest = (total - high.astype(jnp.float32) - low.astype(jnp.float32)).astype(jnp.bfloat16)
    out_ref[...] = mxu(high, order) + mxu(low, order) + mxu(lowest, order)


def per_device(n_train, train_grads, query_grads, basis_in, basis_out, eigvals):
    tr_rows = train_grads.shape[0]
    zs = n_train // (XS * CORES)
    operands = (query_grads, basis_in, basis_out, eigvals)
    mine = precondition(0, *operands)
    twin = precondition(1, *operands)
    flat_train = split_layers(train_grads)
    q_rows, width = mine.shape

    pieces = {}

    def keep(array, dz, dx, dg):
        pieces[dg, dz, dx, 0] = array
        pieces[dg, dz, dx, 1] = hop(array, n_train, dc=1)

    for dz in range(zs):
        own = hop(mine, n_train, dz=dz) if dz else mine
        over_x = hop(own, n_train, dx=1)
        over_g = hop(own, n_train, dg=1) if dz else twin
        corner = hop(over_g, n_train, dx=1) if dz % 2 else hop(over_x, n_train, dg=1)
        keep(own, dz, 0, 0)
        keep(over_x, dz, 1, 0)
        keep(over_g, dz, 0, 1)
        keep(corner, dz, 1, 1)

    n_query = n_train * q_rows
    ordered = [pieces[key] for key in sorted(pieces)]
    partial_scores = pl.pallas_call(
        functools.partial(score_kernel, n_train),
        out_shape=jax.ShapeDtypeStruct((tr_rows, n_query), jnp.float32),
        in_specs=[VMEM] * (1 + len(ordered)),
        out_specs=VMEM,
        compiler_params=pltpu.CompilerParams(vmem_limit_bytes=36 * MIB),
        cost_estimate=pl.CostEstimate(
            flops=4 * tr_rows * n_query * width, bytes_accessed=2 * width * (tr_rows + n_query), transcendentals=0
        ),
        name="scores",
    )(flat_train, *ordered)
    return lax.psum_scatter(partial_scores, "layer", scatter_dimension=1, tiled=True)


def solution(mesh):
    return jax.shard_map(
        functools.partial(per_device, mesh.shape["train"]),
        mesh=mesh,
        in_specs=(
            P(("group", "train"), "layer", None),
            P("train", "layer", None),
            P("layer", None, None),
            P("layer", None, None),
            P("layer", None),
        ),
        out_specs=P(("group", "train"), "layer"),
        check_vma=False,
    )
```

```python
import functools

import jax
import jax.numpy as jnp
from jax import lax
from jax.experimental import pallas as pl
from jax.experimental.pallas import tpu as pltpu
from jax.sharding import PartitionSpec as P

CORES = 2
XS = 2
GROUPS = 2
LANES = 128
BLOCK = 16
MIB = 1024 * 1024
VMEM = pl.BlockSpec(memory_space=pltpu.VMEM)
NN = (((1,), (0,)), ((), ()))
NT = (((1,), (1,)), ((), ()))
TN = (((0,), (0,)), ((), ()))


def mxu(a, b, dims=NN):
    return lax.dot_general(a, b, dims, preferred_element_type=jnp.float32)


def halves(a):
    high = a.astype(jnp.bfloat16)
    return high, (a - high.astype(jnp.float32)).astype(jnp.bfloat16)


def in_hbm(array):
    return pltpu.with_memory_space_constraint(array, pltpu.HBM)


def place():
    t = lax.axis_index("train")
    return t // (XS * CORES), (t // CORES) % XS, t % CORES, lax.axis_index("group")


def hop(array, n_train, dz=0, dx=0, dc=0, dg=0):
    zs = n_train // (XS * CORES)
    perm = []
    for g in range(GROUPS):
        for t in range(n_train):
            z, x, c = t // (XS * CORES), (t // CORES) % XS, t % CORES
            to = (((z + dz) % zs) * XS + (x ^ dx)) * CORES + (c ^ dc)
            perm.append((g * n_train + t, (g ^ dg) * n_train + to))
    return lax.ppermute(array, ("group", "train"), perm)


def precond_kernel(slot, q_ref, in_ref, out_ref, eig_ref, piece_ref, wide_ref, tall_ref, even_ref):
    layer = (lax.axis_index("group") + slot) % GROUPS
    q_rows, width = piece_ref.shape
    rows = width // LANES
    p_in, p_out = in_ref.shape[1:]
    left = lax.broadcasted_iota(jnp.int32, (1, LANES), 1) < p_out

    eig = eig_ref[pl.ds(layer, 1), :]
    damping = 0.1 / width * jnp.sum(eig, axis=1, keepdims=True)
    for j in range(rows):
        pair = eig[:, j * LANES : (j + 1) * LANES]
        turned = pltpu.roll(pair, p_out, 1)
        even_ref[2 * j : 2 * j + 1, :] = jnp.where(left, pair, turned)
        even_ref[2 * j + 1 : 2 * j + 2, :] = jnp.where(left, turned, pair)
    scale = 1.0 / (even_ref[...] + damping)

    by_row = [in_ref[layer, pl.ds(p, rows, stride=2), :] for p in range(2)]
    back_left = jnp.concatenate(by_row, axis=0)
    fore_left = jnp.concatenate(by_row, axis=1)
    back_high, back_low = halves(back_left)
    fore_high, fore_low = halves(fore_left)
    fore = jnp.concatenate([fore_high, fore_high, fore_low], axis=0)
    back = jnp.concatenate([back_high, back_high, back_low], axis=1)

    basis = out_ref[layer]
    empty = jnp.zeros((p_out, p_out), jnp.bfloat16)

    def twice(a):
        return jnp.concatenate(
            [jnp.concatenate([a, empty], axis=1), jnp.concatenate([empty, a], axis=1)], axis=0
        )

    right_high, right_low = halves(basis)
    turned_high, turned_low = halves(basis.T)
    fore_right = jnp.concatenate([twice(right_high), twice(right_low)], axis=1)
    back_high, back_low = twice(turned_high), twice(turned_low)
    back_right = jnp.concatenate(
        [
            jnp.concatenate([back_high, back_low], axis=1),
            jnp.concatenate([back_high, jnp.zeros_like(back_low)], axis=1),
        ],
        axis=0,
    )

    flat = jnp.where(layer == 0, q_ref[:, 0, :].astype(jnp.float32), q_ref[:, 1, :].astype(jnp.float32))
    flat = flat.astype(jnp.bfloat16)
    stacked = jnp.concatenate([flat[:, j * LANES : (j + 1) * LANES] for j in range(rows)], axis=0)
    both = mxu(stacked, fore_right)
    wide_ref[...] = both[:, :LANES] + both[:, LANES:]
    by_query = jnp.concatenate([wide_ref[pl.ds(q, rows, stride=q_rows), :] for q in range(q_rows)], axis=1)
    high, low = halves(by_query)
    both = mxu(fore, jnp.concatenate([high, low, high], axis=0), TN)
    every = jnp.concatenate([left] * q_rows, axis=1)
    rotated = jnp.where(every, both[:p_in], both[p_in:])
    rotated = jnp.concatenate(
        [
            part + pltpu.roll(part, p_out, 1)
            for part in (rotated[:, q * LANES : (q + 1) * LANES] for q in range(q_rows))
        ],
        axis=1,
    )
    scaled = rotated * jnp.concatenate([scale] * q_rows, axis=1)
    high, low = halves(scaled)
    both = mxu(back, jnp.concatenate([high, low, high], axis=0))
    mixed = jnp.where(every, both[:rows], both[rows:])
    stacked = jnp.concatenate([mixed[:, q * LANES : (q + 1) * LANES] for q in range(q_rows)], axis=0)
    both = mxu(jnp.concatenate(halves(stacked), axis=1), back_right)
    tall_ref[...] = both[:, :LANES] + both[:, LANES:]
    for j in range(rows):
        block = tall_ref[pl.ds(j, q_rows, stride=rows), :]
        piece_ref[:, j * LANES : (j + 1) * LANES] = block.astype(jnp.bfloat16)


def precondition(slot, query_grads, basis_in, basis_out, eigvals):
    q_rows, layers, width = query_grads.shape
    space = pltpu.HBM if slot == 0 else pltpu.VMEM
    operands = (query_grads, basis_in, basis_out, eigvals)
    body, scratch = functools.partial(precond_kernel, slot), []
    if slot == 0:
        operands = [in_hbm(a) for a in operands]
        body = functools.partial(fetched, len(operands), body)
        scratch = [pltpu.VMEM(a.shape, a.dtype) for a in operands] + [pltpu.SemaphoreType.DMA((len(operands),))]
    return pl.pallas_call(
        body,
        out_shape=jax.ShapeDtypeStruct((q_rows, width), jnp.bfloat16),
        in_specs=[pl.BlockSpec(memory_space=space)] * len(operands),
        out_specs=VMEM,
        scratch_shapes=[
            pltpu.VMEM((q_rows * width // LANES, LANES), jnp.float32),
            pltpu.VMEM((q_rows * width // LANES, LANES), jnp.float32),
            pltpu.VMEM((2 * width // LANES, LANES), jnp.float32),
        ]
        + scratch,
        compiler_params=pltpu.CompilerParams(vmem_limit_bytes=8 * MIB),
        cost_estimate=pl.CostEstimate(flops=10**9, bytes_accessed=4 * MIB, transcendentals=0),
        name="precond",
    )(*operands)


def fetched(n, body, *refs):
    operands, others = refs[:n], refs[n:]
    others, here, sems = others[: -n - 1], others[-n - 1 : -1], others[-1]
    copies = [pltpu.make_async_copy(a, b, sems.at[i]) for i, (a, b) in enumerate(zip(operands, here))]
    for copy in copies:
        copy.start()
    for copy in copies:
        copy.wait()
    body(*here, *others)


def split_kernel(layers, t_ref, flat_ref, here_ref, wide_ref, sems):
    rows, chunks = BLOCK, sems.shape[0]
    lines = t_ref.shape[1]
    pitch = wide_ref.shape[0] // rows
    chunk = t_ref.shape[0] // chunks
    copies = [
        pltpu.make_async_copy(
            t_ref.at[pl.ds(i * chunk, chunk)], here_ref.at[pl.ds(i * chunk, chunk)], sems.at[i]
        )
        for i in range(chunks)
    ]
    for copy in copies:
        copy.start()
    for i in range(chunks):
        copies[i].wait()

        @pl.loop(i * chunk // rows, (i + 1) * chunk // rows)
        def _(block):
            at = pl.multiple_of(block * rows, rows)
            for row in range(rows):
                wide_ref[row * pitch : row * pitch + lines, :] = here_ref[at + row].astype(jnp.float32)
            for line in range(lines):
                column = ((line % layers) * (lines // layers) + line // layers) * LANES
                out = wide_ref[pl.ds(line, rows, stride=pitch), :].astype(jnp.bfloat16)
                flat_ref[pl.ds(at, rows), column : column + LANES] = out


def split_layers(train_grads):
    tr_rows, layers, width = train_grads.shape
    lines = layers * width // LANES
    by_line = train_grads.reshape(tr_rows, layers, width // LANES, LANES)
    by_line = by_line.transpose(0, 2, 1, 3).reshape(tr_rows, lines, LANES)
    return pl.pallas_call(
        functools.partial(split_kernel, layers),
        out_shape=jax.ShapeDtypeStruct((tr_rows, layers * width), jnp.bfloat16),
        in_specs=[pl.BlockSpec(memory_space=pltpu.HBM)],
        out_specs=VMEM,
        scratch_shapes=[
            pltpu.VMEM((tr_rows, lines, LANES), jnp.bfloat16),
            pltpu.VMEM((BLOCK * (lines + 8), LANES), jnp.float32),
            pltpu.SemaphoreType.DMA((8,)),
        ],
        compiler_params=pltpu.CompilerParams(vmem_limit_bytes=20 * MIB),
        cost_estimate=pl.CostEstimate(flops=10**9, bytes_accessed=16 * MIB, transcendentals=0),
        name="split",
    )(in_hbm(by_line))


def score_kernel(n_train, t_ref, *refs):
    pieces, out_ref = refs[:-1], refs[-1]
    zs = n_train // (XS * CORES)
    q_rows, width = pieces[0].shape
    n_query = n_train * q_rows
    z, x, c, g = place()
    depth = min(width, 1024)
    total = None
    for part in range(GROUPS):
        mine = pieces[part * n_train : (part + 1) * n_train]
        for at in range(0, width, depth):
            columns = pl.ds(pl.multiple_of((g + part) % GROUPS * width + at, depth), depth)
            block = jnp.concatenate([piece[:, at : at + depth] for piece in mine], axis=0)
            term = mxu(t_ref[:, columns], block, NT)
            total = term if total is None else total + term

    came = lax.broadcasted_iota(jnp.int32, (n_query, n_query), 0)
    query = lax.broadcasted_iota(jnp.int32, (n_query, n_query), 1)
    block = came // q_rows
    to_z = (z - block // (XS * CORES) + zs) % zs
    to_x = (x + block // CORES) % XS
    to_c = (c + block) % CORES
    goes = ((to_z * XS + to_x) * CORES + to_c) * q_rows + came % q_rows
    order = jnp.where(goes == query, 1.0, 0.0).astype(jnp.bfloat16)
    high, low = halves(total)
    lowest = (total - high.astype(jnp.float32) - low.astype(jnp.float32)).astype(jnp.bfloat16)
    out_ref[...] = mxu(high, order) + mxu(low, order) + mxu(lowest, order)


def per_device(n_train, train_grads, query_grads, basis_in, basis_out, eigvals):
    tr_rows = train_grads.shape[0]
    zs = n_train // (XS * CORES)
    operands = (query_grads, basis_in, basis_out, eigvals)
    mine = precondition(0, *operands)
    along_z = [hop(mine, n_train, dz=dz) for dz in range(zs - 1, 0, -1)]
    first_x = hop(mine, n_train, dx=1)
    mine, operands, train_grads = lax.optimization_barrier((mine, operands, train_grads))
    twin = precondition(1, *operands)
    flat_train = split_layers(train_grads)
    along_z, first_x, twin, flat_train = lax.optimization_barrier((along_z, first_x, twin, flat_train))
    q_rows, width = mine.shape

    pieces = {}

    def keep(array, dz, dx, dg):
        pieces[dg, dz, dx, 0] = array
        pieces[dg, dz, dx, 1] = hop(array, n_train, dc=1)

    for dz in range(zs):
        own = along_z[zs - 1 - dz] if dz else mine
        over_x = hop(own, n_train, dx=1) if dz else first_x
        over_g = hop(own, n_train, dg=1) if dz else twin
        corner = hop(over_g, n_train, dx=1) if dz % 2 else hop(over_x, n_train, dg=1)
        keep(own, dz, 0, 0)
        keep(over_x, dz, 1, 0)
        keep(over_g, dz, 0, 1)
        keep(corner, dz, 1, 1)

    n_query = n_train * q_rows
    ordered = [pieces[key] for key in sorted(pieces)]
    partial_scores = pl.pallas_call(
        functools.partial(score_kernel, n_train),
        out_shape=jax.ShapeDtypeStruct((tr_rows, n_query), jnp.float32),
        in_specs=[VMEM] * (1 + len(ordered)),
        out_specs=VMEM,
        compiler_params=pltpu.CompilerParams(vmem_limit_bytes=36 * MIB),
        cost_estimate=pl.CostEstimate(
            flops=4 * tr_rows * n_query * width, bytes_accessed=2 * width * (tr_rows + n_query), transcendentals=0
        ),
        name="scores",
    )(flat_train, *ordered)
    return lax.psum_scatter(partial_scores, "layer", scatter_dimension=1, tiled=True)


def solution(mesh):
    return jax.shard_map(
        functools.partial(per_device, mesh.shape["train"]),
        mesh=mesh,
        in_specs=(
            P(("group", "train"), "layer", None),
            P("train", "layer", None),
            P("layer", None, None),
            P("layer", None, None),
            P("layer", None),
        ),
        out_specs=P(("group", "train"), "layer"),
        check_vma=False,
    )
```

```python
import functools

import jax
import jax.numpy as jnp
import numpy as np
from jax import lax
from jax.experimental import pallas as pl
from jax.experimental.pallas import tpu as pltpu
from jax.sharding import PartitionSpec as P

CORES = 2
XS = 2
GROUPS = 2
LANES = 128
BLOCK = 16
MIB = 1024 * 1024
VMEM = pl.BlockSpec(memory_space=pltpu.VMEM)
NN = (((1,), (0,)), ((), ()))
NT = (((1,), (1,)), ((), ()))
TN = (((0,), (0,)), ((), ()))


def mxu(a, b, dims=NN):
    return lax.dot_general(a, b, dims, preferred_element_type=jnp.float32)


def halves(a):
    high = a.astype(jnp.bfloat16)
    return high, (a - high.astype(jnp.float32)).astype(jnp.bfloat16)


def in_hbm(array):
    return pltpu.with_memory_space_constraint(array, pltpu.HBM)


class Blocks:
    def __init__(self, array, came):
        self.array, self.came = array, came

    def hop(self, turn):
        groups, n_train = self.came.shape
        perm, came = [], np.zeros_like(self.came)
        for g in range(groups):
            for t in range(n_train):
                z, x, c = t // (XS * CORES), t // CORES % XS, t % CORES
                to_g, z, x, c = turn(g, z, x, c)
                to_t = (z * XS + x) * CORES + c
                perm.append((g * n_train + t, to_g * n_train + to_t))
                came[to_g, to_t] = self.came[g, t]
        return Blocks(lax.ppermute(self.array, ("group", "train"), perm), came)


def over_core(g, z, x, c):
    return g, z, x, c ^ 1


def over_x(g, z, x, c):
    return g, z, x ^ 1, c


def over_z(g, z, x, c):
    return g, z ^ 1, x, c


def far_z(pair):
    return lambda g, z, x, c: (g, z ^ (2 * pair + 1 - g), x, c)


def x_or_group(g, z, x, c):
    return (g, z, x ^ 1, c) if c == 0 else (g ^ 1, z, x, c)


def group_or_x(g, z, x, c):
    return (g, z, x ^ 1, c) if c == 1 else (g ^ 1, z, x, c)


def precond_kernel(q_ref, in_ref, out_ref, eig_ref, block_ref, *scratch):
    for layer in range(in_ref.shape[0]):
        precond_layer(layer, q_ref, in_ref, out_ref, eig_ref, block_ref, *(ref.at[layer] for ref in scratch))


def precond_layer(layer, q_ref, in_ref, out_ref, eig_ref, block_ref, wide_ref, tall_ref, even_ref):
    q_rows, _, width = q_ref.shape
    rows = width // LANES
    p_in, p_out = in_ref.shape[1:]
    left = lax.broadcasted_iota(jnp.int32, (1, LANES), 1) < p_out

    eig = eig_ref[layer : layer + 1, :]
    damping = 0.1 / width * jnp.sum(eig, axis=1, keepdims=True)
    for j in range(rows):
        pair = eig[:, j * LANES : (j + 1) * LANES]
        turned = pltpu.roll(pair, p_out, 1)
        even_ref[2 * j : 2 * j + 1, :] = jnp.where(left, pair, turned)
        even_ref[2 * j + 1 : 2 * j + 2, :] = jnp.where(left, turned, pair)
    scale = 1.0 / (even_ref[...] + damping)

    by_row = [in_ref[layer, pl.ds(p, rows, stride=2), :] for p in range(2)]
    back_left = jnp.concatenate(by_row, axis=0)
    fore_left = jnp.concatenate(by_row, axis=1)
    back_high, back_low = halves(back_left)
    fore_high, fore_low = halves(fore_left)
    fore = jnp.concatenate([fore_high, fore_high, fore_low], axis=0)
    back = jnp.concatenate([back_high, back_high, back_low], axis=1)

    basis = out_ref[layer]
    empty = jnp.zeros((p_out, p_out), jnp.bfloat16)

    def twice(a):
        return jnp.concatenate(
            [jnp.concatenate([a, empty], axis=1), jnp.concatenate([empty, a], axis=1)], axis=0
        )

    right_high, right_low = halves(basis)
    turned_high, turned_low = halves(basis.T)
    fore_right = jnp.concatenate([twice(right_high), twice(right_low)], axis=1)
    back_high, back_low = twice(turned_high), twice(turned_low)
    back_right = jnp.concatenate(
        [
            jnp.concatenate([back_high, back_low], axis=1),
            jnp.concatenate([back_high, jnp.zeros_like(back_low)], axis=1),
        ],
        axis=0,
    )

    flat = q_ref[:, layer, :]
    stacked = jnp.concatenate([flat[:, j * LANES : (j + 1) * LANES] for j in range(rows)], axis=0)
    both = mxu(stacked, fore_right)
    wide_ref[...] = both[:, :LANES] + both[:, LANES:]
    by_query = jnp.concatenate([wide_ref[pl.ds(q, rows, stride=q_rows), :] for q in range(q_rows)], axis=1)
    high, low = halves(by_query)
    both = mxu(fore, jnp.concatenate([high, low, high], axis=0), TN)
    every = jnp.concatenate([left] * q_rows, axis=1)
    rotated = jnp.where(every, both[:p_in], both[p_in:])
    rotated = jnp.concatenate(
        [
            part + pltpu.roll(part, p_out, 1)
            for part in (rotated[:, q * LANES : (q + 1) * LANES] for q in range(q_rows))
        ],
        axis=1,
    )
    scaled = rotated * jnp.concatenate([scale] * q_rows, axis=1)
    high, low = halves(scaled)
    both = mxu(back, jnp.concatenate([high, low, high], axis=0))
    mixed = jnp.where(every, both[:rows], both[rows:])
    stacked = jnp.concatenate([mixed[:, q * LANES : (q + 1) * LANES] for q in range(q_rows)], axis=0)
    both = mxu(jnp.concatenate(halves(stacked), axis=1), back_right)
    tall_ref[...] = both[:, :LANES] + both[:, LANES:]
    for j in range(rows):
        block = tall_ref[pl.ds(j, q_rows, stride=rows), :]
        column = layer * width + j * LANES
        block_ref[:, column : column + LANES] = block.astype(jnp.bfloat16)


def precondition(query_grads, basis_in, basis_out, eigvals):
    q_rows, layers, width = query_grads.shape
    lines = q_rows * width // LANES
    operands = [in_hbm(a) for a in (query_grads, basis_in, basis_out, eigvals)]
    return pl.pallas_call(
        functools.partial(fetched, len(operands), precond_kernel),
        out_shape=jax.ShapeDtypeStruct((q_rows, layers * width), jnp.bfloat16),
        in_specs=[pl.BlockSpec(memory_space=pltpu.HBM)] * len(operands),
        out_specs=VMEM,
        scratch_shapes=[
            pltpu.VMEM((layers, lines, LANES), jnp.float32),
            pltpu.VMEM((layers, lines, LANES), jnp.float32),
            pltpu.VMEM((layers, 2 * width // LANES, LANES), jnp.float32),
        ]
        + [pltpu.VMEM(a.shape, a.dtype) for a in operands]
        + [pltpu.SemaphoreType.DMA((len(operands),))],
        compiler_params=pltpu.CompilerParams(vmem_limit_bytes=16 * MIB),
        cost_estimate=pl.CostEstimate(flops=10**9, bytes_accessed=4 * MIB, transcendentals=0),
        name="precond",
    )(*operands)


def fetched(n, body, *refs):
    operands, others = refs[:n], refs[n:]
    others, here, sems = others[: -n - 1], others[-n - 1 : -1], others[-1]
    copies = [pltpu.make_async_copy(a, b, sems.at[i]) for i, (a, b) in enumerate(zip(operands, here))]
    for copy in copies:
        copy.start()
    for copy in copies:
        copy.wait()
    body(*here, *others)


def split_kernel(layers, t_ref, flat_ref, here_ref, wide_ref, sems):
    rows, chunks = BLOCK, sems.shape[0]
    lines = t_ref.shape[1]
    pitch = wide_ref.shape[0] // rows
    chunk = t_ref.shape[0] // chunks
    copies = [
        pltpu.make_async_copy(
            t_ref.at[pl.ds(i * chunk, chunk)], here_ref.at[pl.ds(i * chunk, chunk)], sems.at[i]
        )
        for i in range(chunks)
    ]
    for copy in copies:
        copy.start()
    for i in range(chunks):
        copies[i].wait()

        @pl.loop(i * chunk // rows, (i + 1) * chunk // rows)
        def _(block):
            at = pl.multiple_of(block * rows, rows)
            for row in range(rows):
                wide_ref[row * pitch : row * pitch + lines, :] = here_ref[at + row].astype(jnp.float32)
            for line in range(lines):
                column = ((line % layers) * (lines // layers) + line // layers) * LANES
                out = wide_ref[pl.ds(line, rows, stride=pitch), :].astype(jnp.bfloat16)
                flat_ref[pl.ds(at, rows), column : column + LANES] = out


def split_layers(train_grads):
    tr_rows, layers, width = train_grads.shape
    lines = layers * width // LANES
    by_line = train_grads.reshape(tr_rows, layers, width // LANES, LANES)
    by_line = by_line.transpose(0, 2, 1, 3).reshape(tr_rows, lines, LANES)
    return pl.pallas_call(
        functools.partial(split_kernel, layers),
        out_shape=jax.ShapeDtypeStruct((tr_rows, layers * width), jnp.bfloat16),
        in_specs=[pl.BlockSpec(memory_space=pltpu.HBM)],
        out_specs=VMEM,
        scratch_shapes=[
            pltpu.VMEM((tr_rows, lines, LANES), jnp.bfloat16),
            pltpu.VMEM((BLOCK * (lines + 8), LANES), jnp.float32),
            pltpu.SemaphoreType.DMA((8,)),
        ],
        compiler_params=pltpu.CompilerParams(vmem_limit_bytes=20 * MIB),
        cost_estimate=pl.CostEstimate(flops=10**9, bytes_accessed=16 * MIB, transcendentals=0),
        name="split",
    )(in_hbm(by_line))


def score_kernel(masks, t_ref, *refs):
    blocks, out_ref = refs[:-1], refs[-1]
    q_rows, width = blocks[0].shape
    n_query = len(blocks) * q_rows
    depth = min(width, 1024)
    total = None
    for at in range(0, width, depth):
        block = jnp.concatenate([ref[:, at : at + depth] for ref in blocks], axis=0)
        term = mxu(t_ref[:, at : at + depth], block, NT)
        total = term if total is None else total + term

    me, g = lax.axis_index("train"), lax.axis_index("group")
    row = lax.broadcasted_iota(jnp.int32, (q_rows, n_query), 0)
    query = lax.broadcasted_iota(jnp.int32, (q_rows, n_query), 1)
    order = []
    for mask in masks:
        c0, c1 = (jnp.where(g == 0, mask[0][c], mask[1][c]) for c in range(CORES))
        source = me ^ jnp.where(me % CORES == 0, c0, c1)
        order.append(jnp.where(query == source * q_rows + row, 1.0, 0.0))
    order = jnp.concatenate(order, axis=0).astype(jnp.bfloat16)
    high, low = halves(total)
    lowest = (total - high.astype(jnp.float32) - low.astype(jnp.float32)).astype(jnp.bfloat16)
    out_ref[...] = mxu(high, order) + mxu(low, order) + mxu(lowest, order)


def came_masks(blocks, n_train):
    xors = blocks.came ^ np.arange(n_train)[None]
    masks = [[int(xors[g, c]) for c in range(CORES)] for g in range(GROUPS)]
    assert all((xors[g, c::CORES] == masks[g][c]).all() for g in range(GROUPS) for c in range(CORES))
    return masks


def per_device(n_train, train_grads, query_grads, basis_in, basis_out, eigvals):
    tr_rows = train_grads.shape[0]
    zs = n_train // (XS * CORES)
    block = precondition(query_grads, basis_in, basis_out, eigvals)
    q_rows, width = block.shape
    own = Blocks(block, np.tile(np.arange(n_train), (GROUPS, 1)))

    far = [own.hop(far_z(pair)) for pair in range(1, zs // 2)]
    at_x = own.hop(over_x)
    at_z = own.hop(over_z)
    twins = [own.hop(over_core)]
    own.array, train_grads = lax.optimization_barrier((own.array, train_grads))
    flat_train = split_layers(train_grads)
    at_x.array, flat_train = lax.optimization_barrier((at_x.array, flat_train))
    at_xz = at_x.hop(over_z)
    twins.append(at_x.hop(over_core))
    here = [own, at_x, at_z, at_xz]
    for fetched_far in far:
        fetched_far.array, flat_train = lax.optimization_barrier((fetched_far.array, flat_train))
        first = fetched_far.hop(x_or_group)
        second = fetched_far.hop(group_or_x)
        corner = first.hop(group_or_x)
        twins += [a.hop(over_core) for a in (fetched_far, first, second, corner)]
        here += [fetched_far, first, second, corner]
    twins += [a.hop(over_core) for a in (at_z, at_xz)]
    everything = here + twins

    n_query = n_train * q_rows
    partial_scores = pl.pallas_call(
        functools.partial(score_kernel, [came_masks(a, n_train) for a in everything]),
        out_shape=jax.ShapeDtypeStruct((tr_rows, n_query), jnp.float32),
        in_specs=[VMEM] * (1 + len(everything)),
        out_specs=VMEM,
        compiler_params=pltpu.CompilerParams(vmem_limit_bytes=36 * MIB),
        cost_estimate=pl.CostEstimate(
            flops=2 * tr_rows * n_query * width, bytes_accessed=2 * width * (tr_rows + n_query), transcendentals=0
        ),
        name="scores",
    )(flat_train, *(a.array for a in everything))
    return lax.psum_scatter(partial_scores, "layer", scatter_dimension=1, tiled=True)


def solution(mesh):
    return jax.shard_map(
        functools.partial(per_device, mesh.shape["train"]),
        mesh=mesh,
        in_specs=(
            P(("group", "train"), "layer", None),
            P("train", "layer", None),
            P("layer", None, None),
            P("layer", None, None),
            P("layer", None),
        ),
        out_specs=P(("group", "train"), "layer"),
        check_vma=False,
    )
```

```python
import functools

import jax
import jax.numpy as jnp
import numpy as np
from jax import lax
from jax.experimental import pallas as pl
from jax.experimental.pallas import tpu as pltpu
from jax.sharding import PartitionSpec as P

CORES = 2
XS = 2
GROUPS = 2
LANES = 128
BLOCK = 16
MIB = 1024 * 1024
VMEM = pl.BlockSpec(memory_space=pltpu.VMEM)
NN = (((1,), (0,)), ((), ()))
NT = (((1,), (1,)), ((), ()))
TN = (((0,), (0,)), ((), ()))


def mxu(a, b, dims=NN):
    return lax.dot_general(a, b, dims, preferred_element_type=jnp.float32)


def halves(a):
    high = a.astype(jnp.bfloat16)
    return high, (a - high.astype(jnp.float32)).astype(jnp.bfloat16)


def in_hbm(array):
    return pltpu.with_memory_space_constraint(array, pltpu.HBM)


class Blocks:
    def __init__(self, array, came):
        self.array, self.came = array, came

    def hop(self, turn):
        groups, n_train = self.came[0].shape
        perm, came = [], [np.zeros_like(a) for a in self.came]
        for g in range(groups):
            for t in range(n_train):
                z, x, c = t // (XS * CORES), t // CORES % XS, t % CORES
                to_g, z, x, c = turn(g, z, x, c)
                to_t = (z * XS + x) * CORES + c
                perm.append((g * n_train + t, to_g * n_train + to_t))
                for here, there in zip(self.came, came):
                    there[to_g, to_t] = here[g, t]
        return Blocks(lax.ppermute(self.array, ("group", "train"), perm), came)

    def columns(self, start, stop):
        return Blocks(self.array[:, start:stop], self.came)


def stack(*parts):
    return Blocks(jnp.concatenate([a.array for a in parts], axis=0), sum((a.came for a in parts), []))


def beside(left, right):
    assert all((a == b).all() for a, b in zip(left.came, right.came))
    return Blocks(jnp.concatenate([left.array, right.array], axis=1), left.came)


def after(kernel_result, *parts):
    arrays, kernel_result = lax.optimization_barrier(([a.array for a in parts], kernel_result))
    return kernel_result, *(Blocks(array, a.came) for array, a in zip(arrays, parts))


def over_core(g, z, x, c):
    return g, z, x, c ^ 1


def over_x(g, z, x, c):
    return g, z, x ^ 1, c


def over_z(g, z, x, c):
    return g, z ^ 1, x, c


def far_z(pair):
    return lambda g, z, x, c: (g, z ^ (2 * pair + 1 - g), x, c)


def over_group(g, z, x, c):
    return g ^ 1, z, x, c


def precond_kernel(q_ref, in_ref, out_ref, eig_ref, block_ref, *scratch):
    for layer in range(in_ref.shape[0]):
        precond_layer(layer, q_ref, in_ref, out_ref, eig_ref, block_ref, *(ref.at[layer] for ref in scratch))


def precond_layer(layer, q_ref, in_ref, out_ref, eig_ref, block_ref, wide_ref, tall_ref, even_ref):
    q_rows, _, width = q_ref.shape
    rows = width // LANES
    p_in, p_out = in_ref.shape[1:]
    left = lax.broadcasted_iota(jnp.int32, (1, LANES), 1) < p_out

    eig = eig_ref[layer : layer + 1, :]
    damping = 0.1 / width * jnp.sum(eig, axis=1, keepdims=True)
    for j in range(rows):
        pair = eig[:, j * LANES : (j + 1) * LANES]
        turned = pltpu.roll(pair, p_out, 1)
        even_ref[2 * j : 2 * j + 1, :] = jnp.where(left, pair, turned)
        even_ref[2 * j + 1 : 2 * j + 2, :] = jnp.where(left, turned, pair)
    scale = 1.0 / (even_ref[...] + damping)

    by_row = [in_ref[layer, pl.ds(p, rows, stride=2), :] for p in range(2)]
    back_left = jnp.concatenate(by_row, axis=0)
    fore_left = jnp.concatenate(by_row, axis=1)
    back_high, back_low = halves(back_left)
    fore_high, fore_low = halves(fore_left)
    fore = jnp.concatenate([fore_high, fore_high, fore_low], axis=0)
    back = jnp.concatenate([back_high, back_high, back_low], axis=1)

    basis = out_ref[layer]
    empty = jnp.zeros((p_out, p_out), jnp.bfloat16)

    def twice(a):
        return jnp.concatenate(
            [jnp.concatenate([a, empty], axis=1), jnp.concatenate([empty, a], axis=1)], axis=0
        )

    right_high, right_low = halves(basis)
    turned_high, turned_low = halves(basis.T)
    fore_right = jnp.concatenate([twice(right_high), twice(right_low)], axis=1)
    back_high, back_low = twice(turned_high), twice(turned_low)
    back_right = jnp.concatenate(
        [
            jnp.concatenate([back_high, back_low], axis=1),
            jnp.concatenate([back_high, jnp.zeros_like(back_low)], axis=1),
        ],
        axis=0,
    )

    flat = q_ref[:, layer, :]
    stacked = jnp.concatenate([flat[:, j * LANES : (j + 1) * LANES] for j in range(rows)], axis=0)
    both = mxu(stacked, fore_right)
    wide_ref[...] = both[:, :LANES] + both[:, LANES:]
    by_query = jnp.concatenate([wide_ref[pl.ds(q, rows, stride=q_rows), :] for q in range(q_rows)], axis=1)
    high, low = halves(by_query)
    both = mxu(fore, jnp.concatenate([high, low, high], axis=0), TN)
    every = jnp.concatenate([left] * q_rows, axis=1)
    rotated = jnp.where(every, both[:p_in], both[p_in:])
    rotated = jnp.concatenate(
        [
            part + pltpu.roll(part, p_out, 1)
            for part in (rotated[:, q * LANES : (q + 1) * LANES] for q in range(q_rows))
        ],
        axis=1,
    )
    scaled = rotated * jnp.concatenate([scale] * q_rows, axis=1)
    high, low = halves(scaled)
    both = mxu(back, jnp.concatenate([high, low, high], axis=0))
    mixed = jnp.where(every, both[:rows], both[rows:])
    stacked = jnp.concatenate([mixed[:, q * LANES : (q + 1) * LANES] for q in range(q_rows)], axis=0)
    both = mxu(jnp.concatenate(halves(stacked), axis=1), back_right)
    tall_ref[...] = both[:, :LANES] + both[:, LANES:]
    for j in range(rows):
        block = tall_ref[pl.ds(j, q_rows, stride=rows), :]
        column = layer * width + j * LANES
        block_ref[:, column : column + LANES] = block.astype(jnp.bfloat16)


def precondition(query_grads, basis_in, basis_out, eigvals):
    q_rows, layers, width = query_grads.shape
    lines = q_rows * width // LANES
    operands = [in_hbm(a) for a in (query_grads, basis_in, basis_out, eigvals)]
    return pl.pallas_call(
        functools.partial(fetched, len(operands), precond_kernel),
        out_shape=jax.ShapeDtypeStruct((q_rows, layers * width), jnp.bfloat16),
        in_specs=[pl.BlockSpec(memory_space=pltpu.HBM)] * len(operands),
        out_specs=VMEM,
        scratch_shapes=[
            pltpu.VMEM((layers, lines, LANES), jnp.float32),
            pltpu.VMEM((layers, lines, LANES), jnp.float32),
            pltpu.VMEM((layers, 2 * width // LANES, LANES), jnp.float32),
        ]
        + [pltpu.VMEM(a.shape, a.dtype) for a in operands]
        + [pltpu.SemaphoreType.DMA((len(operands),))],
        compiler_params=pltpu.CompilerParams(vmem_limit_bytes=16 * MIB),
        cost_estimate=pl.CostEstimate(flops=10**9, bytes_accessed=4 * MIB, transcendentals=0),
        name="precond",
    )(*operands)


def fetched(n, body, *refs):
    operands, others = refs[:n], refs[n:]
    others, here, sems = others[: -n - 1], others[-n - 1 : -1], others[-1]
    copies = [pltpu.make_async_copy(a, b, sems.at[i]) for i, (a, b) in enumerate(zip(operands, here))]
    for copy in copies:
        copy.start()
    for copy in copies:
        copy.wait()
    body(*here, *others)


def split_kernel(layers, t_ref, flat_ref, here_ref, wide_ref, sems):
    rows, chunks = BLOCK, sems.shape[0]
    lines = t_ref.shape[1]
    pitch = wide_ref.shape[0] // rows
    chunk = t_ref.shape[0] // chunks
    copies = [
        pltpu.make_async_copy(
            t_ref.at[pl.ds(i * chunk, chunk)], here_ref.at[pl.ds(i * chunk, chunk)], sems.at[i]
        )
        for i in range(chunks)
    ]
    for copy in copies:
        copy.start()
    for i in range(chunks):
        copies[i].wait()

        @pl.loop(i * chunk // rows, (i + 1) * chunk // rows)
        def _(block):
            at = pl.multiple_of(block * rows, rows)
            for row in range(rows):
                wide_ref[row * pitch : row * pitch + lines, :] = here_ref[at + row].astype(jnp.float32)
            for line in range(lines):
                column = ((line % layers) * (lines // layers) + line // layers) * LANES
                out = wide_ref[pl.ds(line, rows, stride=pitch), :].astype(jnp.bfloat16)
                flat_ref[pl.ds(at, rows), column : column + LANES] = out


def split_layers(train_grads):
    tr_rows, layers, width = train_grads.shape
    lines = layers * width // LANES
    by_line = train_grads.reshape(tr_rows, layers, width // LANES, LANES)
    by_line = by_line.transpose(0, 2, 1, 3).reshape(tr_rows, lines, LANES)
    return pl.pallas_call(
        functools.partial(split_kernel, layers),
        out_shape=jax.ShapeDtypeStruct((tr_rows, layers * width), jnp.bfloat16),
        in_specs=[pl.BlockSpec(memory_space=pltpu.HBM)],
        out_specs=VMEM,
        scratch_shapes=[
            pltpu.VMEM((tr_rows, lines, LANES), jnp.bfloat16),
            pltpu.VMEM((BLOCK * (lines + 8), LANES), jnp.float32),
            pltpu.SemaphoreType.DMA((8,)),
        ],
        compiler_params=pltpu.CompilerParams(vmem_limit_bytes=20 * MIB),
        cost_estimate=pl.CostEstimate(flops=10**9, bytes_accessed=16 * MIB, transcendentals=0),
        name="split",
    )(in_hbm(by_line))


def score_kernel(masks, t_ref, *refs):
    blocks, out_ref = refs[:-1], refs[-1]
    q_rows, width = blocks[0].shape
    n_query = len(masks) * q_rows
    depth = min(width, 1024)
    total = None
    for at in range(0, width, depth):
        block = jnp.concatenate([ref[:, at : at + depth] for ref in blocks], axis=0)
        term = mxu(t_ref[:, at : at + depth], block, NT)
        total = term if total is None else total + term

    me, g = lax.axis_index("train"), lax.axis_index("group")
    row = lax.broadcasted_iota(jnp.int32, (q_rows, n_query), 0)
    query = lax.broadcasted_iota(jnp.int32, (q_rows, n_query), 1)
    order = []
    for mask in masks:
        c0, c1 = (jnp.where(g == 0, mask[0][c], mask[1][c]) for c in range(CORES))
        source = me ^ jnp.where(me % CORES == 0, c0, c1)
        order.append(jnp.where(query == source * q_rows + row, 1.0, 0.0))
    order = jnp.concatenate(order, axis=0).astype(jnp.bfloat16)
    high, low = halves(total)
    lowest = (total - high.astype(jnp.float32) - low.astype(jnp.float32)).astype(jnp.bfloat16)
    out_ref[...] = mxu(high, order) + mxu(low, order) + mxu(lowest, order)


def came_masks(came):
    xors = came ^ np.arange(came.shape[1])[None]
    masks = [[int(xors[g, c]) for c in range(CORES)] for g in range(GROUPS)]
    assert all((xors[g, c::CORES] == masks[g][c]).all() for g in range(GROUPS) for c in range(CORES))
    return masks


def per_device(n_train, train_grads, query_grads, basis_in, basis_out, eigvals):
    tr_rows = train_grads.shape[0]
    zs = n_train // (XS * CORES)
    block = precondition(query_grads, basis_in, basis_out, eigvals)
    q_rows, width = block.shape
    own = Blocks(block, [np.tile(np.arange(n_train), (GROUPS, 1))])

    far = [own.hop(far_z(pair)) for pair in range(1, zs // 2)]
    at_x = own.hop(over_x)
    at_z = own.hop(over_z)
    twins = [own.hop(over_core)]
    train_grads, own = after(train_grads, own)
    flat_train = split_layers(train_grads)
    here = [own, at_x, at_z]
    for pair, one in enumerate(far):
        flat_train, one = after(flat_train, one)
        by_x, by_group = one.hop(over_x), one.hop(over_group)
        if pair == 0:
            one.array, at_x = after(one.array, at_x)
            at_xz = at_x.hop(over_z)
            twins.append(stack(at_x, one).hop(over_core))
            twins.append(stack(at_z, at_xz).hop(over_core))
            here.append(at_xz)
        else:
            twins.append(one.hop(over_core))
        twins.append(stack(by_x, by_group).hop(over_core))
        corner = beside(
            by_x.columns(0, width // 2).hop(over_group), by_group.columns(width // 2, width).hop(over_x)
        )
        twins.append(corner.hop(over_core))
        here += [one, by_x, by_group, corner]
    everything = here + twins
    masks = [came_masks(came) for a in everything for came in a.came]

    n_query = n_train * q_rows
    partial_scores = pl.pallas_call(
        functools.partial(score_kernel, masks),
        out_shape=jax.ShapeDtypeStruct((tr_rows, n_query), jnp.float32),
        in_specs=[VMEM] * (1 + len(everything)),
        out_specs=VMEM,
        compiler_params=pltpu.CompilerParams(vmem_limit_bytes=36 * MIB),
        cost_estimate=pl.CostEstimate(
            flops=2 * tr_rows * n_query * width, bytes_accessed=2 * width * (tr_rows + n_query), transcendentals=0
        ),
        name="scores",
    )(flat_train, *(a.array for a in everything))
    return lax.psum_scatter(partial_scores, "layer", scatter_dimension=1, tiled=True)


def solution(mesh):
    return jax.shard_map(
        functools.partial(per_device, mesh.shape["train"]),
        mesh=mesh,
        in_specs=(
            P(("group", "train"), "layer", None),
            P("train", "layer", None),
            P("layer", None, None),
            P("layer", None, None),
            P("layer", None),
        ),
        out_specs=P(("group", "train"), "layer"),
        check_vma=False,
    )
```

```python
import functools

import jax
import jax.numpy as jnp
import numpy as np
from jax import lax
from jax.experimental import pallas as pl
from jax.experimental.pallas import tpu as pltpu
from jax.sharding import PartitionSpec as P

CORES = 2
XS = 2
GROUPS = 2
LANES = 128
BLOCK = 16
MIB = 1024 * 1024
VMEM = pl.BlockSpec(memory_space=pltpu.VMEM)
NN = (((1,), (0,)), ((), ()))
NT = (((1,), (1,)), ((), ()))
TN = (((0,), (0,)), ((), ()))


def mxu(a, b, dims=NN):
    return lax.dot_general(a, b, dims, preferred_element_type=jnp.float32)


def halves(a):
    high = a.astype(jnp.bfloat16)
    return high, (a - high.astype(jnp.float32)).astype(jnp.bfloat16)


def in_hbm(array):
    return pltpu.with_memory_space_constraint(array, pltpu.HBM)


class Blocks:
    def __init__(self, array, came):
        self.array, self.came = array, came

    def hop(self, turn):
        groups, n_train = self.came[0].shape
        perm, came = [], [np.zeros_like(a) for a in self.came]
        for g in range(groups):
            for t in range(n_train):
                z, x, c = t // (XS * CORES), t // CORES % XS, t % CORES
                to_g, z, x, c = turn(g, z, x, c)
                to_t = (z * XS + x) * CORES + c
                perm.append((g * n_train + t, to_g * n_train + to_t))
                for here, there in zip(self.came, came):
                    there[to_g, to_t] = here[g, t]
        return Blocks(lax.ppermute(self.array, ("group", "train"), perm), came)

    def columns(self, start, stop):
        return Blocks(self.array[:, start:stop], self.came)


def stack(*parts):
    return Blocks(jnp.concatenate([a.array for a in parts], axis=0), sum((a.came for a in parts), []))


def beside(left, right):
    assert all((a == b).all() for a, b in zip(left.came, right.came))
    return Blocks(jnp.concatenate([left.array, right.array], axis=1), left.came)


def after(kernel_result, *parts):
    arrays, kernel_result = lax.optimization_barrier(([a.array for a in parts], kernel_result))
    return kernel_result, *(Blocks(array, a.came) for array, a in zip(arrays, parts))


def over_core(g, z, x, c):
    return g, z, x, c ^ 1


def over_x(g, z, x, c):
    return g, z, x ^ 1, c


def over_z(g, z, x, c):
    return g, z ^ 1, x, c


def far_z(pair):
    return lambda g, z, x, c: (g, z ^ (2 * pair + 1 - g), x, c)


def over_group(g, z, x, c):
    return g ^ 1, z, x, c


def precond_kernel(q_ref, in_ref, out_ref, eig_ref, block_ref, lines_ref, *scratch):
    q_rows, lines, _ = q_ref.shape
    pitch = lines_ref.shape[0] // q_rows
    for q in range(q_rows):
        lines_ref[q * pitch : q * pitch + lines, :] = q_ref[q].astype(jnp.float32)
    for layer in range(in_ref.shape[0]):
        precond_layer(layer, lines_ref, in_ref, out_ref, eig_ref, block_ref, *(ref.at[layer] for ref in scratch))


def precond_layer(layer, lines_ref, in_ref, out_ref, eig_ref, block_ref, wide_ref, tall_ref, even_ref):
    q_rows = block_ref.shape[0]
    layers, width = eig_ref.shape
    rows = width // LANES
    pitch = lines_ref.shape[0] // q_rows
    p_in, p_out = in_ref.shape[1:]
    left = lax.broadcasted_iota(jnp.int32, (1, LANES), 1) < p_out

    eig = eig_ref[layer : layer + 1, :]
    damping = 0.1 / width * jnp.sum(eig, axis=1, keepdims=True)
    for j in range(rows):
        pair = eig[:, j * LANES : (j + 1) * LANES]
        turned = pltpu.roll(pair, p_out, 1)
        even_ref[2 * j : 2 * j + 1, :] = jnp.where(left, pair, turned)
        even_ref[2 * j + 1 : 2 * j + 2, :] = jnp.where(left, turned, pair)
    scale = 1.0 / (even_ref[...] + damping)

    by_row = [in_ref[layer, pl.ds(p, rows, stride=2), :] for p in range(2)]
    back_left = jnp.concatenate(by_row, axis=0)
    fore_left = jnp.concatenate(by_row, axis=1)
    back_high, back_low = halves(back_left)
    fore_high, fore_low = halves(fore_left)
    fore = jnp.concatenate([fore_high, fore_high, fore_low], axis=0)
    back = jnp.concatenate([back_high, back_high, back_low], axis=1)

    basis = out_ref[layer]
    empty = jnp.zeros((p_out, p_out), jnp.bfloat16)

    def twice(a):
        return jnp.concatenate(
            [jnp.concatenate([a, empty], axis=1), jnp.concatenate([empty, a], axis=1)], axis=0
        )

    right_high, right_low = halves(basis)
    turned_high, turned_low = halves(basis.T)
    fore_right = jnp.concatenate([twice(right_high), twice(right_low)], axis=1)
    back_high, back_low = twice(turned_high), twice(turned_low)
    back_right = jnp.concatenate(
        [
            jnp.concatenate([back_high, back_low], axis=1),
            jnp.concatenate([back_high, jnp.zeros_like(back_low)], axis=1),
        ],
        axis=0,
    )

    stacked = jnp.concatenate(
        [lines_ref[pl.ds(layers * j + layer, q_rows, stride=pitch), :] for j in range(rows)], axis=0
    ).astype(jnp.bfloat16)
    both = mxu(stacked, fore_right)
    wide_ref[...] = both[:, :LANES] + both[:, LANES:]
    by_query = jnp.concatenate([wide_ref[pl.ds(q, rows, stride=q_rows), :] for q in range(q_rows)], axis=1)
    high, low = halves(by_query)
    both = mxu(fore, jnp.concatenate([high, low, high], axis=0), TN)
    every = jnp.concatenate([left] * q_rows, axis=1)
    rotated = jnp.where(every, both[:p_in], both[p_in:])
    rotated = jnp.concatenate(
        [
            part + pltpu.roll(part, p_out, 1)
            for part in (rotated[:, q * LANES : (q + 1) * LANES] for q in range(q_rows))
        ],
        axis=1,
    )
    scaled = rotated * jnp.concatenate([scale] * q_rows, axis=1)
    high, low = halves(scaled)
    both = mxu(back, jnp.concatenate([high, low, high], axis=0))
    mixed = jnp.where(every, both[:rows], both[rows:])
    stacked = jnp.concatenate([mixed[:, q * LANES : (q + 1) * LANES] for q in range(q_rows)], axis=0)
    both = mxu(jnp.concatenate(halves(stacked), axis=1), back_right)
    tall_ref[...] = both[:, :LANES] + both[:, LANES:]
    for j in range(rows):
        block = tall_ref[pl.ds(j, q_rows, stride=rows), :]
        column = layer * width + j * LANES
        block_ref[:, column : column + LANES] = block.astype(jnp.bfloat16)


def by_lines(array):
    rows, layers, width = array.shape
    array = array.reshape(rows, layers, width // LANES, LANES)
    return array.transpose(0, 2, 1, 3).reshape(rows, -1, LANES)


def precondition(queries, basis_in, basis_out, eigvals, here=False):
    q_rows, lines, _ = queries.shape
    layers, width = eigvals.shape
    operands, body, scratch = [queries, basis_in, basis_out, eigvals], precond_kernel, []
    if not here:
        operands = [in_hbm(a) for a in operands]
        body = functools.partial(fetched, len(operands), body)
        scratch = [pltpu.VMEM(a.shape, a.dtype) for a in operands] + [pltpu.SemaphoreType.DMA((len(operands),))]
    space = pltpu.VMEM if here else pltpu.HBM
    return pl.pallas_call(
        body,
        out_shape=jax.ShapeDtypeStruct((q_rows, layers * width), jnp.bfloat16),
        in_specs=[pl.BlockSpec(memory_space=space)] * len(operands),
        out_specs=VMEM,
        scratch_shapes=[
            pltpu.VMEM((q_rows * (lines + 8), LANES), jnp.float32),
            pltpu.VMEM((layers, q_rows * width // LANES, LANES), jnp.float32),
            pltpu.VMEM((layers, q_rows * width // LANES, LANES), jnp.float32),
            pltpu.VMEM((layers, 2 * width // LANES, LANES), jnp.float32),
        ]
        + scratch,
        compiler_params=pltpu.CompilerParams(vmem_limit_bytes=16 * MIB),
        cost_estimate=pl.CostEstimate(flops=10**9, bytes_accessed=4 * MIB, transcendentals=0),
        name="precond",
    )(*operands)


def fetched(n, body, *refs):
    operands, others = refs[:n], refs[n:]
    others, here, sems = others[: -n - 1], others[-n - 1 : -1], others[-1]
    copies = [pltpu.make_async_copy(a, b, sems.at[i]) for i, (a, b) in enumerate(zip(operands, here))]
    for copy in copies:
        copy.start()
    for copy in copies:
        copy.wait()
    body(*here, *others)


def split_kernel(layers, t_ref, flat_ref, here_ref, wide_ref, sems):
    rows, chunks = BLOCK, sems.shape[0]
    lines = t_ref.shape[1]
    pitch = wide_ref.shape[0] // rows
    chunk = t_ref.shape[0] // chunks
    copies = [
        pltpu.make_async_copy(
            t_ref.at[pl.ds(i * chunk, chunk)], here_ref.at[pl.ds(i * chunk, chunk)], sems.at[i]
        )
        for i in range(chunks)
    ]
    for copy in copies:
        copy.start()
    for i in range(chunks):
        copies[i].wait()

        @pl.loop(i * chunk // rows, (i + 1) * chunk // rows)
        def _(block):
            at = pl.multiple_of(block * rows, rows)
            for row in range(rows):
                wide_ref[row * pitch : row * pitch + lines, :] = here_ref[at + row].astype(jnp.float32)
            for line in range(lines):
                column = ((line % layers) * (lines // layers) + line // layers) * LANES
                out = wide_ref[pl.ds(line, rows, stride=pitch), :].astype(jnp.bfloat16)
                flat_ref[pl.ds(at, rows), column : column + LANES] = out


def split_layers(train_grads):
    tr_rows, layers, width = train_grads.shape
    lines = layers * width // LANES
    return pl.pallas_call(
        functools.partial(split_kernel, layers),
        out_shape=jax.ShapeDtypeStruct((tr_rows, layers * width), jnp.bfloat16),
        in_specs=[pl.BlockSpec(memory_space=pltpu.HBM)],
        out_specs=VMEM,
        scratch_shapes=[
            pltpu.VMEM((tr_rows, lines, LANES), jnp.bfloat16),
            pltpu.VMEM((BLOCK * (lines + 8), LANES), jnp.float32),
            pltpu.SemaphoreType.DMA((8,)),
        ],
        compiler_params=pltpu.CompilerParams(vmem_limit_bytes=20 * MIB),
        cost_estimate=pl.CostEstimate(flops=10**9, bytes_accessed=16 * MIB, transcendentals=0),
        name="split",
    )(in_hbm(by_lines(train_grads)))


def score_kernel(masks, t_ref, *refs):
    blocks, out_ref = refs[:-1], refs[-1]
    q_rows, width = blocks[0].shape
    n_query = len(masks) * q_rows
    depth = min(width, 1024)
    total = None
    for at in range(0, width, depth):
        block = jnp.concatenate([ref[:, at : at + depth] for ref in blocks], axis=0)
        term = mxu(t_ref[:, at : at + depth], block, NT)
        total = term if total is None else total + term

    me, g = lax.axis_index("train"), lax.axis_index("group")
    row = lax.broadcasted_iota(jnp.int32, (q_rows, n_query), 0)
    query = lax.broadcasted_iota(jnp.int32, (q_rows, n_query), 1)
    order = []
    for mask in masks:
        c0, c1 = (jnp.where(g == 0, mask[0][c], mask[1][c]) for c in range(CORES))
        source = me ^ jnp.where(me % CORES == 0, c0, c1)
        order.append(jnp.where(query == source * q_rows + row, 1.0, 0.0))
    order = jnp.concatenate(order, axis=0).astype(jnp.bfloat16)
    high, low = halves(total)
    lowest = (total - high.astype(jnp.float32) - low.astype(jnp.float32)).astype(jnp.bfloat16)
    out_ref[...] = mxu(high, order) + mxu(low, order) + mxu(lowest, order)


def came_masks(came):
    xors = came ^ np.arange(came.shape[1])[None]
    masks = [[int(xors[g, c]) for c in range(CORES)] for g in range(GROUPS)]
    assert all((xors[g, c::CORES] == masks[g][c]).all() for g in range(GROUPS) for c in range(CORES))
    return masks


def per_device(n_train, train_grads, query_grads, basis_in, basis_out, eigvals):
    tr_rows = train_grads.shape[0]
    zs = n_train // (XS * CORES)
    rest = basis_in, basis_out, eigvals
    queries = by_lines(query_grads)
    places = [np.tile(np.arange(n_train), (GROUPS, 1))]
    far = [Blocks(queries, places).hop(far_z(pair)) for pair in range(1, zs // 2)]
    own = Blocks(precondition(queries, *rest), places)
    q_rows, width = own.array.shape
    at_x = own.hop(over_x)
    at_z = own.hop(over_z)
    twins = [own.hop(over_core)]
    train_grads, own = after(train_grads, own)
    flat_train = split_layers(train_grads)
    here = [own, at_x, at_z]
    for pair, one in enumerate(far):
        flat_train, one = after(flat_train, one)
        one = Blocks(precondition(one.array, *rest, here=True), one.came)
        by_x, by_group = one.hop(over_x), one.hop(over_group)
        if pair == 0:
            one.array, at_x = after(one.array, at_x)
            at_xz = at_x.hop(over_z)
            twins.append(stack(at_x, one).hop(over_core))
            twins.append(stack(at_z, at_xz).hop(over_core))
            here.append(at_xz)
        else:
            twins.append(one.hop(over_core))
        twins.append(stack(by_x, by_group).hop(over_core))
        corner = beside(
            by_x.columns(0, width // 2).hop(over_group), by_group.columns(width // 2, width).hop(over_x)
        )
        twins.append(corner.hop(over_core))
        here += [one, by_x, by_group, corner]
    everything = here + twins
    masks = [came_masks(came) for a in everything for came in a.came]

    n_query = n_train * q_rows
    partial_scores = pl.pallas_call(
        functools.partial(score_kernel, masks),
        out_shape=jax.ShapeDtypeStruct((tr_rows, n_query), jnp.float32),
        in_specs=[VMEM] * (1 + len(everything)),
        out_specs=VMEM,
        compiler_params=pltpu.CompilerParams(vmem_limit_bytes=36 * MIB),
        cost_estimate=pl.CostEstimate(
            flops=2 * tr_rows * n_query * width, bytes_accessed=2 * width * (tr_rows + n_query), transcendentals=0
        ),
        name="scores",
    )(flat_train, *(a.array for a in everything))
    return lax.psum_scatter(partial_scores, "layer", scatter_dimension=1, tiled=True)


def solution(mesh):
    return jax.shard_map(
        functools.partial(per_device, mesh.shape["train"]),
        mesh=mesh,
        in_specs=(
            P(("group", "train"), "layer", None),
            P("train", "layer", None),
            P("layer", None, None),
            P("layer", None, None),
            P("layer", None),
        ),
        out_specs=P(("group", "train"), "layer"),
        check_vma=False,
    )
```

```python
import functools

import jax
import jax.numpy as jnp
import numpy as np
from jax import lax
from jax.experimental import pallas as pl
from jax.experimental.pallas import tpu as pltpu
from jax.sharding import PartitionSpec as P

CORES = 2
XS = 2
GROUPS = 2
LANES = 128
BLOCK = 16
MIB = 1024 * 1024
VMEM = pl.BlockSpec(memory_space=pltpu.VMEM)
NN = (((1,), (0,)), ((), ()))
NT = (((1,), (1,)), ((), ()))
TN = (((0,), (0,)), ((), ()))


def mxu(a, b, dims=NN):
    return lax.dot_general(a, b, dims, preferred_element_type=jnp.float32)


def halves(a):
    high = a.astype(jnp.bfloat16)
    return high, (a - high.astype(jnp.float32)).astype(jnp.bfloat16)


def in_hbm(array):
    return pltpu.with_memory_space_constraint(array, pltpu.HBM)


class Blocks:
    def __init__(self, array, came):
        self.array, self.came = array, came

    def hop(self, turn):
        groups, n_train = self.came[0].shape
        perm, came = [], [np.zeros_like(a) for a in self.came]
        for g in range(groups):
            for t in range(n_train):
                z, x, c = t // (XS * CORES), t // CORES % XS, t % CORES
                to_g, z, x, c = turn(g, z, x, c)
                to_t = (z * XS + x) * CORES + c
                perm.append((g * n_train + t, to_g * n_train + to_t))
                for here, there in zip(self.came, came):
                    there[to_g, to_t] = here[g, t]
        return Blocks(lax.ppermute(self.array, ("group", "train"), perm), came)

    def columns(self, start, stop):
        return Blocks(self.array[:, start:stop], self.came)


def stack(*parts):
    return Blocks(jnp.concatenate([a.array for a in parts], axis=0), sum((a.came for a in parts), []))


def beside(left, right):
    assert all((a == b).all() for a, b in zip(left.came, right.came))
    return Blocks(jnp.concatenate([left.array, right.array], axis=1), left.came)


def after(kernel_result, *parts):
    arrays, kernel_result = lax.optimization_barrier(([a.array for a in parts], kernel_result))
    return kernel_result, *(Blocks(array, a.came) for array, a in zip(arrays, parts))


def over_core(g, z, x, c):
    return g, z, x, c ^ 1


def over_x(g, z, x, c):
    return g, z, x ^ 1, c


def over_z(g, z, x, c):
    return g, z ^ 1, x, c


def far_z(pair):
    return lambda g, z, x, c: (g, z ^ (2 * pair + 1 - g), x, c)


def over_group(g, z, x, c):
    return g ^ 1, z, x, c


def precond_kernel(q_ref, in_ref, out_ref, eig_ref, block_ref, lines_ref, *scratch):
    q_rows, lines, _ = q_ref.shape
    pitch = lines_ref.shape[0] // q_rows
    for q in range(q_rows):
        lines_ref[q * pitch : q * pitch + lines, :] = q_ref[q].astype(jnp.float32)
    for layer in range(in_ref.shape[0]):
        precond_layer(layer, lines_ref, in_ref, out_ref, eig_ref, block_ref, *(ref.at[layer] for ref in scratch))


def precond_layer(layer, lines_ref, in_ref, out_ref, eig_ref, block_ref, wide_ref, tall_ref, even_ref):
    q_rows = block_ref.shape[0]
    layers, width = eig_ref.shape
    rows = width // LANES
    pitch = lines_ref.shape[0] // q_rows
    p_in, p_out = in_ref.shape[1:]
    left = lax.broadcasted_iota(jnp.int32, (1, LANES), 1) < p_out

    eig = eig_ref[layer : layer + 1, :]
    damping = 0.1 / width * jnp.sum(eig, axis=1, keepdims=True)
    for j in range(rows):
        pair = eig[:, j * LANES : (j + 1) * LANES]
        turned = pltpu.roll(pair, p_out, 1)
        even_ref[2 * j : 2 * j + 1, :] = jnp.where(left, pair, turned)
        even_ref[2 * j + 1 : 2 * j + 2, :] = jnp.where(left, turned, pair)
    scale = 1.0 / (even_ref[...] + damping)

    by_row = [in_ref[layer, pl.ds(p, rows, stride=2), :] for p in range(2)]
    back_left = jnp.concatenate(by_row, axis=0)
    fore_left = jnp.concatenate(by_row, axis=1)
    back_high, back_low = halves(back_left)
    fore_high, fore_low = halves(fore_left)
    fore = jnp.concatenate([fore_high, fore_high, fore_low], axis=0)
    back = jnp.concatenate([back_high, back_high, back_low], axis=1)

    basis = out_ref[layer]
    empty = jnp.zeros((p_out, p_out), jnp.bfloat16)

    def twice(a):
        return jnp.concatenate(
            [jnp.concatenate([a, empty], axis=1), jnp.concatenate([empty, a], axis=1)], axis=0
        )

    right_high, right_low = halves(basis)
    turned_high, turned_low = halves(basis.T)
    fore_right = jnp.concatenate([twice(right_high), twice(right_low)], axis=1)
    back_high, back_low = twice(turned_high), twice(turned_low)
    back_right = jnp.concatenate(
        [
            jnp.concatenate([back_high, back_low], axis=1),
            jnp.concatenate([back_high, jnp.zeros_like(back_low)], axis=1),
        ],
        axis=0,
    )

    stacked = jnp.concatenate(
        [lines_ref[pl.ds(layers * j + layer, q_rows, stride=pitch), :] for j in range(rows)], axis=0
    ).astype(jnp.bfloat16)
    both = mxu(stacked, fore_right)
    wide_ref[...] = both[:, :LANES] + both[:, LANES:]
    by_query = jnp.concatenate([wide_ref[pl.ds(q, rows, stride=q_rows), :] for q in range(q_rows)], axis=1)
    high, low = halves(by_query)
    both = mxu(fore, jnp.concatenate([high, low, high], axis=0), TN)
    every = jnp.concatenate([left] * q_rows, axis=1)
    rotated = jnp.where(every, both[:p_in], both[p_in:])
    rotated = jnp.concatenate(
        [
            part + pltpu.roll(part, p_out, 1)
            for part in (rotated[:, q * LANES : (q + 1) * LANES] for q in range(q_rows))
        ],
        axis=1,
    )
    scaled = rotated * jnp.concatenate([scale] * q_rows, axis=1)
    high, low = halves(scaled)
    both = mxu(back, jnp.concatenate([high, low, high], axis=0))
    mixed = jnp.where(every, both[:rows], both[rows:])
    stacked = jnp.concatenate([mixed[:, q * LANES : (q + 1) * LANES] for q in range(q_rows)], axis=0)
    both = mxu(jnp.concatenate(halves(stacked), axis=1), back_right)
    tall_ref[...] = both[:, :LANES] + both[:, LANES:]
    for j in range(rows):
        block = tall_ref[pl.ds(j, q_rows, stride=rows), :]
        column = layer * width + j * LANES
        block_ref[:, column : column + LANES] = block.astype(jnp.bfloat16)


def by_lines(array):
    rows, layers, width = array.shape
    array = array.reshape(rows, layers, width // LANES, LANES)
    return array.transpose(0, 2, 1, 3).reshape(rows, -1, LANES)


def precondition(queries, basis_in, basis_out, eigvals, here=False):
    q_rows, lines, _ = queries.shape
    layers, width = eigvals.shape
    operands, body, scratch = [queries, basis_in, basis_out, eigvals], precond_kernel, []
    if not here:
        operands = [in_hbm(a) for a in operands]
        body = functools.partial(fetched, len(operands), body)
        scratch = [pltpu.VMEM(a.shape, a.dtype) for a in operands] + [pltpu.SemaphoreType.DMA((len(operands),))]
    space = pltpu.VMEM if here else pltpu.HBM
    return pl.pallas_call(
        body,
        out_shape=jax.ShapeDtypeStruct((q_rows, layers * width), jnp.bfloat16),
        in_specs=[pl.BlockSpec(memory_space=space)] * len(operands),
        out_specs=VMEM,
        scratch_shapes=[
            pltpu.VMEM((q_rows * (lines + 8), LANES), jnp.float32),
            pltpu.VMEM((layers, q_rows * width // LANES, LANES), jnp.float32),
            pltpu.VMEM((layers, q_rows * width // LANES, LANES), jnp.float32),
            pltpu.VMEM((layers, 2 * width // LANES, LANES), jnp.float32),
        ]
        + scratch,
        compiler_params=pltpu.CompilerParams(vmem_limit_bytes=16 * MIB),
        cost_estimate=pl.CostEstimate(flops=10**9, bytes_accessed=4 * MIB, transcendentals=0),
        name="precond",
    )(*operands)


def fetched(n, body, *refs):
    operands, others = refs[:n], refs[n:]
    others, here, sems = others[: -n - 1], others[-n - 1 : -1], others[-1]
    copies = [pltpu.make_async_copy(a, b, sems.at[i]) for i, (a, b) in enumerate(zip(operands, here))]
    for copy in copies:
        copy.start()
    for copy in copies:
        copy.wait()
    body(*here, *others)


def split_kernel(layers, t_ref, flat_ref, here_ref, wide_ref, sems):
    rows, chunks = BLOCK, sems.shape[0]
    lines = t_ref.shape[1]
    pitch = wide_ref.shape[0] // rows
    chunk = t_ref.shape[0] // chunks
    copies = [
        pltpu.make_async_copy(
            t_ref.at[pl.ds(i * chunk, chunk)], here_ref.at[pl.ds(i * chunk, chunk)], sems.at[i]
        )
        for i in range(chunks)
    ]
    for copy in copies:
        copy.start()
    for i in range(chunks):
        copies[i].wait()

        @pl.loop(i * chunk // rows, (i + 1) * chunk // rows)
        def _(block):
            at = pl.multiple_of(block * rows, rows)
            for row in range(rows):
                wide_ref[row * pitch : row * pitch + lines, :] = here_ref[at + row].astype(jnp.float32)
            for line in range(lines):
                column = ((line % layers) * (lines // layers) + line // layers) * LANES
                out = wide_ref[pl.ds(line, rows, stride=pitch), :].astype(jnp.bfloat16)
                flat_ref[pl.ds(at, rows), column : column + LANES] = out


def split_layers(train_grads):
    tr_rows, layers, width = train_grads.shape
    lines = layers * width // LANES
    return pl.pallas_call(
        functools.partial(split_kernel, layers),
        out_shape=jax.ShapeDtypeStruct((tr_rows, layers * width), jnp.bfloat16),
        in_specs=[pl.BlockSpec(memory_space=pltpu.HBM)],
        out_specs=VMEM,
        scratch_shapes=[
            pltpu.VMEM((tr_rows, lines, LANES), jnp.bfloat16),
            pltpu.VMEM((BLOCK * (lines + 8), LANES), jnp.float32),
            pltpu.SemaphoreType.DMA((8,)),
        ],
        compiler_params=pltpu.CompilerParams(vmem_limit_bytes=20 * MIB),
        cost_estimate=pl.CostEstimate(flops=10**9, bytes_accessed=16 * MIB, transcendentals=0),
        name="split",
    )(in_hbm(by_lines(train_grads)))


def score_kernel(masks, added, t_ref, *refs):
    blocks, out_ref = refs[added:-1], refs[-1]
    q_rows, width = sum(ref.shape[0] for ref in blocks) // len(masks), t_ref.shape[1]
    n_query = out_ref.shape[1]
    depth = min(width, 1024)
    total = None
    for at in range(0, width, depth):
        block = jnp.concatenate([ref[:, at : at + depth] for ref in blocks], axis=0)
        term = mxu(t_ref[:, at : at + depth], block, NT)
        total = term if total is None else total + term

    me, g = lax.axis_index("train"), lax.axis_index("group")
    row = lax.broadcasted_iota(jnp.int32, (q_rows, n_query), 0)
    query = lax.broadcasted_iota(jnp.int32, (q_rows, n_query), 1)
    order = []
    for mask in masks:
        c0, c1 = (jnp.where(g == 0, mask[0][c], mask[1][c]) for c in range(CORES))
        source = me ^ jnp.where(me % CORES == 0, c0, c1)
        order.append(jnp.where(query == source * q_rows + row, 1.0, 0.0))
    order = jnp.concatenate(order, axis=0).astype(jnp.bfloat16)
    high, low = halves(total)
    lowest = (total - high.astype(jnp.float32) - low.astype(jnp.float32)).astype(jnp.bfloat16)
    placed = mxu(high, order) + mxu(low, order) + mxu(lowest, order)
    out_ref[...] = refs[0][...] + placed if added else placed


def scores(flat_train, parts, n_query, earlier=None):
    tr_rows, width = flat_train.shape
    masks = [came_masks(came) for a in parts for came in a.came]
    operands = [flat_train] + ([] if earlier is None else [earlier]) + [a.array for a in parts]
    rows = sum(a.array.shape[0] for a in parts)
    return pl.pallas_call(
        functools.partial(score_kernel, masks, 0 if earlier is None else 1),
        out_shape=jax.ShapeDtypeStruct((tr_rows, n_query), jnp.float32),
        in_specs=[VMEM] * len(operands),
        out_specs=VMEM,
        compiler_params=pltpu.CompilerParams(vmem_limit_bytes=32 * MIB),
        cost_estimate=pl.CostEstimate(
            flops=2 * tr_rows * n_query * width, bytes_accessed=2 * width * (tr_rows + rows), transcendentals=0
        ),
        name="scores",
    )(*operands)


def came_masks(came):
    xors = came ^ np.arange(came.shape[1])[None]
    masks = [[int(xors[g, c]) for c in range(CORES)] for g in range(GROUPS)]
    assert all((xors[g, c::CORES] == masks[g][c]).all() for g in range(GROUPS) for c in range(CORES))
    return masks


def per_device(n_train, train_grads, query_grads, basis_in, basis_out, eigvals):
    zs = n_train // (XS * CORES)
    rest = basis_in, basis_out, eigvals
    queries = by_lines(query_grads)
    places = [np.tile(np.arange(n_train), (GROUPS, 1))]
    far = [Blocks(queries, places).hop(far_z(pair)) for pair in range(1, zs // 2)]
    own = Blocks(precondition(queries, *rest), places)
    q_rows, width = own.array.shape
    n_query = n_train * q_rows
    at_x = own.hop(over_x)
    twin = own.hop(over_core)
    train_grads, own = after(train_grads, own)
    flat_train = split_layers(train_grads)
    flat_train, own = after(flat_train, own)
    at_z = own.hop(over_z)
    early, parts = [own, twin], [at_z]
    for pair, one in enumerate(far):
        flat_train, one = after(flat_train, one)
        one = Blocks(precondition(one.array, *rest, here=True), one.came)
        by_x, by_group = one.hop(over_x), one.hop(over_group)
        if pair == 0:
            one.array, at_x = after(one.array, at_x)
            at_xz = at_x.hop(over_z)
            early += [at_x, one]
            first_scores = scores(flat_train, early, n_query)
            first_scores, by_x = after(first_scores, by_x)
            parts.append(stack(at_x, one).hop(over_core))
            parts.append(at_xz)
        else:
            parts += [one, one.hop(over_core)]
        parts.append(stack(by_x, by_group).hop(over_core))
        half = by_x.columns(0, width // 2).hop(over_group)
        if pair == 0:
            half.array, near, near_x = after(half.array, at_z, at_xz)
            parts.append(stack(near, near_x).hop(over_core))
        corner = beside(half, by_group.columns(width // 2, width).hop(over_x))
        parts += [by_x, by_group, corner, corner.hop(over_core)]
    partial_scores = scores(flat_train, parts, n_query, first_scores)
    return lax.psum_scatter(partial_scores, "layer", scatter_dimension=1, tiled=True)


def solution(mesh):
    return jax.shard_map(
        functools.partial(per_device, mesh.shape["train"]),
        mesh=mesh,
        in_specs=(
            P(("group", "train"), "layer", None),
            P("train", "layer", None),
            P("layer", None, None),
            P("layer", None, None),
            P("layer", None),
        ),
        out_specs=P(("group", "train"), "layer"),
        check_vma=False,
    )
```

```python
import functools

import jax
import jax.numpy as jnp
import numpy as np
from jax import lax
from jax.experimental import pallas as pl
from jax.experimental.pallas import tpu as pltpu
from jax.sharding import PartitionSpec as P

CORES = 2
XS = 2
GROUPS = 2
LANES = 128
BLOCK = 16
MIB = 1024 * 1024
VMEM = pl.BlockSpec(memory_space=pltpu.VMEM)
NN = (((1,), (0,)), ((), ()))
NT = (((1,), (1,)), ((), ()))
TN = (((0,), (0,)), ((), ()))


def mxu(a, b, dims=NN):
    return lax.dot_general(a, b, dims, preferred_element_type=jnp.float32)


def halves(a):
    high = a.astype(jnp.bfloat16)
    return high, (a - high.astype(jnp.float32)).astype(jnp.bfloat16)


def in_hbm(array):
    return pltpu.with_memory_space_constraint(array, pltpu.HBM)


class Blocks:
    def __init__(self, array, came):
        self.array, self.came = array, came

    def hop(self, turn):
        groups, n_train = self.came[0].shape
        perm, came = [], [np.zeros_like(a) for a in self.came]
        for g in range(groups):
            for t in range(n_train):
                z, x, c = t // (XS * CORES), t // CORES % XS, t % CORES
                to_g, z, x, c = turn(g, z, x, c)
                to_t = (z * XS + x) * CORES + c
                perm.append((g * n_train + t, to_g * n_train + to_t))
                for here, there in zip(self.came, came):
                    there[to_g, to_t] = here[g, t]
        return Blocks(lax.ppermute(self.array, ("group", "train"), perm), came)

    def columns(self, start, stop):
        return Blocks(self.array[:, start:stop], self.came)


def stack(*parts):
    return Blocks(jnp.concatenate([a.array for a in parts], axis=0), sum((a.came for a in parts), []))


def beside(left, right):
    assert all((a == b).all() for a, b in zip(left.came, right.came))
    return Blocks(jnp.concatenate([left.array, right.array], axis=1), left.came)


def after(kernel_result, *parts):
    arrays, kernel_result = lax.optimization_barrier(([a.array for a in parts], kernel_result))
    return kernel_result, *(Blocks(array, a.came) for array, a in zip(arrays, parts))


def over_core(g, z, x, c):
    return g, z, x, c ^ 1


def over_x(g, z, x, c):
    return g, z, x ^ 1, c


def over_z(g, z, x, c):
    return g, z ^ 1, x, c


def far_z(pair):
    return lambda g, z, x, c: (g, z ^ (2 * pair + (g == c)), x, c)


def over_group(g, z, x, c):
    return g ^ 1, z, x, c


def precond_kernel(q_ref, in_ref, out_ref, eig_ref, block_ref, lines_ref, *scratch):
    q_rows, lines, _ = q_ref.shape
    pitch = lines_ref.shape[0] // q_rows
    for q in range(q_rows):
        lines_ref[q * pitch : q * pitch + lines, :] = q_ref[q].astype(jnp.float32)
    for layer in range(in_ref.shape[0]):
        precond_layer(layer, lines_ref, in_ref, out_ref, eig_ref, block_ref, *(ref.at[layer] for ref in scratch))


def precond_layer(layer, lines_ref, in_ref, out_ref, eig_ref, block_ref, wide_ref, tall_ref, even_ref):
    q_rows = block_ref.shape[0]
    layers, width = eig_ref.shape
    rows = width // LANES
    pitch = lines_ref.shape[0] // q_rows
    p_in, p_out = in_ref.shape[1:]
    left = lax.broadcasted_iota(jnp.int32, (1, LANES), 1) < p_out

    eig = eig_ref[layer : layer + 1, :]
    damping = 0.1 / width * jnp.sum(eig, axis=1, keepdims=True)
    for j in range(rows):
        pair = eig[:, j * LANES : (j + 1) * LANES]
        turned = pltpu.roll(pair, p_out, 1)
        even_ref[2 * j : 2 * j + 1, :] = jnp.where(left, pair, turned)
        even_ref[2 * j + 1 : 2 * j + 2, :] = jnp.where(left, turned, pair)
    scale = 1.0 / (even_ref[...] + damping)

    by_row = [in_ref[layer, pl.ds(p, rows, stride=2), :] for p in range(2)]
    back_left = jnp.concatenate(by_row, axis=0)
    fore_left = jnp.concatenate(by_row, axis=1)
    back_high, back_low = halves(back_left)
    fore_high, fore_low = halves(fore_left)
    fore = jnp.concatenate([fore_high, fore_high, fore_low], axis=0)
    back = jnp.concatenate([back_high, back_high, back_low], axis=1)

    basis = out_ref[layer]
    empty = jnp.zeros((p_out, p_out), jnp.bfloat16)

    def twice(a):
        return jnp.concatenate(
            [jnp.concatenate([a, empty], axis=1), jnp.concatenate([empty, a], axis=1)], axis=0
        )

    right_high, right_low = halves(basis)
    turned_high, turned_low = halves(basis.T)
    fore_right = jnp.concatenate([twice(right_high), twice(right_low)], axis=1)
    back_high, back_low = twice(turned_high), twice(turned_low)
    back_right = jnp.concatenate(
        [
            jnp.concatenate([back_high, back_low], axis=1),
            jnp.concatenate([back_high, jnp.zeros_like(back_low)], axis=1),
        ],
        axis=0,
    )

    stacked = jnp.concatenate(
        [lines_ref[pl.ds(layers * j + layer, q_rows, stride=pitch), :] for j in range(rows)], axis=0
    ).astype(jnp.bfloat16)
    both = mxu(stacked, fore_right)
    wide_ref[...] = both[:, :LANES] + both[:, LANES:]
    by_query = jnp.concatenate([wide_ref[pl.ds(q, rows, stride=q_rows), :] for q in range(q_rows)], axis=1)
    high, low = halves(by_query)
    both = mxu(fore, jnp.concatenate([high, low, high], axis=0), TN)
    every = jnp.concatenate([left] * q_rows, axis=1)
    rotated = jnp.where(every, both[:p_in], both[p_in:])
    rotated = jnp.concatenate(
        [
            part + pltpu.roll(part, p_out, 1)
            for part in (rotated[:, q * LANES : (q + 1) * LANES] for q in range(q_rows))
        ],
        axis=1,
    )
    scaled = rotated * jnp.concatenate([scale] * q_rows, axis=1)
    high, low = halves(scaled)
    both = mxu(back, jnp.concatenate([high, low, high], axis=0))
    mixed = jnp.where(every, both[:rows], both[rows:])
    stacked = jnp.concatenate([mixed[:, q * LANES : (q + 1) * LANES] for q in range(q_rows)], axis=0)
    both = mxu(jnp.concatenate(halves(stacked), axis=1), back_right)
    tall_ref[...] = both[:, :LANES] + both[:, LANES:]
    for j in range(rows):
        block = tall_ref[pl.ds(j, q_rows, stride=rows), :]
        column = layer * width + j * LANES
        block_ref[:, column : column + LANES] = block.astype(jnp.bfloat16)


def by_lines(array):
    rows, layers, width = array.shape
    array = array.reshape(rows, layers, width // LANES, LANES)
    return array.transpose(0, 2, 1, 3).reshape(rows, -1, LANES)


def precondition(queries, basis_in, basis_out, eigvals, here=False):
    q_rows, lines, _ = queries.shape
    layers, width = eigvals.shape
    operands, body, scratch = [queries, basis_in, basis_out, eigvals], precond_kernel, []
    if not here:
        operands = [in_hbm(a) for a in operands]
        body = functools.partial(fetched, len(operands), body)
        scratch = [pltpu.VMEM(a.shape, a.dtype) for a in operands] + [pltpu.SemaphoreType.DMA((len(operands),))]
    space = pltpu.VMEM if here else pltpu.HBM
    return pl.pallas_call(
        body,
        out_shape=jax.ShapeDtypeStruct((q_rows, layers * width), jnp.bfloat16),
        in_specs=[pl.BlockSpec(memory_space=space)] * len(operands),
        out_specs=VMEM,
        scratch_shapes=[
            pltpu.VMEM((q_rows * (lines + 8), LANES), jnp.float32),
            pltpu.VMEM((layers, q_rows * width // LANES, LANES), jnp.float32),
            pltpu.VMEM((layers, q_rows * width // LANES, LANES), jnp.float32),
            pltpu.VMEM((layers, 2 * width // LANES, LANES), jnp.float32),
        ]
        + scratch,
        compiler_params=pltpu.CompilerParams(vmem_limit_bytes=16 * MIB),
        cost_estimate=pl.CostEstimate(flops=10**9, bytes_accessed=4 * MIB, transcendentals=0),
        name="precond",
    )(*operands)


def fetched(n, body, *refs):
    operands, others = refs[:n], refs[n:]
    others, here, sems = others[: -n - 1], others[-n - 1 : -1], others[-1]
    copies = [pltpu.make_async_copy(a, b, sems.at[i]) for i, (a, b) in enumerate(zip(operands, here))]
    for copy in copies:
        copy.start()
    for copy in copies:
        copy.wait()
    body(*here, *others)


def split_kernel(layers, t_ref, flat_ref, here_ref, wide_ref, sems):
    rows, chunks = BLOCK, sems.shape[0]
    lines = t_ref.shape[1]
    pitch = wide_ref.shape[0] // rows
    chunk = t_ref.shape[0] // chunks
    copies = [
        pltpu.make_async_copy(
            t_ref.at[pl.ds(i * chunk, chunk)], here_ref.at[pl.ds(i * chunk, chunk)], sems.at[i]
        )
        for i in range(chunks)
    ]
    for copy in copies:
        copy.start()
    for i in range(chunks):
        copies[i].wait()

        @pl.loop(i * chunk // rows, (i + 1) * chunk // rows)
        def _(block):
            at = pl.multiple_of(block * rows, rows)
            for row in range(rows):
                wide_ref[row * pitch : row * pitch + lines, :] = here_ref[at + row].astype(jnp.float32)
            for line in range(lines):
                column = ((line % layers) * (lines // layers) + line // layers) * LANES
                out = wide_ref[pl.ds(line, rows, stride=pitch), :].astype(jnp.bfloat16)
                flat_ref[pl.ds(at, rows), column : column + LANES] = out


def split_layers(train_grads):
    tr_rows, layers, width = train_grads.shape
    lines = layers * width // LANES
    return pl.pallas_call(
        functools.partial(split_kernel, layers),
        out_shape=jax.ShapeDtypeStruct((tr_rows, layers * width), jnp.bfloat16),
        in_specs=[pl.BlockSpec(memory_space=pltpu.HBM)],
        out_specs=VMEM,
        scratch_shapes=[
            pltpu.VMEM((tr_rows, lines, LANES), jnp.bfloat16),
            pltpu.VMEM((BLOCK * (lines + 8), LANES), jnp.float32),
            pltpu.SemaphoreType.DMA((8,)),
        ],
        compiler_params=pltpu.CompilerParams(vmem_limit_bytes=20 * MIB),
        cost_estimate=pl.CostEstimate(flops=10**9, bytes_accessed=16 * MIB, transcendentals=0),
        name="split",
    )(in_hbm(by_lines(train_grads)))


def score_kernel(masks, added, t_ref, *refs):
    blocks, out_ref = refs[added:-1], refs[-1]
    q_rows, width = sum(ref.shape[0] for ref in blocks) // len(masks), t_ref.shape[1]
    n_query = out_ref.shape[1]
    depth = min(width, 1024)
    total = None
    for at in range(0, width, depth):
        block = jnp.concatenate([ref[:, at : at + depth] for ref in blocks], axis=0)
        sides = t_ref[:, at : at + depth], block
        term = mxu(*(sides[::-1] if added else sides), NT)
        total = term if total is None else total + term

    me, g = lax.axis_index("train"), lax.axis_index("group")
    row = lax.broadcasted_iota(jnp.int32, (q_rows, n_query), 0)
    query = lax.broadcasted_iota(jnp.int32, (q_rows, n_query), 1)
    order = []
    for mask in masks:
        c0, c1 = (jnp.where(g == 0, mask[0][c], mask[1][c]) for c in range(CORES))
        source = me ^ jnp.where(me % CORES == 0, c0, c1)
        order.append(jnp.where(query == source * q_rows + row, 1.0, 0.0))
    order = jnp.concatenate(order, axis=0).astype(jnp.bfloat16)
    high, low = halves(total)
    lowest = (total - high.astype(jnp.float32) - low.astype(jnp.float32)).astype(jnp.bfloat16)
    placed = sum(mxu(part, order, TN if added else NN) for part in (high, low, lowest))
    out_ref[...] = refs[0][...] + placed if added else placed


def scores(flat_train, parts, n_query, earlier=None):
    tr_rows, width = flat_train.shape
    masks = [came_masks(came) for a in parts for came in a.came]
    operands = [flat_train] + ([] if earlier is None else [earlier]) + [a.array for a in parts]
    rows = sum(a.array.shape[0] for a in parts)
    return pl.pallas_call(
        functools.partial(score_kernel, masks, 0 if earlier is None else 1),
        out_shape=jax.ShapeDtypeStruct((tr_rows, n_query), jnp.float32),
        in_specs=[VMEM] * len(operands),
        out_specs=VMEM,
        compiler_params=pltpu.CompilerParams(vmem_limit_bytes=32 * MIB),
        cost_estimate=pl.CostEstimate(
            flops=2 * tr_rows * n_query * width, bytes_accessed=2 * width * (tr_rows + rows), transcendentals=0
        ),
        name="scores",
    )(*operands)


def came_masks(came):
    xors = came ^ np.arange(came.shape[1])[None]
    masks = [[int(xors[g, c]) for c in range(CORES)] for g in range(GROUPS)]
    assert all((xors[g, c::CORES] == masks[g][c]).all() for g in range(GROUPS) for c in range(CORES))
    return masks


def per_device(n_train, train_grads, query_grads, basis_in, basis_out, eigvals):
    zs = n_train // (XS * CORES)
    rest = basis_in, basis_out, eigvals
    queries = by_lines(query_grads)
    places = [np.tile(np.arange(n_train), (GROUPS, 1))]
    far = [Blocks(queries, places).hop(far_z(pair)) for pair in range(1, zs // 2)]
    own = Blocks(precondition(queries, *rest), places)
    q_rows, width = own.array.shape
    n_query = n_train * q_rows
    at_x = own.hop(over_x)
    twin = own.hop(over_core)
    train_grads, own = after(train_grads, own)
    flat_train = split_layers(train_grads)
    flat_train, own = after(flat_train, own)
    at_z = own.hop(over_z)
    early, parts = [own, twin, at_x, at_z], []
    for pair, one in enumerate(far):
        flat_train, one = after(flat_train, one)
        one = Blocks(precondition(one.array, *rest, here=True), one.came)
        by_x, by_group = one.hop(over_x), one.hop(over_group)
        if pair == 0:
            one.array, at_x = after(one.array, at_x)
            at_xz = at_x.hop(over_z)
            early += [at_xz, one, stack(at_x, one).hop(over_core), by_x, by_group]
        else:
            parts += [one, one.hop(over_core), by_x, by_group]
        parts.append(stack(by_x, by_group).hop(over_core))
        half = by_x.columns(0, width // 2).hop(over_group)
        other_half = by_group.columns(width // 2, width).hop(over_x)
        if pair == 0:
            first_scores = scores(flat_train, early, n_query)
            first_scores, half = after(first_scores, half)
            half.array, near, near_x = after(half.array, at_z, at_xz)
            parts.append(stack(near, near_x).hop(over_core))
        corner = beside(half, other_half)
        parts += [corner, corner.hop(over_core)]
    partial_scores = scores(flat_train, parts, n_query, first_scores)
    return lax.psum_scatter(partial_scores, "layer", scatter_dimension=1, tiled=True)


def solution(mesh):
    return jax.shard_map(
        functools.partial(per_device, mesh.shape["train"]),
        mesh=mesh,
        in_specs=(
            P(("group", "train"), "layer", None),
            P("train", "layer", None),
            P("layer", None, None),
            P("layer", None, None),
            P("layer", None),
        ),
        out_specs=P(("group", "train"), "layer"),
        check_vma=False,
    )
```

```python
import functools

import jax
import jax.numpy as jnp
import numpy as np
from jax import lax
from jax.experimental import pallas as pl
from jax.experimental.pallas import tpu as pltpu
from jax.sharding import PartitionSpec as P

CORES = 2
XS = 2
GROUPS = 2
LANES = 128
BLOCK = 16
MIB = 1024 * 1024
VMEM = pl.BlockSpec(memory_space=pltpu.VMEM)
NN = (((1,), (0,)), ((), ()))
NT = (((1,), (1,)), ((), ()))
TN = (((0,), (0,)), ((), ()))


def mxu(a, b, dims=NN):
    return lax.dot_general(a, b, dims, preferred_element_type=jnp.float32)


def halves(a):
    high = a.astype(jnp.bfloat16)
    return high, (a - high.astype(jnp.float32)).astype(jnp.bfloat16)


def in_hbm(array):
    return pltpu.with_memory_space_constraint(array, pltpu.HBM)


class Blocks:
    def __init__(self, array, came):
        self.array, self.came = array, came

    def hop(self, turn):
        groups, n_train = self.came[0].shape
        perm, came = [], [np.zeros_like(a) for a in self.came]
        for g in range(groups):
            for t in range(n_train):
                z, x, c = t // (XS * CORES), t // CORES % XS, t % CORES
                to_g, z, x, c = turn(g, z, x, c)
                to_t = (z * XS + x) * CORES + c
                perm.append((g * n_train + t, to_g * n_train + to_t))
                for here, there in zip(self.came, came):
                    there[to_g, to_t] = here[g, t]
        return Blocks(lax.ppermute(self.array, ("group", "train"), perm), came)

    def columns(self, start, stop):
        return Blocks(self.array[:, start:stop], self.came)


def stack(*parts):
    return Blocks(jnp.concatenate([a.array for a in parts], axis=0), sum((a.came for a in parts), []))


def beside(left, right):
    assert all((a == b).all() for a, b in zip(left.came, right.came))
    return Blocks(jnp.concatenate([left.array, right.array], axis=1), left.came)


def after(kernel_result, *parts):
    arrays, kernel_result = lax.optimization_barrier(([a.array for a in parts], kernel_result))
    return kernel_result, *(Blocks(array, a.came) for array, a in zip(arrays, parts))


def over_core(g, z, x, c):
    return g, z, x, c ^ 1


def over_x(g, z, x, c):
    return g, z, x ^ 1, c


def over_z(g, z, x, c):
    return g, z ^ 1, x, c


def far_z(pair):
    return lambda g, z, x, c: (g, z ^ (2 * pair + (g == c)), x, c)


def over_group(g, z, x, c):
    return g ^ 1, z, x, c


def precond_kernel(q_ref, in_ref, out_ref, eig_ref, block_ref, lines_ref, *scratch):
    q_rows, lines, _ = q_ref.shape
    pitch = lines_ref.shape[0] // q_rows
    for q in range(q_rows):
        lines_ref[q * pitch : q * pitch + lines, :] = q_ref[q].astype(jnp.float32)
    for layer in range(in_ref.shape[0]):
        precond_layer(layer, lines_ref, in_ref, out_ref, eig_ref, block_ref, *(ref.at[layer] for ref in scratch))


def precond_layer(layer, lines_ref, in_ref, out_ref, eig_ref, block_ref, wide_ref, tall_ref, even_ref):
    q_rows = block_ref.shape[0]
    layers, width = eig_ref.shape
    rows = width // LANES
    pitch = lines_ref.shape[0] // q_rows
    p_in, p_out = in_ref.shape[1:]
    left = lax.broadcasted_iota(jnp.int32, (1, LANES), 1) < p_out

    eig = eig_ref[layer : layer + 1, :]
    damping = 0.1 / width * jnp.sum(eig, axis=1, keepdims=True)
    for j in range(rows):
        pair = eig[:, j * LANES : (j + 1) * LANES]
        turned = pltpu.roll(pair, p_out, 1)
        even_ref[2 * j : 2 * j + 1, :] = jnp.where(left, pair, turned)
        even_ref[2 * j + 1 : 2 * j + 2, :] = jnp.where(left, turned, pair)
    scale = 1.0 / (even_ref[...] + damping)

    by_row = [in_ref[layer, pl.ds(p, rows, stride=2), :] for p in range(2)]
    back_left = jnp.concatenate(by_row, axis=0)
    fore_left = jnp.concatenate(by_row, axis=1)
    back_high, back_low = halves(back_left)
    fore_high, fore_low = halves(fore_left)
    fore = jnp.concatenate([fore_high, fore_high, fore_low], axis=0)
    back = jnp.concatenate([back_high, back_high, back_low], axis=1)

    basis = out_ref[layer]
    empty = jnp.zeros((p_out, p_out), jnp.bfloat16)

    def twice(a):
        return jnp.concatenate(
            [jnp.concatenate([a, empty], axis=1), jnp.concatenate([empty, a], axis=1)], axis=0
        )

    right_high, right_low = halves(basis)
    turned_high, turned_low = halves(basis.T)
    fore_right = jnp.concatenate([twice(right_high), twice(right_low)], axis=1)
    back_high, back_low = twice(turned_high), twice(turned_low)
    back_right = jnp.concatenate(
        [
            jnp.concatenate([back_high, back_low], axis=1),
            jnp.concatenate([back_high, jnp.zeros_like(back_low)], axis=1),
        ],
        axis=0,
    )

    stacked = jnp.concatenate(
        [lines_ref[pl.ds(layers * j + layer, q_rows, stride=pitch), :] for j in range(rows)], axis=0
    ).astype(jnp.bfloat16)
    both = mxu(stacked, fore_right)
    wide_ref[...] = both[:, :LANES] + both[:, LANES:]
    by_query = jnp.concatenate([wide_ref[pl.ds(q, rows, stride=q_rows), :] for q in range(q_rows)], axis=1)
    high, low = halves(by_query)
    both = mxu(fore, jnp.concatenate([high, low, high], axis=0), TN)
    every = jnp.concatenate([left] * q_rows, axis=1)
    rotated = jnp.where(every, both[:p_in], both[p_in:])
    rotated = jnp.concatenate(
        [
            part + pltpu.roll(part, p_out, 1)
            for part in (rotated[:, q * LANES : (q + 1) * LANES] for q in range(q_rows))
        ],
        axis=1,
    )
    scaled = rotated * jnp.concatenate([scale] * q_rows, axis=1)
    high, low = halves(scaled)
    both = mxu(back, jnp.concatenate([high, low, high], axis=0))
    mixed = jnp.where(every, both[:rows], both[rows:])
    stacked = jnp.concatenate([mixed[:, q * LANES : (q + 1) * LANES] for q in range(q_rows)], axis=0)
    both = mxu(jnp.concatenate(halves(stacked), axis=1), back_right)
    tall_ref[...] = both[:, :LANES] + both[:, LANES:]
    for j in range(rows):
        block = tall_ref[pl.ds(j, q_rows, stride=rows), :]
        column = layer * width + j * LANES
        block_ref[:, column : column + LANES] = block.astype(jnp.bfloat16)


def by_lines(array):
    rows, layers, width = array.shape
    array = array.reshape(rows, layers, width // LANES, LANES)
    return array.transpose(0, 2, 1, 3).reshape(rows, -1, LANES)


def precondition(queries, basis_in, basis_out, eigvals, here=False):
    q_rows, lines, _ = queries.shape
    layers, width = eigvals.shape
    operands, body, scratch = [queries, basis_in, basis_out, eigvals], precond_kernel, []
    if not here:
        operands = [in_hbm(a) for a in operands]
        body = functools.partial(fetched, len(operands), body)
        scratch = [pltpu.VMEM(a.shape, a.dtype) for a in operands] + [pltpu.SemaphoreType.DMA((len(operands),))]
    space = pltpu.VMEM if here else pltpu.HBM
    return pl.pallas_call(
        body,
        out_shape=jax.ShapeDtypeStruct((q_rows, layers * width), jnp.bfloat16),
        in_specs=[pl.BlockSpec(memory_space=space)] * len(operands),
        out_specs=VMEM,
        scratch_shapes=[
            pltpu.VMEM((q_rows * (lines + 8), LANES), jnp.float32),
            pltpu.VMEM((layers, q_rows * width // LANES, LANES), jnp.float32),
            pltpu.VMEM((layers, q_rows * width // LANES, LANES), jnp.float32),
            pltpu.VMEM((layers, 2 * width // LANES, LANES), jnp.float32),
        ]
        + scratch,
        compiler_params=pltpu.CompilerParams(vmem_limit_bytes=16 * MIB),
        cost_estimate=pl.CostEstimate(flops=10**9, bytes_accessed=4 * MIB, transcendentals=0),
        name="precond",
    )(*operands)


def fetched(n, body, *refs):
    operands, others = refs[:n], refs[n:]
    others, here, sems = others[: -n - 1], others[-n - 1 : -1], others[-1]
    copies = [pltpu.make_async_copy(a, b, sems.at[i]) for i, (a, b) in enumerate(zip(operands, here))]
    for copy in copies:
        copy.start()
    for copy in copies:
        copy.wait()
    body(*here, *others)


def split_kernel(layers, t_ref, slabs_ref, here_ref, wide_ref, sems):
    rows, chunks = BLOCK, sems.shape[0]
    lines = t_ref.shape[1]
    pitch = wide_ref.shape[0] // rows
    chunk = t_ref.shape[0] // chunks
    copies = [
        pltpu.make_async_copy(
            t_ref.at[pl.ds(i * chunk, chunk)], here_ref.at[pl.ds(i * chunk, chunk)], sems.at[i]
        )
        for i in range(chunks)
    ]
    for copy in copies:
        copy.start()
    for i in range(chunks):
        copies[i].wait()

        @pl.loop(i * chunk // rows, (i + 1) * chunk // rows)
        def _(block):
            at = pl.multiple_of(block * rows, rows)
            for row in range(rows):
                wide_ref[row * pitch : row * pitch + lines, :] = here_ref[at + row].astype(jnp.float32)
            for line in range(lines):
                slab = (line % layers) * (lines // layers) + line // layers
                slabs_ref[slab, pl.ds(at, rows), :] = wide_ref[pl.ds(line, rows, stride=pitch), :].astype(jnp.bfloat16)


def split_layers(train_grads):
    tr_rows, layers, width = train_grads.shape
    lines = layers * width // LANES
    return pl.pallas_call(
        functools.partial(split_kernel, layers),
        out_shape=jax.ShapeDtypeStruct((lines, tr_rows, LANES), jnp.bfloat16),
        in_specs=[pl.BlockSpec(memory_space=pltpu.HBM)],
        out_specs=VMEM,
        scratch_shapes=[
            pltpu.VMEM((tr_rows, lines, LANES), jnp.bfloat16),
            pltpu.VMEM((BLOCK * (lines + 8), LANES), jnp.float32),
            pltpu.SemaphoreType.DMA((8,)),
        ],
        compiler_params=pltpu.CompilerParams(vmem_limit_bytes=20 * MIB),
        cost_estimate=pl.CostEstimate(flops=10**9, bytes_accessed=16 * MIB, transcendentals=0),
        name="split",
    )(in_hbm(by_lines(train_grads)))


def score_kernel(masks, slabs_ref, *refs):
    blocks, out_ref = refs[:-1], refs[-1]
    slabs = slabs_ref.shape[0]
    q_rows = out_ref.shape[1] // len(masks)
    n_query = out_ref.shape[1]
    step = min(slabs, 8)
    total = None
    for at in range(0, slabs, step):
        train = jnp.concatenate([slabs_ref[at + i] for i in range(step)], axis=1)
        columns = slice(at * LANES, (at + step) * LANES)
        block = jnp.concatenate([ref[:, columns] for ref in blocks], axis=0)
        term = mxu(train, block, NT)
        total = term if total is None else total + term

    me, g = lax.axis_index("train"), lax.axis_index("group")
    row = lax.broadcasted_iota(jnp.int32, (q_rows, n_query), 0)
    query = lax.broadcasted_iota(jnp.int32, (q_rows, n_query), 1)
    order = []
    for mask in masks:
        c0, c1 = (jnp.where(g == 0, mask[0][c], mask[1][c]) for c in range(CORES))
        source = me ^ jnp.where(me % CORES == 0, c0, c1)
        order.append(jnp.where(query == source * q_rows + row, 1.0, 0.0))
    order = jnp.concatenate(order, axis=0).astype(jnp.bfloat16)
    high, low = halves(total)
    lowest = (total - high.astype(jnp.float32) - low.astype(jnp.float32)).astype(jnp.bfloat16)
    out_ref[...] = mxu(high, order) + mxu(low, order) + mxu(lowest, order)


def came_masks(came):
    xors = came ^ np.arange(came.shape[1])[None]
    masks = [[int(xors[g, c]) for c in range(CORES)] for g in range(GROUPS)]
    assert all((xors[g, c::CORES] == masks[g][c]).all() for g in range(GROUPS) for c in range(CORES))
    return masks


def per_device(n_train, train_grads, query_grads, basis_in, basis_out, eigvals):
    zs = n_train // (XS * CORES)
    rest = basis_in, basis_out, eigvals
    queries = by_lines(query_grads)
    places = [np.tile(np.arange(n_train), (GROUPS, 1))]
    far = [Blocks(queries, places).hop(far_z(pair)) for pair in range(1, zs // 2)]
    own = Blocks(precondition(queries, *rest), places)
    q_rows, width = own.array.shape
    n_query = n_train * q_rows
    at_x = own.hop(over_x)
    twin = own.hop(over_core)
    train_grads, own = after(train_grads, own)
    slabs = split_layers(train_grads)
    slabs, own = after(slabs, own)
    at_z = own.hop(over_z)
    parts = [own, twin, at_x, at_z]
    for pair, one in enumerate(far):
        slabs, one = after(slabs, one)
        one = Blocks(precondition(one.array, *rest, here=True), one.came)
        by_x, by_group = one.hop(over_x), one.hop(over_group)
        parts.append(one)
        if pair == 0:
            one.array, at_x = after(one.array, at_x)
            at_xz = at_x.hop(over_z)
            stacked = stack(at_x, one)
            stacked.array, by_x = after(stacked.array, by_x)
            parts += [at_xz, stacked.hop(over_core)]
        else:
            parts.append(one.hop(over_core))
        parts += [by_x, by_group, stack(by_x, by_group).hop(over_core)]
        half = by_x.columns(0, width // 2).hop(over_group)
        if pair == 0:
            half.array, near, near_x = after(half.array, at_z, at_xz)
            parts.append(stack(near, near_x).hop(over_core))
        corner = beside(half, by_group.columns(width // 2, width).hop(over_x))
        parts += [corner, corner.hop(over_core)]

    tr_rows = train_grads.shape[0]
    operands = [slabs] + [a.array for a in parts]
    partial_scores = pl.pallas_call(
        functools.partial(score_kernel, [came_masks(came) for a in parts for came in a.came]),
        out_shape=jax.ShapeDtypeStruct((tr_rows, n_query), jnp.float32),
        in_specs=[VMEM] * len(operands),
        out_specs=VMEM,
        compiler_params=pltpu.CompilerParams(vmem_limit_bytes=32 * MIB),
        cost_estimate=pl.CostEstimate(
            flops=2 * tr_rows * n_query * width, bytes_accessed=2 * width * (tr_rows + n_query), transcendentals=0
        ),
        name="scores",
    )(*operands)
    return lax.psum_scatter(partial_scores, "layer", scatter_dimension=1, tiled=True)


def solution(mesh):
    return jax.shard_map(
        functools.partial(per_device, mesh.shape["train"]),
        mesh=mesh,
        in_specs=(
            P(("group", "train"), "layer", None),
            P("train", "layer", None),
            P("layer", None, None),
            P("layer", None, None),
            P("layer", None),
        ),
        out_specs=P(("group", "train"), "layer"),
        check_vma=False,
    )
```

```python
import functools

import jax
import jax.numpy as jnp
import numpy as np
from jax import lax
from jax.experimental import pallas as pl
from jax.experimental.pallas import tpu as pltpu
from jax.sharding import PartitionSpec as P

CORES = 2
XS = 2
GROUPS = 2
LANES = 128
BLOCK = 16
MIB = 1024 * 1024
VMEM = pl.BlockSpec(memory_space=pltpu.VMEM)
NN = (((1,), (0,)), ((), ()))
NT = (((1,), (1,)), ((), ()))
TN = (((0,), (0,)), ((), ()))


def mxu(a, b, dims=NN):
    return lax.dot_general(a, b, dims, preferred_element_type=jnp.float32)


def halves(a):
    high = a.astype(jnp.bfloat16)
    return high, (a - high.astype(jnp.float32)).astype(jnp.bfloat16)


def in_hbm(array):
    return pltpu.with_memory_space_constraint(array, pltpu.HBM)


class Blocks:
    def __init__(self, array, came):
        self.array, self.came = array, came

    def hop(self, turn):
        groups, n_train = self.came[0].shape
        perm, came = [], [np.zeros_like(a) for a in self.came]
        for g in range(groups):
            for t in range(n_train):
                z, x, c = t // (XS * CORES), t // CORES % XS, t % CORES
                to_g, z, x, c = turn(g, z, x, c)
                to_t = (z * XS + x) * CORES + c
                perm.append((g * n_train + t, to_g * n_train + to_t))
                for here, there in zip(self.came, came):
                    there[to_g, to_t] = here[g, t]
        return Blocks(lax.ppermute(self.array, ("group", "train"), perm), came)

    def columns(self, start, stop):
        return Blocks(self.array[:, start:stop], self.came)


def stack(*parts):
    return Blocks(jnp.concatenate([a.array for a in parts], axis=0), sum((a.came for a in parts), []))


def beside(left, right):
    assert all((a == b).all() for a, b in zip(left.came, right.came))
    return Blocks(jnp.concatenate([left.array, right.array], axis=1), left.came)


def after(kernel_result, *parts):
    arrays, kernel_result = lax.optimization_barrier(([a.array for a in parts], kernel_result))
    return kernel_result, *(Blocks(array, a.came) for array, a in zip(arrays, parts))


def over_core(g, z, x, c):
    return g, z, x, c ^ 1


def over_x(g, z, x, c):
    return g, z, x ^ 1, c


def over_z(g, z, x, c):
    return g, z ^ 1, x, c


def far_z(pair):
    return lambda g, z, x, c: (g, z ^ (2 * pair + (g == c)), x, c)


def over_group(g, z, x, c):
    return g ^ 1, z, x, c


def precond_kernel(q_ref, in_ref, out_ref, eig_ref, block_ref, lines_ref, *scratch):
    q_rows, lines, _ = q_ref.shape
    pitch = lines_ref.shape[0] // q_rows
    for q in range(q_rows):
        lines_ref[q * pitch : q * pitch + lines, :] = q_ref[q].astype(jnp.float32)
    for layer in range(in_ref.shape[0]):
        precond_layer(layer, lines_ref, in_ref, out_ref, eig_ref, block_ref, *(ref.at[layer] for ref in scratch))


def precond_layer(layer, lines_ref, in_ref, out_ref, eig_ref, block_ref, wide_ref, tall_ref, even_ref):
    q_rows = block_ref.shape[0]
    layers, width = eig_ref.shape
    rows = width // LANES
    pitch = lines_ref.shape[0] // q_rows
    p_in, p_out = in_ref.shape[1:]
    left = lax.broadcasted_iota(jnp.int32, (1, LANES), 1) < p_out

    eig = eig_ref[layer : layer + 1, :]
    damping = 0.1 / width * jnp.sum(eig, axis=1, keepdims=True)
    for j in range(rows):
        pair = eig[:, j * LANES : (j + 1) * LANES]
        turned = pltpu.roll(pair, p_out, 1)
        even_ref[2 * j : 2 * j + 1, :] = jnp.where(left, pair, turned)
        even_ref[2 * j + 1 : 2 * j + 2, :] = jnp.where(left, turned, pair)
    scale = 1.0 / (even_ref[...] + damping)

    by_row = [in_ref[layer, pl.ds(p, rows, stride=2), :] for p in range(2)]
    back_left = jnp.concatenate(by_row, axis=0)
    fore_left = jnp.concatenate(by_row, axis=1)
    back_high, back_low = halves(back_left)
    fore_high, fore_low = halves(fore_left)
    fore = jnp.concatenate([fore_high, fore_high, fore_low], axis=0)
    back = jnp.concatenate([back_high, back_high, back_low], axis=1)

    basis = out_ref[layer]
    empty = jnp.zeros((p_out, p_out), jnp.bfloat16)

    def twice(a):
        return jnp.concatenate(
            [jnp.concatenate([a, empty], axis=1), jnp.concatenate([empty, a], axis=1)], axis=0
        )

    right_high, right_low = halves(basis)
    turned_high, turned_low = halves(basis.T)
    fore_right = jnp.concatenate([twice(right_high), twice(right_low)], axis=1)
    back_high, back_low = twice(turned_high), twice(turned_low)
    back_right = jnp.concatenate(
        [
            jnp.concatenate([back_high, back_low], axis=1),
            jnp.concatenate([back_high, jnp.zeros_like(back_low)], axis=1),
        ],
        axis=0,
    )

    stacked = jnp.concatenate(
        [lines_ref[pl.ds(layers * j + layer, q_rows, stride=pitch), :] for j in range(rows)], axis=0
    ).astype(jnp.bfloat16)
    both = mxu(stacked, fore_right)
    wide_ref[...] = both[:, :LANES] + both[:, LANES:]
    by_query = jnp.concatenate([wide_ref[pl.ds(q, rows, stride=q_rows), :] for q in range(q_rows)], axis=1)
    high, low = halves(by_query)
    both = mxu(fore, jnp.concatenate([high, low, high], axis=0), TN)
    every = jnp.concatenate([left] * q_rows, axis=1)
    rotated = jnp.where(every, both[:p_in], both[p_in:])
    rotated = jnp.concatenate(
        [
            part + pltpu.roll(part, p_out, 1)
            for part in (rotated[:, q * LANES : (q + 1) * LANES] for q in range(q_rows))
        ],
        axis=1,
    )
    scaled = rotated * jnp.concatenate([scale] * q_rows, axis=1)
    high, low = halves(scaled)
    both = mxu(back, jnp.concatenate([high, low, high], axis=0))
    mixed = jnp.where(every, both[:rows], both[rows:])
    stacked = jnp.concatenate([mixed[:, q * LANES : (q + 1) * LANES] for q in range(q_rows)], axis=0)
    both = mxu(jnp.concatenate(halves(stacked), axis=1), back_right)
    tall_ref[...] = both[:, :LANES] + both[:, LANES:]
    for j in range(rows):
        block = tall_ref[pl.ds(j, q_rows, stride=rows), :]
        column = layer * width + j * LANES
        block_ref[:, column : column + LANES] = block.astype(jnp.bfloat16)


def by_lines(array):
    rows, layers, width = array.shape
    array = array.reshape(rows, layers, width // LANES, LANES)
    return array.transpose(0, 2, 1, 3).reshape(rows, -1, LANES)


def precondition(queries, basis_in, basis_out, eigvals, here=False):
    q_rows, lines, _ = queries.shape
    layers, width = eigvals.shape
    operands, body, scratch = [queries, basis_in, basis_out, eigvals], precond_kernel, []
    if not here:
        operands = [in_hbm(a) for a in operands]
        body = functools.partial(fetched, len(operands), body)
        scratch = [pltpu.VMEM(a.shape, a.dtype) for a in operands] + [pltpu.SemaphoreType.DMA((len(operands),))]
    space = pltpu.VMEM if here else pltpu.HBM
    return pl.pallas_call(
        body,
        out_shape=jax.ShapeDtypeStruct((q_rows, layers * width), jnp.bfloat16),
        in_specs=[pl.BlockSpec(memory_space=space)] * len(operands),
        out_specs=VMEM,
        scratch_shapes=[
            pltpu.VMEM((q_rows * (lines + 8), LANES), jnp.float32),
            pltpu.VMEM((layers, q_rows * width // LANES, LANES), jnp.float32),
            pltpu.VMEM((layers, q_rows * width // LANES, LANES), jnp.float32),
            pltpu.VMEM((layers, 2 * width // LANES, LANES), jnp.float32),
        ]
        + scratch,
        compiler_params=pltpu.CompilerParams(vmem_limit_bytes=16 * MIB),
        cost_estimate=pl.CostEstimate(flops=10**9, bytes_accessed=4 * MIB, transcendentals=0),
        name="precond",
    )(*operands)


def fetched(n, body, *refs):
    operands, others = refs[:n], refs[n:]
    others, here, sems = others[: -n - 1], others[-n - 1 : -1], others[-1]
    copies = [pltpu.make_async_copy(a, b, sems.at[i]) for i, (a, b) in enumerate(zip(operands, here))]
    for copy in copies:
        copy.start()
    for copy in copies:
        copy.wait()
    body(*here, *others)


def split_kernel(layers, t_ref, slabs_ref, here_ref, wide_ref, sems):
    rows, chunks = BLOCK, sems.shape[0]
    lines = t_ref.shape[1]
    pitch = wide_ref.shape[0] // rows
    chunk = t_ref.shape[0] // chunks
    copies = [
        pltpu.make_async_copy(
            t_ref.at[pl.ds(i * chunk, chunk)], here_ref.at[pl.ds(i * chunk, chunk)], sems.at[i]
        )
        for i in range(chunks)
    ]
    for copy in copies:
        copy.start()
    for i in range(chunks):
        copies[i].wait()

        @pl.loop(i * chunk // rows, (i + 1) * chunk // rows)
        def _(block):
            at = pl.multiple_of(block * rows, rows)
            for row in range(rows):
                wide_ref[row * pitch : row * pitch + lines, :] = here_ref[at + row].astype(jnp.float32)
            for line in range(lines):
                slab = (line % layers) * (lines // layers) + line // layers
                slabs_ref[slab, pl.ds(at, rows), :] = wide_ref[pl.ds(line, rows, stride=pitch), :].astype(jnp.bfloat16)


def split_layers(train_grads):
    tr_rows, layers, width = train_grads.shape
    lines = layers * width // LANES
    return pl.pallas_call(
        functools.partial(split_kernel, layers),
        out_shape=jax.ShapeDtypeStruct((lines, tr_rows, LANES), jnp.bfloat16),
        in_specs=[pl.BlockSpec(memory_space=pltpu.HBM)],
        out_specs=VMEM,
        scratch_shapes=[
            pltpu.VMEM((tr_rows, lines, LANES), jnp.bfloat16),
            pltpu.VMEM((BLOCK * (lines + 8), LANES), jnp.float32),
            pltpu.SemaphoreType.DMA((8,)),
        ],
        compiler_params=pltpu.CompilerParams(vmem_limit_bytes=20 * MIB),
        cost_estimate=pl.CostEstimate(flops=10**9, bytes_accessed=16 * MIB, transcendentals=0),
        name="split",
    )(in_hbm(by_lines(train_grads)))


def order_rows(masks, q_rows, n_query):
    me, g = lax.axis_index("train"), lax.axis_index("group")
    row = lax.broadcasted_iota(jnp.int32, (q_rows, n_query), 0)
    query = lax.broadcasted_iota(jnp.int32, (q_rows, n_query), 1)
    order = []
    for mask in masks:
        c0, c1 = (jnp.where(g == 0, mask[0][c], mask[1][c]) for c in range(CORES))
        source = me ^ jnp.where(me % CORES == 0, c0, c1)
        order.append(jnp.where(query == source * q_rows + row, 1.0, 0.0))
    return jnp.concatenate(order, axis=0).astype(jnp.bfloat16)


def order_kernel(masks, q_rows, *refs):
    order_ref = refs[-1]
    order_ref[...] = order_rows(masks, q_rows, order_ref.shape[1])


def first_order(parts, stands_after, q_rows, n_query):
    masks = [came_masks(came) for a in parts for came in a.came]
    return pl.pallas_call(
        functools.partial(order_kernel, masks, q_rows),
        out_shape=jax.ShapeDtypeStruct((len(masks) * q_rows, n_query), jnp.bfloat16),
        in_specs=[pl.BlockSpec(memory_space=pl.ANY)] * len(stands_after),
        out_specs=VMEM,
        compiler_params=pltpu.CompilerParams(vmem_limit_bytes=16 * MIB),
        cost_estimate=pl.CostEstimate(flops=4 * 10**9, bytes_accessed=16 * MIB, transcendentals=0),
        name="order",
    )(*(a.array for a in stands_after))


def score_kernel(q_rows, masks, slabs_ref, first_ref, *refs):
    blocks, out_ref = refs[:-1], refs[-1]
    slabs = slabs_ref.shape[0]
    n_query = out_ref.shape[1]
    step = min(slabs, 8)
    total = None
    for at in range(0, slabs, step):
        train = jnp.concatenate([slabs_ref[at + i] for i in range(step)], axis=1)
        columns = slice(at * LANES, (at + step) * LANES)
        block = jnp.concatenate([ref[:, columns] for ref in blocks], axis=0)
        term = mxu(train, block, NT)
        total = term if total is None else total + term

    order = jnp.concatenate([first_ref[...], order_rows(masks, q_rows, n_query)], axis=0)
    high, low = halves(total)
    lowest = (total - high.astype(jnp.float32) - low.astype(jnp.float32)).astype(jnp.bfloat16)
    out_ref[...] = mxu(high, order) + mxu(low, order) + mxu(lowest, order)


def came_masks(came):
    xors = came ^ np.arange(came.shape[1])[None]
    masks = [[int(xors[g, c]) for c in range(CORES)] for g in range(GROUPS)]
    assert all((xors[g, c::CORES] == masks[g][c]).all() for g in range(GROUPS) for c in range(CORES))
    return masks


def per_device(n_train, train_grads, query_grads, basis_in, basis_out, eigvals):
    zs = n_train // (XS * CORES)
    rest = basis_in, basis_out, eigvals
    queries = by_lines(query_grads)
    places = [np.tile(np.arange(n_train), (GROUPS, 1))]
    far = [Blocks(queries, places).hop(far_z(pair)) for pair in range(1, zs // 2)]
    own = Blocks(precondition(queries, *rest), places)
    q_rows, width = own.array.shape
    n_query = n_train * q_rows
    at_x = own.hop(over_x)
    twin = own.hop(over_core)
    train_grads, own = after(train_grads, own)
    slabs = split_layers(train_grads)
    slabs, own = after(slabs, own)
    at_z = own.hop(over_z)
    parts = [own, twin, at_x, at_z]
    for pair, one in enumerate(far):
        slabs, one = after(slabs, one)
        one = Blocks(precondition(one.array, *rest, here=True), one.came)
        by_x, by_group = one.hop(over_x), one.hop(over_group)
        parts.append(one)
        if pair == 0:
            one.array, at_x = after(one.array, at_x)
            at_xz = at_x.hop(over_z)
            stacked = stack(at_x, one)
            parts += [at_xz, stacked.hop(over_core)]
            n_first = sum(len(a.came) for a in parts)
            order = first_order(parts, [twin, at_x], q_rows, n_query)
            order, by_x = after(order, by_x)
        else:
            parts.append(one.hop(over_core))
        parts += [by_x, by_group, stack(by_x, by_group).hop(over_core)]
        half = by_x.columns(0, width // 2).hop(over_group)
        if pair == 0:
            half.array, near, near_x = after(half.array, at_z, at_xz)
            parts.append(stack(near, near_x).hop(over_core))
        corner = beside(half, by_group.columns(width // 2, width).hop(over_x))
        parts += [corner, corner.hop(over_core)]

    tr_rows = train_grads.shape[0]
    operands = [slabs, order] + [a.array for a in parts]
    masks = [came_masks(came) for a in parts for came in a.came]
    partial_scores = pl.pallas_call(
        functools.partial(score_kernel, q_rows, masks[n_first:]),
        out_shape=jax.ShapeDtypeStruct((tr_rows, n_query), jnp.float32),
        in_specs=[VMEM] * len(operands),
        out_specs=VMEM,
        compiler_params=pltpu.CompilerParams(vmem_limit_bytes=32 * MIB),
        cost_estimate=pl.CostEstimate(
            flops=2 * tr_rows * n_query * width, bytes_accessed=2 * width * (tr_rows + n_query), transcendentals=0
        ),
        name="scores",
    )(*operands)
    return lax.psum_scatter(partial_scores, "layer", scatter_dimension=1, tiled=True)


def solution(mesh):
    return jax.shard_map(
        functools.partial(per_device, mesh.shape["train"]),
        mesh=mesh,
        in_specs=(
            P(("group", "train"), "layer", None),
            P("train", "layer", None),
            P("layer", None, None),
            P("layer", None, None),
            P("layer", None),
        ),
        out_specs=P(("group", "train"), "layer"),
        check_vma=False,
    )
```

```python
import functools

import jax
import jax.numpy as jnp
import numpy as np
from jax import lax
from jax.experimental import pallas as pl
from jax.experimental.pallas import tpu as pltpu
from jax.sharding import PartitionSpec as P

CORES = 2
XS = 2
GROUPS = 2
LANES = 128
BLOCK = 16
MIB = 1024 * 1024
VMEM = pl.BlockSpec(memory_space=pltpu.VMEM)
NN = (((1,), (0,)), ((), ()))
NT = (((1,), (1,)), ((), ()))
TN = (((0,), (0,)), ((), ()))


def mxu(a, b, dims=NN):
    return lax.dot_general(a, b, dims, preferred_element_type=jnp.float32)


def halves(a):
    high = a.astype(jnp.bfloat16)
    return high, (a - high.astype(jnp.float32)).astype(jnp.bfloat16)


def in_hbm(array):
    return pltpu.with_memory_space_constraint(array, pltpu.HBM)


class Blocks:
    def __init__(self, array, came):
        self.array, self.came = array, came

    def hop(self, turn):
        groups, n_train = self.came[0].shape
        perm, came = [], [np.zeros_like(a) for a in self.came]
        for g in range(groups):
            for t in range(n_train):
                z, x, c = t // (XS * CORES), t // CORES % XS, t % CORES
                to_g, z, x, c = turn(g, z, x, c)
                to_t = (z * XS + x) * CORES + c
                perm.append((g * n_train + t, to_g * n_train + to_t))
                for here, there in zip(self.came, came):
                    there[to_g, to_t] = here[g, t]
        return Blocks(lax.ppermute(self.array, ("group", "train"), perm), came)

    def columns(self, start, stop):
        return Blocks(self.array[:, start:stop], self.came)


def stack(*parts):
    return Blocks(jnp.concatenate([a.array for a in parts], axis=0), sum((a.came for a in parts), []))


def beside(left, right):
    assert all((a == b).all() for a, b in zip(left.came, right.came))
    return Blocks(jnp.concatenate([left.array, right.array], axis=1), left.came)


def after(kernel_result, *parts):
    arrays, kernel_result = lax.optimization_barrier(([a.array for a in parts], kernel_result))
    return kernel_result, *(Blocks(array, a.came) for array, a in zip(arrays, parts))


def over_core(g, z, x, c):
    return g, z, x, c ^ 1


def over_x(g, z, x, c):
    return g, z, x ^ 1, c


def over_z(g, z, x, c):
    return g, z ^ 1, x, c


def far_z(pair):
    return lambda g, z, x, c: (g, z ^ (2 * pair + (g == c)), x, c)


def over_group(g, z, x, c):
    return g ^ 1, z, x, c


def precond_kernel(q_ref, in_ref, out_ref, eig_ref, block_ref, lines_ref, *scratch):
    q_rows, lines, _ = q_ref.shape
    pitch = lines_ref.shape[0] // q_rows
    for q in range(q_rows):
        lines_ref[q * pitch : q * pitch + lines, :] = q_ref[q].astype(jnp.float32)
    for layer in range(in_ref.shape[0]):
        precond_layer(layer, lines_ref, in_ref, out_ref, eig_ref, block_ref, *(ref.at[layer] for ref in scratch))


def precond_layer(layer, lines_ref, in_ref, out_ref, eig_ref, block_ref, wide_ref, tall_ref, even_ref):
    q_rows = block_ref.shape[0]
    layers, width = eig_ref.shape
    rows = width // LANES
    pitch = lines_ref.shape[0] // q_rows
    p_in, p_out = in_ref.shape[1:]
    left = lax.broadcasted_iota(jnp.int32, (1, LANES), 1) < p_out

    eig = eig_ref[layer : layer + 1, :]
    damping = 0.1 / width * jnp.sum(eig, axis=1, keepdims=True)
    for j in range(rows):
        pair = eig[:, j * LANES : (j + 1) * LANES]
        turned = pltpu.roll(pair, p_out, 1)
        even_ref[2 * j : 2 * j + 1, :] = jnp.where(left, pair, turned)
        even_ref[2 * j + 1 : 2 * j + 2, :] = jnp.where(left, turned, pair)
    scale = 1.0 / (even_ref[...] + damping)

    by_row = [in_ref[layer, pl.ds(p, rows, stride=2), :] for p in range(2)]
    back_left = jnp.concatenate(by_row, axis=0)
    fore_left = jnp.concatenate(by_row, axis=1)
    back_high, back_low = halves(back_left)
    fore_high, fore_low = halves(fore_left)
    fore = jnp.concatenate([fore_high, fore_high, fore_low], axis=0)
    back = jnp.concatenate([back_high, back_high, back_low], axis=1)

    basis = out_ref[layer]
    empty = jnp.zeros((p_out, p_out), jnp.bfloat16)

    def twice(a):
        return jnp.concatenate(
            [jnp.concatenate([a, empty], axis=1), jnp.concatenate([empty, a], axis=1)], axis=0
        )

    right_high, right_low = halves(basis)
    turned_high, turned_low = halves(basis.T)
    fore_right = jnp.concatenate([twice(right_high), twice(right_low)], axis=1)
    back_high, back_low = twice(turned_high), twice(turned_low)
    back_right = jnp.concatenate(
        [
            jnp.concatenate([back_high, back_low], axis=1),
            jnp.concatenate([back_high, jnp.zeros_like(back_low)], axis=1),
        ],
        axis=0,
    )

    stacked = jnp.concatenate(
        [lines_ref[pl.ds(layers * j + layer, q_rows, stride=pitch), :] for j in range(rows)], axis=0
    ).astype(jnp.bfloat16)
    both = mxu(stacked, fore_right)
    wide_ref[...] = both[:, :LANES] + both[:, LANES:]
    by_query = jnp.concatenate([wide_ref[pl.ds(q, rows, stride=q_rows), :] for q in range(q_rows)], axis=1)
    high, low = halves(by_query)
    both = mxu(fore, jnp.concatenate([high, low, high], axis=0), TN)
    every = jnp.concatenate([left] * q_rows, axis=1)
    rotated = jnp.where(every, both[:p_in], both[p_in:])
    rotated = jnp.concatenate(
        [
            part + pltpu.roll(part, p_out, 1)
            for part in (rotated[:, q * LANES : (q + 1) * LANES] for q in range(q_rows))
        ],
        axis=1,
    )
    scaled = rotated * jnp.concatenate([scale] * q_rows, axis=1)
    high, low = halves(scaled)
    both = mxu(back, jnp.concatenate([high, low, high], axis=0))
    mixed = jnp.where(every, both[:rows], both[rows:])
    stacked = jnp.concatenate([mixed[:, q * LANES : (q + 1) * LANES] for q in range(q_rows)], axis=0)
    both = mxu(jnp.concatenate(halves(stacked), axis=1), back_right)
    tall_ref[...] = both[:, :LANES] + both[:, LANES:]
    for j in range(rows):
        block = tall_ref[pl.ds(j, q_rows, stride=rows), :]
        column = layer * width + j * LANES
        block_ref[:, column : column + LANES] = block.astype(jnp.bfloat16)


def by_lines(array):
    rows, layers, width = array.shape
    array = array.reshape(rows, layers, width // LANES, LANES)
    return array.transpose(0, 2, 1, 3).reshape(rows, -1, LANES)


def precondition(queries, basis_in, basis_out, eigvals, here=False):
    q_rows, lines, _ = queries.shape
    layers, width = eigvals.shape
    operands, body, scratch = [queries, basis_in, basis_out, eigvals], precond_kernel, []
    if not here:
        operands = [in_hbm(a) for a in operands]
        body = functools.partial(fetched, len(operands), body)
        scratch = [pltpu.VMEM(a.shape, a.dtype) for a in operands] + [pltpu.SemaphoreType.DMA((len(operands),))]
    space = pltpu.VMEM if here else pltpu.HBM
    return pl.pallas_call(
        body,
        out_shape=jax.ShapeDtypeStruct((q_rows, layers * width), jnp.bfloat16),
        in_specs=[pl.BlockSpec(memory_space=space)] * len(operands),
        out_specs=VMEM,
        scratch_shapes=[
            pltpu.VMEM((q_rows * (lines + 8), LANES), jnp.float32),
            pltpu.VMEM((layers, q_rows * width // LANES, LANES), jnp.float32),
            pltpu.VMEM((layers, q_rows * width // LANES, LANES), jnp.float32),
            pltpu.VMEM((layers, 2 * width // LANES, LANES), jnp.float32),
        ]
        + scratch,
        compiler_params=pltpu.CompilerParams(vmem_limit_bytes=16 * MIB),
        cost_estimate=pl.CostEstimate(flops=10**9, bytes_accessed=4 * MIB, transcendentals=0),
        name="precond",
    )(*operands)


def fetched(n, body, *refs):
    operands, others = refs[:n], refs[n:]
    others, here, sems = others[: -n - 1], others[-n - 1 : -1], others[-1]
    copies = [pltpu.make_async_copy(a, b, sems.at[i]) for i, (a, b) in enumerate(zip(operands, here))]
    for copy in copies:
        copy.start()
    for copy in copies:
        copy.wait()
    body(*here, *others)


def split_kernel(layers, t_ref, slabs_ref, here_ref, wide_ref, sems):
    rows, chunks = BLOCK, sems.shape[0]
    lines = t_ref.shape[1]
    pitch = wide_ref.shape[0] // rows
    chunk = t_ref.shape[0] // chunks
    copies = [
        pltpu.make_async_copy(
            t_ref.at[pl.ds(i * chunk, chunk)], here_ref.at[pl.ds(i * chunk, chunk)], sems.at[i]
        )
        for i in range(chunks)
    ]
    for copy in copies:
        copy.start()
    for i in range(chunks):
        copies[i].wait()

        @pl.loop(i * chunk // rows, (i + 1) * chunk // rows)
        def _(block):
            at = pl.multiple_of(block * rows, rows)
            for row in range(rows):
                wide_ref[row * pitch : row * pitch + lines, :] = here_ref[at + row].astype(jnp.float32)
            for line in range(lines):
                slab = (line % layers) * (lines // layers) + line // layers
                slabs_ref[slab, pl.ds(at, rows), :] = wide_ref[pl.ds(line, rows, stride=pitch), :].astype(jnp.bfloat16)


def split_layers(train_grads):
    tr_rows, layers, width = train_grads.shape
    lines = layers * width // LANES
    return pl.pallas_call(
        functools.partial(split_kernel, layers),
        out_shape=jax.ShapeDtypeStruct((lines, tr_rows, LANES), jnp.bfloat16),
        in_specs=[pl.BlockSpec(memory_space=pltpu.HBM)],
        out_specs=VMEM,
        scratch_shapes=[
            pltpu.VMEM((tr_rows, lines, LANES), jnp.bfloat16),
            pltpu.VMEM((BLOCK * (lines + 8), LANES), jnp.float32),
            pltpu.SemaphoreType.DMA((8,)),
        ],
        compiler_params=pltpu.CompilerParams(vmem_limit_bytes=20 * MIB),
        cost_estimate=pl.CostEstimate(flops=10**9, bytes_accessed=16 * MIB, transcendentals=0),
        name="split",
    )(in_hbm(by_lines(train_grads)))


def order_rows(masks, q_rows, n_query):
    me, g = lax.axis_index("train"), lax.axis_index("group")
    row = lax.broadcasted_iota(jnp.int32, (q_rows, n_query), 0)
    query = lax.broadcasted_iota(jnp.int32, (q_rows, n_query), 1)
    order = []
    for mask in masks:
        c0, c1 = (jnp.where(g == 0, mask[0][c], mask[1][c]) for c in range(CORES))
        source = me ^ jnp.where(me % CORES == 0, c0, c1)
        order.append(jnp.where(query == source * q_rows + row, 1.0, 0.0))
    return jnp.concatenate(order, axis=0).astype(jnp.bfloat16)


def order_kernel(masks, q_rows, *refs):
    order_ref = refs[-1]
    order_ref[...] = order_rows(masks, q_rows, order_ref.shape[1])


def first_order(parts, stands_after, q_rows, n_query):
    masks = [came_masks(came) for a in parts for came in a.came]
    return pl.pallas_call(
        functools.partial(order_kernel, masks, q_rows),
        out_shape=jax.ShapeDtypeStruct((len(masks) * q_rows, n_query), jnp.bfloat16),
        in_specs=[pl.BlockSpec(memory_space=pl.ANY)] * len(stands_after),
        out_specs=VMEM,
        compiler_params=pltpu.CompilerParams(vmem_limit_bytes=16 * MIB),
        cost_estimate=pl.CostEstimate(flops=4 * 10**9, bytes_accessed=16 * MIB, transcendentals=0),
        name="order",
    )(*(a.array for a in stands_after))


def score_kernel(q_rows, masks, slabs_ref, first_ref, *refs):
    blocks, out_ref = refs[:-1], refs[-1]
    slabs = slabs_ref.shape[0]
    n_query = out_ref.shape[1]
    step = min(slabs, 8)
    total = None
    for at in range(0, slabs, step):
        train = jnp.concatenate([slabs_ref[at + i] for i in range(step)], axis=1)
        columns = slice(at * LANES, (at + step) * LANES)
        block = jnp.concatenate([ref[:, columns] for ref in blocks], axis=0)
        term = mxu(train, block, NT)
        total = term if total is None else total + term

    order = jnp.concatenate([first_ref[...], order_rows(masks, q_rows, n_query)], axis=0)
    high, low = halves(total)
    lowest = (total - high.astype(jnp.float32) - low.astype(jnp.float32)).astype(jnp.bfloat16)
    out_ref[...] = mxu(high, order) + mxu(low, order) + mxu(lowest, order)


def came_masks(came):
    xors = came ^ np.arange(came.shape[1])[None]
    masks = [[int(xors[g, c]) for c in range(CORES)] for g in range(GROUPS)]
    assert all((xors[g, c::CORES] == masks[g][c]).all() for g in range(GROUPS) for c in range(CORES))
    return masks


def per_device(n_train, train_grads, query_grads, basis_in, basis_out, eigvals):
    zs = n_train // (XS * CORES)
    rest = basis_in, basis_out, eigvals
    queries = by_lines(query_grads)
    places = [np.tile(np.arange(n_train), (GROUPS, 1))]
    far = [Blocks(queries, places).hop(far_z(pair)) for pair in range(1, zs // 2)]
    own = Blocks(precondition(queries, *rest), places)
    q_rows, width = own.array.shape
    n_query = n_train * q_rows
    at_x = own.hop(over_x)
    twin = own.hop(over_core)
    train_grads, own = after(train_grads, own)
    slabs = split_layers(train_grads)
    slabs, own = after(slabs, own)
    at_z = own.hop(over_z)
    parts = [own, twin, at_x, at_z]
    for pair, one in enumerate(far):
        slabs, one = after(slabs, one)
        one = Blocks(precondition(one.array, *rest, here=True), one.came)
        by_x, by_group = one.hop(over_x), one.hop(over_group)
        parts.append(one)
        if pair == 0:
            one.array, at_x = after(one.array, at_x)
            at_xz = at_x.hop(over_z)
            stacked = stack(at_x, one)
            parts += [at_xz, stacked.hop(over_core)]
            n_first = sum(len(a.came) for a in parts)
            order = first_order(parts, [twin, at_x], q_rows, n_query)
            order, by_x = after(order, by_x)
        else:
            parts.append(one.hop(over_core))
        half = by_x.columns(0, width // 2).hop(over_group)
        swapped = [by_x, by_group] + ([at_z, at_xz] if pair == 0 else [])
        half.array, *swapped = after(half.array, *swapped)
        parts += [by_x, by_group, stack(*swapped).hop(over_core)]
        corner = beside(half, by_group.columns(width // 2, width).hop(over_x))
        parts += [corner, corner.hop(over_core)]

    tr_rows = train_grads.shape[0]
    operands = [slabs, order] + [a.array for a in parts]
    masks = [came_masks(came) for a in parts for came in a.came]
    partial_scores = pl.pallas_call(
        functools.partial(score_kernel, q_rows, masks[n_first:]),
        out_shape=jax.ShapeDtypeStruct((tr_rows, n_query), jnp.float32),
        in_specs=[VMEM] * len(operands),
        out_specs=VMEM,
        compiler_params=pltpu.CompilerParams(vmem_limit_bytes=32 * MIB),
        cost_estimate=pl.CostEstimate(
            flops=2 * tr_rows * n_query * width, bytes_accessed=2 * width * (tr_rows + n_query), transcendentals=0
        ),
        name="scores",
    )(*operands)
    return lax.psum_scatter(partial_scores, "layer", scatter_dimension=1, tiled=True)


def solution(mesh):
    return jax.shard_map(
        functools.partial(per_device, mesh.shape["train"]),
        mesh=mesh,
        in_specs=(
            P(("group", "train"), "layer", None),
            P("train", "layer", None),
            P("layer", None, None),
            P("layer", None, None),
            P("layer", None),
        ),
        out_specs=P(("group", "train"), "layer"),
        check_vma=False,
    )
```

```python
import functools

import jax
import jax.numpy as jnp
import numpy as np
from jax import lax
from jax.experimental import pallas as pl
from jax.experimental.pallas import tpu as pltpu
from jax.sharding import PartitionSpec as P

CORES = 2
XS = 2
GROUPS = 2
LANES = 128
BLOCK = 16
MIB = 1024 * 1024
VMEM = pl.BlockSpec(memory_space=pltpu.VMEM)
NN = (((1,), (0,)), ((), ()))
NT = (((1,), (1,)), ((), ()))
TN = (((0,), (0,)), ((), ()))


def mxu(a, b, dims=NN):
    return lax.dot_general(a, b, dims, preferred_element_type=jnp.float32)


def halves(a):
    high = a.astype(jnp.bfloat16)
    return high, (a - high.astype(jnp.float32)).astype(jnp.bfloat16)


def in_hbm(array):
    return pltpu.with_memory_space_constraint(array, pltpu.HBM)


class Blocks:
    def __init__(self, array, came):
        self.array, self.came = array, came

    def hop(self, turn):
        groups, n_train = self.came[0].shape
        perm, came = [], [np.zeros_like(a) for a in self.came]
        for g in range(groups):
            for t in range(n_train):
                z, x, c = t // (XS * CORES), t // CORES % XS, t % CORES
                to_g, z, x, c = turn(g, z, x, c)
                to_t = (z * XS + x) * CORES + c
                perm.append((g * n_train + t, to_g * n_train + to_t))
                for here, there in zip(self.came, came):
                    there[to_g, to_t] = here[g, t]
        return Blocks(lax.ppermute(self.array, ("group", "train"), perm), came)

    def columns(self, start, stop):
        return Blocks(self.array[:, start:stop], self.came)


def stack(*parts):
    return Blocks(jnp.concatenate([a.array for a in parts], axis=0), sum((a.came for a in parts), []))


def beside(left, right):
    assert all((a == b).all() for a, b in zip(left.came, right.came))
    return Blocks(jnp.concatenate([left.array, right.array], axis=1), left.came)


def after(kernel_result, *parts):
    arrays, kernel_result = lax.optimization_barrier(([a.array for a in parts], kernel_result))
    return kernel_result, *(Blocks(array, a.came) for array, a in zip(arrays, parts))


def over_core(g, z, x, c):
    return g, z, x, c ^ 1


def over_x(g, z, x, c):
    return g, z, x ^ 1, c


def over_z(g, z, x, c):
    return g, z ^ 1, x, c


def far_z(pair):
    return lambda g, z, x, c: (g, z ^ (2 * pair + (g == c)), x, c)


def over_group(g, z, x, c):
    return g ^ 1, z, x, c


def spread_lines(q_ref, lines_ref):
    q_rows, lines, _ = q_ref.shape
    pitch = lines_ref.shape[0] // q_rows
    for q in range(q_rows):
        lines_ref[q * pitch : q * pitch + lines, :] = q_ref[q].astype(jnp.float32)


def precond_kernel(q_ref, in_ref, out_ref, eig_ref, block_ref, *refs):
    made, (lines_ref, wide_ref, tall_ref, even_ref) = refs[:-4], refs[-4:]
    spread_lines(q_ref, lines_ref)
    for layer in range(in_ref.shape[0]):
        factors = prepare_layer(layer, in_ref, out_ref, eig_ref, even_ref.at[layer])
        for ref, factor in zip(made, factors):
            ref[layer] = factor
        precond_layer(layer, factors, lines_ref, block_ref, wide_ref.at[layer], tall_ref.at[layer])


def later_kernel(q_ref, *refs):
    made, (block_ref, lines_ref, wide_ref, tall_ref) = refs[:-4], refs[-4:]
    spread_lines(q_ref, lines_ref)
    for layer in range(wide_ref.shape[0]):
        factors = [ref[layer] for ref in made]
        precond_layer(layer, factors, lines_ref, block_ref, wide_ref.at[layer], tall_ref.at[layer])


def prepare_layer(layer, in_ref, out_ref, eig_ref, even_ref):
    width = eig_ref.shape[1]
    rows = width // LANES
    p_out = out_ref.shape[2]
    left = lax.broadcasted_iota(jnp.int32, (1, LANES), 1) < p_out

    eig = eig_ref[layer : layer + 1, :]
    damping = 0.1 / width * jnp.sum(eig, axis=1, keepdims=True)
    for j in range(rows):
        pair = eig[:, j * LANES : (j + 1) * LANES]
        turned = pltpu.roll(pair, p_out, 1)
        even_ref[2 * j : 2 * j + 1, :] = jnp.where(left, pair, turned)
        even_ref[2 * j + 1 : 2 * j + 2, :] = jnp.where(left, turned, pair)
    scale = 1.0 / (even_ref[...] + damping)

    by_row = [in_ref[layer, pl.ds(p, rows, stride=2), :] for p in range(2)]
    back_left = jnp.concatenate(by_row, axis=0)
    fore_left = jnp.concatenate(by_row, axis=1)
    back_high, back_low = halves(back_left)
    fore_high, fore_low = halves(fore_left)
    fore = jnp.concatenate([fore_high, fore_high, fore_low], axis=0)
    back = jnp.concatenate([back_high, back_high, back_low], axis=1)

    basis = out_ref[layer]
    empty = jnp.zeros((p_out, p_out), jnp.bfloat16)

    def twice(a):
        return jnp.concatenate(
            [jnp.concatenate([a, empty], axis=1), jnp.concatenate([empty, a], axis=1)], axis=0
        )

    right_high, right_low = halves(basis)
    turned_high, turned_low = halves(basis.T)
    fore_right = jnp.concatenate([twice(right_high), twice(right_low)], axis=1)
    back_high, back_low = twice(turned_high), twice(turned_low)
    back_right = jnp.concatenate(
        [
            jnp.concatenate([back_high, back_low], axis=1),
            jnp.concatenate([back_high, jnp.zeros_like(back_low)], axis=1),
        ],
        axis=0,
    )
    return scale, fore, back, fore_right, back_right


def precond_layer(layer, factors, lines_ref, block_ref, wide_ref, tall_ref):
    scale, fore, back, fore_right, back_right = factors
    q_rows = block_ref.shape[0]
    width = wide_ref.shape[0] * LANES // q_rows
    layers = block_ref.shape[1] // width
    rows = width // LANES
    pitch = lines_ref.shape[0] // q_rows
    p_in = scale.shape[0]
    p_out = width // p_in
    left = lax.broadcasted_iota(jnp.int32, (1, LANES), 1) < p_out

    stacked = jnp.concatenate(
        [lines_ref[pl.ds(layers * j + layer, q_rows, stride=pitch), :] for j in range(rows)], axis=0
    ).astype(jnp.bfloat16)
    both = mxu(stacked, fore_right)
    wide_ref[...] = both[:, :LANES] + both[:, LANES:]
    by_query = jnp.concatenate([wide_ref[pl.ds(q, rows, stride=q_rows), :] for q in range(q_rows)], axis=1)
    high, low = halves(by_query)
    both = mxu(fore, jnp.concatenate([high, low, high], axis=0), TN)
    every = jnp.concatenate([left] * q_rows, axis=1)
    rotated = jnp.where(every, both[:p_in], both[p_in:])
    rotated = jnp.concatenate(
        [
            part + pltpu.roll(part, p_out, 1)
            for part in (rotated[:, q * LANES : (q + 1) * LANES] for q in range(q_rows))
        ],
        axis=1,
    )
    scaled = rotated * jnp.concatenate([scale] * q_rows, axis=1)
    high, low = halves(scaled)
    both = mxu(back, jnp.concatenate([high, low, high], axis=0))
    mixed = jnp.where(every, both[:rows], both[rows:])
    stacked = jnp.concatenate([mixed[:, q * LANES : (q + 1) * LANES] for q in range(q_rows)], axis=0)
    both = mxu(jnp.concatenate(halves(stacked), axis=1), back_right)
    tall_ref[...] = both[:, :LANES] + both[:, LANES:]
    for j in range(rows):
        block = tall_ref[pl.ds(j, q_rows, stride=rows), :]
        column = layer * width + j * LANES
        block_ref[:, column : column + LANES] = block.astype(jnp.bfloat16)


def by_lines(array):
    rows, layers, width = array.shape
    array = array.reshape(rows, layers, width // LANES, LANES)
    return array.transpose(0, 2, 1, 3).reshape(rows, -1, LANES)


def block_scratch(q_rows, layers, width):
    lines = layers * width // LANES
    return [pltpu.VMEM((q_rows * (lines + 8), LANES), jnp.float32)] + [
        pltpu.VMEM((layers, q_rows * width // LANES, LANES), jnp.float32)
    ] * 2


def precondition(queries, basis_in, basis_out, eigvals):
    q_rows = queries.shape[0]
    layers, width = eigvals.shape
    p_in, rows = basis_in.shape[1], width // LANES
    operands = [in_hbm(a) for a in (queries, basis_in, basis_out, eigvals)]
    shapes = [(p_in, LANES), (3 * rows, 2 * p_in), (2 * rows, 3 * p_in), (LANES, 2 * LANES), (2 * LANES, 2 * LANES)]
    types = [jnp.float32] + [jnp.bfloat16] * 4
    block, *factors = pl.pallas_call(
        functools.partial(fetched, len(operands), precond_kernel),
        out_shape=[jax.ShapeDtypeStruct((q_rows, layers * width), jnp.bfloat16)]
        + [jax.ShapeDtypeStruct((layers, *shape), dtype) for shape, dtype in zip(shapes, types)],
        in_specs=[pl.BlockSpec(memory_space=pltpu.HBM)] * len(operands),
        out_specs=[VMEM] * 6,
        scratch_shapes=block_scratch(q_rows, layers, width)
        + [pltpu.VMEM((layers, 2 * rows, LANES), jnp.float32)]
        + [pltpu.VMEM(a.shape, a.dtype) for a in operands]
        + [pltpu.SemaphoreType.DMA((len(operands),))],
        compiler_params=pltpu.CompilerParams(vmem_limit_bytes=16 * MIB),
        cost_estimate=pl.CostEstimate(flops=10**9, bytes_accessed=4 * MIB, transcendentals=0),
        name="precond",
    )(*operands)
    return block, factors


def precondition_more(queries, factors):
    q_rows, lines, _ = queries.shape
    layers = factors[0].shape[0]
    operands = [queries, *factors]
    return pl.pallas_call(
        later_kernel,
        out_shape=jax.ShapeDtypeStruct((q_rows, lines * LANES), jnp.bfloat16),
        in_specs=[VMEM] * len(operands),
        out_specs=VMEM,
        scratch_shapes=block_scratch(q_rows, layers, lines * LANES // layers),
        compiler_params=pltpu.CompilerParams(vmem_limit_bytes=16 * MIB),
        cost_estimate=pl.CostEstimate(flops=10**9, bytes_accessed=4 * MIB, transcendentals=0),
        name="precond",
    )(*operands)


def fetched(n, body, *refs):
    operands, others = refs[:n], refs[n:]
    others, here, sems = others[: -n - 1], others[-n - 1 : -1], others[-1]
    copies = [pltpu.make_async_copy(a, b, sems.at[i]) for i, (a, b) in enumerate(zip(operands, here))]
    for copy in copies:
        copy.start()
    for copy in copies:
        copy.wait()
    body(*here, *others)


def split_kernel(layers, t_ref, slabs_ref, here_ref, wide_ref, sems):
    rows, chunks = BLOCK, sems.shape[0]
    lines = t_ref.shape[1]
    pitch = wide_ref.shape[0] // rows
    chunk = t_ref.shape[0] // chunks
    copies = [
        pltpu.make_async_copy(
            t_ref.at[pl.ds(i * chunk, chunk)], here_ref.at[pl.ds(i * chunk, chunk)], sems.at[i]
        )
        for i in range(chunks)
    ]
    for copy in copies:
        copy.start()
    for i in range(chunks):
        copies[i].wait()

        @pl.loop(i * chunk // rows, (i + 1) * chunk // rows)
        def _(block):
            at = pl.multiple_of(block * rows, rows)
            for row in range(rows):
                wide_ref[row * pitch : row * pitch + lines, :] = here_ref[at + row].astype(jnp.float32)
            for line in range(lines):
                slab = (line % layers) * (lines // layers) + line // layers
                slabs_ref[slab, pl.ds(at, rows), :] = wide_ref[pl.ds(line, rows, stride=pitch), :].astype(jnp.bfloat16)


def split_layers(train_grads):
    tr_rows, layers, width = train_grads.shape
    lines = layers * width // LANES
    return pl.pallas_call(
        functools.partial(split_kernel, layers),
        out_shape=jax.ShapeDtypeStruct((lines, tr_rows, LANES), jnp.bfloat16),
        in_specs=[pl.BlockSpec(memory_space=pltpu.HBM)],
        out_specs=VMEM,
        scratch_shapes=[
            pltpu.VMEM((tr_rows, lines, LANES), jnp.bfloat16),
            pltpu.VMEM((BLOCK * (lines + 8), LANES), jnp.float32),
            pltpu.SemaphoreType.DMA((8,)),
        ],
        compiler_params=pltpu.CompilerParams(vmem_limit_bytes=20 * MIB),
        cost_estimate=pl.CostEstimate(flops=10**9, bytes_accessed=16 * MIB, transcendentals=0),
        name="split",
    )(in_hbm(by_lines(train_grads)))


def score_kernel(masks, slabs_ref, *refs):
    blocks, out_ref = refs[:-1], refs[-1]
    slabs = slabs_ref.shape[0]
    q_rows = out_ref.shape[1] // len(masks)
    n_query = out_ref.shape[1]
    step = min(slabs, 8)
    total = None
    for at in range(0, slabs, step):
        train = jnp.concatenate([slabs_ref[at + i] for i in range(step)], axis=1)
        columns = slice(at * LANES, (at + step) * LANES)
        block = jnp.concatenate([ref[:, columns] for ref in blocks], axis=0)
        term = mxu(train, block, NT)
        total = term if total is None else total + term

    me, g = lax.axis_index("train"), lax.axis_index("group")
    row = lax.broadcasted_iota(jnp.int32, (q_rows, n_query), 0)
    query = lax.broadcasted_iota(jnp.int32, (q_rows, n_query), 1)
    order = []
    for mask in masks:
        c0, c1 = (jnp.where(g == 0, mask[0][c], mask[1][c]) for c in range(CORES))
        source = me ^ jnp.where(me % CORES == 0, c0, c1)
        order.append(jnp.where(query == source * q_rows + row, 1.0, 0.0))
    order = jnp.concatenate(order, axis=0).astype(jnp.bfloat16)
    high, low = halves(total)
    lowest = (total - high.astype(jnp.float32) - low.astype(jnp.float32)).astype(jnp.bfloat16)
    out_ref[...] = mxu(high, order) + mxu(low, order) + mxu(lowest, order)


def came_masks(came):
    xors = came ^ np.arange(came.shape[1])[None]
    masks = [[int(xors[g, c]) for c in range(CORES)] for g in range(GROUPS)]
    assert all((xors[g, c::CORES] == masks[g][c]).all() for g in range(GROUPS) for c in range(CORES))
    return masks


def per_device(n_train, train_grads, query_grads, basis_in, basis_out, eigvals):
    zs = n_train // (XS * CORES)
    rest = basis_in, basis_out, eigvals
    queries = by_lines(query_grads)
    places = [np.tile(np.arange(n_train), (GROUPS, 1))]
    far = [Blocks(queries, places).hop(far_z(pair)) for pair in range(1, zs // 2)]
    block, factors = precondition(queries, *rest)
    own = Blocks(block, places)
    q_rows, width = own.array.shape
    n_query = n_train * q_rows
    at_x = own.hop(over_x)
    twin = own.hop(over_core)
    train_grads, own = after(train_grads, own)
    slabs = split_layers(train_grads)
    slabs, own = after(slabs, own)
    at_z = own.hop(over_z)
    parts = [own, twin, at_x, at_z]
    for pair, one in enumerate(far):
        slabs, one = after(slabs, one)
        one = Blocks(precondition_more(one.array, factors), one.came)
        by_x, by_group = one.hop(over_x), one.hop(over_group)
        parts.append(one)
        if pair == 0:
            one.array, at_x = after(one.array, at_x)
            at_xz = at_x.hop(over_z)
            stacked = stack(at_x, one)
            stacked.array, by_x = after(stacked.array, by_x)
            parts += [at_xz, stacked.hop(over_core)]
        else:
            parts.append(one.hop(over_core))
        parts += [by_x, by_group, stack(by_x, by_group).hop(over_core)]
        half = by_x.columns(0, width // 2).hop(over_group)
        if pair == 0:
            half.array, near, near_x = after(half.array, at_z, at_xz)
            parts.append(stack(near, near_x).hop(over_core))
        corner = beside(half, by_group.columns(width // 2, width).hop(over_x))
        parts += [corner, corner.hop(over_core)]

    tr_rows = train_grads.shape[0]
    operands = [slabs] + [a.array for a in parts]
    partial_scores = pl.pallas_call(
        functools.partial(score_kernel, [came_masks(came) for a in parts for came in a.came]),
        out_shape=jax.ShapeDtypeStruct((tr_rows, n_query), jnp.float32),
        in_specs=[VMEM] * len(operands),
        out_specs=VMEM,
        compiler_params=pltpu.CompilerParams(vmem_limit_bytes=32 * MIB),
        cost_estimate=pl.CostEstimate(
            flops=2 * tr_rows * n_query * width, bytes_accessed=2 * width * (tr_rows + n_query), transcendentals=0
        ),
        name="scores",
    )(*operands)
    return lax.psum_scatter(partial_scores, "layer", scatter_dimension=1, tiled=True)


def solution(mesh):
    return jax.shard_map(
        functools.partial(per_device, mesh.shape["train"]),
        mesh=mesh,
        in_specs=(
            P(("group", "train"), "layer", None),
            P("train", "layer", None),
            P("layer", None, None),
            P("layer", None, None),
            P("layer", None),
        ),
        out_specs=P(("group", "train"), "layer"),
        check_vma=False,
    )
```

```python
import functools

import jax
import jax.numpy as jnp
import numpy as np
from jax import lax
from jax.experimental import pallas as pl
from jax.experimental.pallas import tpu as pltpu
from jax.sharding import PartitionSpec as P

CORES = 2
XS = 2
GROUPS = 2
LANES = 128
BLOCK = 16
MIB = 1024 * 1024
VMEM = pl.BlockSpec(memory_space=pltpu.VMEM)
NN = (((1,), (0,)), ((), ()))
NT = (((1,), (1,)), ((), ()))
TN = (((0,), (0,)), ((), ()))


def mxu(a, b, dims=NN):
    return lax.dot_general(a, b, dims, preferred_element_type=jnp.float32)


def halves(a):
    high = a.astype(jnp.bfloat16)
    return high, (a - high.astype(jnp.float32)).astype(jnp.bfloat16)


def in_hbm(array):
    return pltpu.with_memory_space_constraint(array, pltpu.HBM)


class Blocks:
    def __init__(self, array, came):
        self.array, self.came = array, came

    def hop(self, turn):
        groups, n_train = self.came[0].shape
        perm, came = [], [np.zeros_like(a) for a in self.came]
        for g in range(groups):
            for t in range(n_train):
                z, x, c = t // (XS * CORES), t // CORES % XS, t % CORES
                to_g, z, x, c = turn(g, z, x, c)
                to_t = (z * XS + x) * CORES + c
                perm.append((g * n_train + t, to_g * n_train + to_t))
                for here, there in zip(self.came, came):
                    there[to_g, to_t] = here[g, t]
        return Blocks(lax.ppermute(self.array, ("group", "train"), perm), came)

    def columns(self, start, stop):
        return Blocks(self.array[:, start:stop], self.came)


def stack(*parts):
    return Blocks(jnp.concatenate([a.array for a in parts], axis=0), sum((a.came for a in parts), []))


def beside(left, right):
    assert all((a == b).all() for a, b in zip(left.came, right.came))
    return Blocks(jnp.concatenate([left.array, right.array], axis=1), left.came)


def after(kernel_result, *parts):
    arrays, kernel_result = lax.optimization_barrier(([a.array for a in parts], kernel_result))
    return kernel_result, *(Blocks(array, a.came) for array, a in zip(arrays, parts))


def over_core(g, z, x, c):
    return g, z, x, c ^ 1


def over_x(g, z, x, c):
    return g, z, x ^ 1, c


def over_z(g, z, x, c):
    return g, z ^ 1, x, c


def far_z(pair):
    return lambda g, z, x, c: (g, z ^ (2 * pair + (g == c)), x, c)


def over_group(g, z, x, c):
    return g ^ 1, z, x, c


def spread_lines(q_ref, lines_ref):
    q_rows, lines, _ = q_ref.shape
    pitch = lines_ref.shape[0] // q_rows
    for q in range(q_rows):
        lines_ref[q * pitch : q * pitch + lines, :] = q_ref[q].astype(jnp.float32)


def precond_kernel(q_ref, in_ref, out_ref, eig_ref, block_ref, *refs):
    made, (lines_ref, wide_ref, tall_ref, even_ref) = refs[:-4], refs[-4:]
    spread_lines(q_ref, lines_ref)
    for layer in range(in_ref.shape[0]):
        factors = prepare_layer(layer, in_ref, out_ref, eig_ref, even_ref.at[layer])
        for ref, factor in zip(made, factors):
            ref[layer] = factor
        precond_layer(layer, factors, lines_ref, block_ref, wide_ref.at[layer], tall_ref.at[layer])


def later_kernel(q_ref, *refs):
    made, (block_ref, lines_ref, wide_ref, tall_ref) = refs[:-4], refs[-4:]
    spread_lines(q_ref, lines_ref)
    for layer in range(wide_ref.shape[0]):
        factors = [ref[layer] for ref in made]
        precond_layer(layer, factors, lines_ref, block_ref, wide_ref.at[layer], tall_ref.at[layer])


def prepare_layer(layer, in_ref, out_ref, eig_ref, even_ref):
    width = eig_ref.shape[1]
    rows = width // LANES
    p_out = out_ref.shape[2]
    left = lax.broadcasted_iota(jnp.int32, (1, LANES), 1) < p_out

    eig = eig_ref[layer : layer + 1, :]
    damping = 0.1 / width * jnp.sum(eig, axis=1, keepdims=True)
    for j in range(rows):
        pair = eig[:, j * LANES : (j + 1) * LANES]
        turned = pltpu.roll(pair, p_out, 1)
        even_ref[2 * j : 2 * j + 1, :] = jnp.where(left, pair, turned)
        even_ref[2 * j + 1 : 2 * j + 2, :] = jnp.where(left, turned, pair)
    scale = 1.0 / (even_ref[...] + damping)

    by_row = [in_ref[layer, pl.ds(p, rows, stride=2), :] for p in range(2)]
    back_left = jnp.concatenate(by_row, axis=0)
    fore_left = jnp.concatenate(by_row, axis=1)
    back_high, back_low = halves(back_left)
    fore_high, fore_low = halves(fore_left)
    fore = jnp.concatenate([fore_high, fore_high, fore_low], axis=0)
    back = jnp.concatenate([back_high, back_high, back_low], axis=1)

    basis = out_ref[layer]
    empty = jnp.zeros((p_out, p_out), jnp.bfloat16)

    def twice(a):
        return jnp.concatenate(
            [jnp.concatenate([a, empty], axis=1), jnp.concatenate([empty, a], axis=1)], axis=0
        )

    right_high, right_low = halves(basis)
    turned_high, turned_low = halves(basis.T)
    fore_right = jnp.concatenate([twice(right_high), twice(right_low)], axis=1)
    back_high, back_low = twice(turned_high), twice(turned_low)
    back_right = jnp.concatenate(
        [
            jnp.concatenate([back_high, back_low], axis=1),
            jnp.concatenate([back_high, jnp.zeros_like(back_low)], axis=1),
        ],
        axis=0,
    )
    return scale, fore, back, fore_right, back_right


def precond_layer(layer, factors, lines_ref, block_ref, wide_ref, tall_ref):
    scale, fore, back, fore_right, back_right = factors
    q_rows = block_ref.shape[0]
    width = wide_ref.shape[0] * LANES // q_rows
    layers = block_ref.shape[1] // width
    rows = width // LANES
    pitch = lines_ref.shape[0] // q_rows
    p_in = scale.shape[0]
    p_out = width // p_in
    left = lax.broadcasted_iota(jnp.int32, (1, LANES), 1) < p_out

    stacked = jnp.concatenate(
        [lines_ref[pl.ds(layers * j + layer, q_rows, stride=pitch), :] for j in range(rows)], axis=0
    ).astype(jnp.bfloat16)
    both = mxu(stacked, fore_right)
    wide_ref[...] = both[:, :LANES] + both[:, LANES:]
    by_query = jnp.concatenate([wide_ref[pl.ds(q, rows, stride=q_rows), :] for q in range(q_rows)], axis=1)
    high, low = halves(by_query)
    both = mxu(fore, jnp.concatenate([high, low, high], axis=0), TN)
    every = jnp.concatenate([left] * q_rows, axis=1)
    rotated = jnp.where(every, both[:p_in], both[p_in:])
    rotated = jnp.concatenate(
        [
            part + pltpu.roll(part, p_out, 1)
            for part in (rotated[:, q * LANES : (q + 1) * LANES] for q in range(q_rows))
        ],
        axis=1,
    )
    scaled = rotated * jnp.concatenate([scale] * q_rows, axis=1)
    high, low = halves(scaled)
    both = mxu(back, jnp.concatenate([high, low, high], axis=0))
    mixed = jnp.where(every, both[:rows], both[rows:])
    stacked = jnp.concatenate([mixed[:, q * LANES : (q + 1) * LANES] for q in range(q_rows)], axis=0)
    both = mxu(jnp.concatenate(halves(stacked), axis=1), back_right)
    tall_ref[...] = both[:, :LANES] + both[:, LANES:]
    for j in range(rows):
        block = tall_ref[pl.ds(j, q_rows, stride=rows), :]
        column = layer * width + j * LANES
        block_ref[:, column : column + LANES] = block.astype(jnp.bfloat16)


def by_lines(array):
    rows, layers, width = array.shape
    array = array.reshape(rows, layers, width // LANES, LANES)
    return array.transpose(0, 2, 1, 3).reshape(rows, -1, LANES)


def block_scratch(q_rows, layers, width):
    lines = layers * width // LANES
    return [pltpu.VMEM((q_rows * (lines + 8), LANES), jnp.float32)] + [
        pltpu.VMEM((layers, q_rows * width // LANES, LANES), jnp.float32)
    ] * 2


def precondition(queries, basis_in, basis_out, eigvals):
    q_rows = queries.shape[0]
    layers, width = eigvals.shape
    p_in, rows = basis_in.shape[1], width // LANES
    operands = [in_hbm(a) for a in (queries, basis_in, basis_out, eigvals)]
    shapes = [(p_in, LANES), (3 * rows, 2 * p_in), (2 * rows, 3 * p_in), (LANES, 2 * LANES), (2 * LANES, 2 * LANES)]
    types = [jnp.float32] + [jnp.bfloat16] * 4
    block, *factors = pl.pallas_call(
        functools.partial(fetched, len(operands), precond_kernel),
        out_shape=[jax.ShapeDtypeStruct((q_rows, layers * width), jnp.bfloat16)]
        + [jax.ShapeDtypeStruct((layers, *shape), dtype) for shape, dtype in zip(shapes, types)],
        in_specs=[pl.BlockSpec(memory_space=pltpu.HBM)] * len(operands),
        out_specs=[VMEM] * 6,
        scratch_shapes=block_scratch(q_rows, layers, width)
        + [pltpu.VMEM((layers, 2 * rows, LANES), jnp.float32)]
        + [pltpu.VMEM(a.shape, a.dtype) for a in operands]
        + [pltpu.SemaphoreType.DMA((len(operands),))],
        compiler_params=pltpu.CompilerParams(vmem_limit_bytes=16 * MIB),
        cost_estimate=pl.CostEstimate(flops=10**9, bytes_accessed=4 * MIB, transcendentals=0),
        name="precond",
    )(*operands)
    return block, factors


def precondition_more(queries, factors):
    q_rows, lines, _ = queries.shape
    layers = factors[0].shape[0]
    operands = [queries, *factors]
    return pl.pallas_call(
        later_kernel,
        out_shape=jax.ShapeDtypeStruct((q_rows, lines * LANES), jnp.bfloat16),
        in_specs=[VMEM] * len(operands),
        out_specs=VMEM,
        scratch_shapes=block_scratch(q_rows, layers, lines * LANES // layers),
        compiler_params=pltpu.CompilerParams(vmem_limit_bytes=16 * MIB),
        cost_estimate=pl.CostEstimate(flops=10**9, bytes_accessed=4 * MIB, transcendentals=0),
        name="precond",
    )(*operands)


def fetched(n, body, *refs):
    operands, others = refs[:n], refs[n:]
    others, here, sems = others[: -n - 1], others[-n - 1 : -1], others[-1]
    copies = [pltpu.make_async_copy(a, b, sems.at[i]) for i, (a, b) in enumerate(zip(operands, here))]
    for copy in copies:
        copy.start()
    for copy in copies:
        copy.wait()
    body(*here, *others)


def split_kernel(layers, t_ref, slabs_ref, here_ref, wide_ref, sems):
    rows, chunks = BLOCK, sems.shape[0]
    lines = t_ref.shape[1]
    pitch = wide_ref.shape[0] // rows
    chunk = t_ref.shape[0] // chunks
    copies = [
        pltpu.make_async_copy(
            t_ref.at[pl.ds(i * chunk, chunk)], here_ref.at[pl.ds(i * chunk, chunk)], sems.at[i]
        )
        for i in range(chunks)
    ]
    for copy in copies:
        copy.start()
    for i in range(chunks):
        copies[i].wait()

        @pl.loop(i * chunk // rows, (i + 1) * chunk // rows)
        def _(block):
            at = pl.multiple_of(block * rows, rows)
            for row in range(rows):
                wide_ref[row * pitch : row * pitch + lines, :] = here_ref[at + row].astype(jnp.float32)
            for line in range(lines):
                slab = (line % layers) * (lines // layers) + line // layers
                slabs_ref[slab, pl.ds(at, rows), :] = wide_ref[pl.ds(line, rows, stride=pitch), :].astype(jnp.bfloat16)


def split_layers(train_grads):
    tr_rows, layers, width = train_grads.shape
    lines = layers * width // LANES
    return pl.pallas_call(
        functools.partial(split_kernel, layers),
        out_shape=jax.ShapeDtypeStruct((lines, tr_rows, LANES), jnp.bfloat16),
        in_specs=[pl.BlockSpec(memory_space=pltpu.HBM)],
        out_specs=VMEM,
        scratch_shapes=[
            pltpu.VMEM((tr_rows, lines, LANES), jnp.bfloat16),
            pltpu.VMEM((BLOCK * (lines + 8), LANES), jnp.float32),
            pltpu.SemaphoreType.DMA((8,)),
        ],
        compiler_params=pltpu.CompilerParams(vmem_limit_bytes=20 * MIB),
        cost_estimate=pl.CostEstimate(flops=10**9, bytes_accessed=16 * MIB, transcendentals=0),
        name="split",
    )(in_hbm(by_lines(train_grads)))


def score_kernel(masks, slabs_ref, *refs):
    blocks, out_ref = refs[:-1], refs[-1]
    slabs = slabs_ref.shape[0]
    q_rows = out_ref.shape[1] // len(masks)
    n_query = out_ref.shape[1]
    step = min(slabs, 8)
    total = None
    for at in range(0, slabs, step):
        train = jnp.concatenate([slabs_ref[at + i] for i in range(step)], axis=1)
        columns = slice(at * LANES, (at + step) * LANES)
        block = jnp.concatenate([ref[:, columns] for ref in blocks], axis=0)
        term = mxu(train, block, NT)
        total = term if total is None else total + term

    me, g = lax.axis_index("train"), lax.axis_index("group")
    row = lax.broadcasted_iota(jnp.int32, (q_rows, n_query), 0)
    query = lax.broadcasted_iota(jnp.int32, (q_rows, n_query), 1)
    order = []
    for mask in masks:
        c0, c1 = (jnp.where(g == 0, mask[0][c], mask[1][c]) for c in range(CORES))
        source = me ^ jnp.where(me % CORES == 0, c0, c1)
        order.append(jnp.where(query == source * q_rows + row, 1.0, 0.0))
    order = jnp.concatenate(order, axis=0).astype(jnp.bfloat16)
    high, low = halves(total)
    lowest = (total - high.astype(jnp.float32) - low.astype(jnp.float32)).astype(jnp.bfloat16)
    out_ref[...] = mxu(high, order) + mxu(low, order) + mxu(lowest, order)


def came_masks(came):
    xors = came ^ np.arange(came.shape[1])[None]
    masks = [[int(xors[g, c]) for c in range(CORES)] for g in range(GROUPS)]
    assert all((xors[g, c::CORES] == masks[g][c]).all() for g in range(GROUPS) for c in range(CORES))
    return masks


def per_device(n_train, train_grads, query_grads, basis_in, basis_out, eigvals):
    zs = n_train // (XS * CORES)
    rest = basis_in, basis_out, eigvals
    queries = by_lines(query_grads)
    places = [np.tile(np.arange(n_train), (GROUPS, 1))]
    far = [Blocks(queries, places).hop(far_z(pair)) for pair in range(1, zs // 2)]
    block, factors = precondition(queries, *rest)
    own = Blocks(block, places)
    q_rows, width = own.array.shape
    n_query = n_train * q_rows
    cut = 3 * width // 4
    at_x = own.hop(over_x)
    twin = own.hop(over_core)
    train_grads, own = after(train_grads, own)
    slabs = split_layers(train_grads)
    slabs, own = after(slabs, own)
    at_z = own.hop(over_z)
    parts = [own, twin, at_x, at_z]
    for pair, one in enumerate(far):
        slabs, one = after(slabs, one)
        one = Blocks(precondition_more(one.array, factors), one.came)
        by_x, by_group = one.hop(over_x), one.hop(over_group)
        parts.append(one)
        if pair == 0:
            one.array, at_x = after(one.array, at_x)
            at_xz = at_x.hop(over_z)
            stacked = stack(at_x, one)
            stacked.array, by_x = after(stacked.array, by_x)
            parts += [at_xz, stacked.hop(over_core)]
        else:
            parts.append(one.hop(over_core))
        parts += [by_x, by_group, stack(by_x, by_group).hop(over_core)]
        half = by_x.columns(0, cut).hop(over_group)
        if pair == 0:
            half.array, near, near_x = after(half.array, at_z, at_xz)
            parts.append(stack(near, near_x).hop(over_core))
        corner = beside(half, by_group.columns(cut, width).hop(over_x))
        parts += [corner, corner.hop(over_core)]

    tr_rows = train_grads.shape[0]
    operands = [slabs] + [a.array for a in parts]
    partial_scores = pl.pallas_call(
        functools.partial(score_kernel, [came_masks(came) for a in parts for came in a.came]),
        out_shape=jax.ShapeDtypeStruct((tr_rows, n_query), jnp.float32),
        in_specs=[VMEM] * len(operands),
        out_specs=VMEM,
        compiler_params=pltpu.CompilerParams(vmem_limit_bytes=32 * MIB),
        cost_estimate=pl.CostEstimate(
            flops=2 * tr_rows * n_query * width, bytes_accessed=2 * width * (tr_rows + n_query), transcendentals=0
        ),
        name="scores",
    )(*operands)
    return lax.psum_scatter(partial_scores, "layer", scatter_dimension=1, tiled=True)


def solution(mesh):
    return jax.shard_map(
        functools.partial(per_device, mesh.shape["train"]),
        mesh=mesh,
        in_specs=(
            P(("group", "train"), "layer", None),
            P("train", "layer", None),
            P("layer", None, None),
            P("layer", None, None),
            P("layer", None),
        ),
        out_specs=P(("group", "train"), "layer"),
        check_vma=False,
    )
```

```python
import functools

import jax
import jax.numpy as jnp
import numpy as np
from jax import lax
from jax.experimental import pallas as pl
from jax.experimental.pallas import tpu as pltpu
from jax.sharding import PartitionSpec as P

CORES = 2
XS = 2
GROUPS = 2
LANES = 128
BLOCK = 16
MIB = 1024 * 1024
VMEM = pl.BlockSpec(memory_space=pltpu.VMEM)
NN = (((1,), (0,)), ((), ()))
NT = (((1,), (1,)), ((), ()))
TN = (((0,), (0,)), ((), ()))


def mxu(a, b, dims=NN):
    return lax.dot_general(a, b, dims, preferred_element_type=jnp.float32)


def halves(a):
    high = a.astype(jnp.bfloat16)
    return high, (a - high.astype(jnp.float32)).astype(jnp.bfloat16)


def in_hbm(array):
    return pltpu.with_memory_space_constraint(array, pltpu.HBM)


class Blocks:
    def __init__(self, array, came):
        self.array, self.came = array, came

    def hop(self, turn):
        groups, n_train = self.came[0].shape
        perm, came = [], [np.zeros_like(a) for a in self.came]
        for g in range(groups):
            for t in range(n_train):
                z, x, c = t // (XS * CORES), t // CORES % XS, t % CORES
                to_g, z, x, c = turn(g, z, x, c)
                to_t = (z * XS + x) * CORES + c
                perm.append((g * n_train + t, to_g * n_train + to_t))
                for here, there in zip(self.came, came):
                    there[to_g, to_t] = here[g, t]
        return Blocks(lax.ppermute(self.array, ("group", "train"), perm), came)

    def columns(self, start, stop):
        return Blocks(self.array[:, start:stop], self.came)


def stack(*parts):
    return Blocks(jnp.concatenate([a.array for a in parts], axis=0), sum((a.came for a in parts), []))


def beside(left, right):
    assert all((a == b).all() for a, b in zip(left.came, right.came))
    return Blocks(jnp.concatenate([left.array, right.array], axis=1), left.came)


def after(kernel_result, *parts):
    arrays, kernel_result = lax.optimization_barrier(([a.array for a in parts], kernel_result))
    return kernel_result, *(Blocks(array, a.came) for array, a in zip(arrays, parts))


def over_core(g, z, x, c):
    return g, z, x, c ^ 1


def over_x(g, z, x, c):
    return g, z, x ^ 1, c


def over_z(g, z, x, c):
    return g, z ^ 1, x, c


def far_z(pair):
    return lambda g, z, x, c: (g, z ^ (2 * pair + (g == c)), x, c)


def over_group(g, z, x, c):
    return g ^ 1, z, x, c


def spread_lines(q_ref, lines_ref):
    q_rows, lines, _ = q_ref.shape
    pitch = lines_ref.shape[0] // q_rows
    for q in range(q_rows):
        lines_ref[q * pitch : q * pitch + lines, :] = q_ref[q].astype(jnp.float32)


def precond_kernel(q_ref, in_ref, out_ref, eig_ref, block_ref, *refs):
    made, (lines_ref, wide_ref, tall_ref, even_ref) = refs[:-4], refs[-4:]
    spread_lines(q_ref, lines_ref)
    for layer in range(in_ref.shape[0]):
        factors = prepare_layer(layer, in_ref, out_ref, eig_ref, even_ref.at[layer])
        for ref, factor in zip(made, factors):
            ref[layer] = factor
        precond_layer(layer, factors, lines_ref, block_ref, wide_ref.at[layer], tall_ref.at[layer])


def later_kernel(q_ref, *refs):
    made, (block_ref, lines_ref, wide_ref, tall_ref) = refs[:-4], refs[-4:]
    spread_lines(q_ref, lines_ref)
    for layer in range(wide_ref.shape[0]):
        factors = [ref[layer] for ref in made]
        precond_layer(layer, factors, lines_ref, block_ref, wide_ref.at[layer], tall_ref.at[layer])


def prepare_layer(layer, in_ref, out_ref, eig_ref, even_ref):
    width = eig_ref.shape[1]
    rows = width // LANES
    p_out = out_ref.shape[2]
    left = lax.broadcasted_iota(jnp.int32, (1, LANES), 1) < p_out

    eig = eig_ref[layer : layer + 1, :]
    damping = 0.1 / width * jnp.sum(eig, axis=1, keepdims=True)
    for j in range(rows):
        pair = eig[:, j * LANES : (j + 1) * LANES]
        turned = pltpu.roll(pair, p_out, 1)
        even_ref[2 * j : 2 * j + 1, :] = jnp.where(left, pair, turned)
        even_ref[2 * j + 1 : 2 * j + 2, :] = jnp.where(left, turned, pair)
    scale = 1.0 / (even_ref[...] + damping)

    by_row = [in_ref[layer, pl.ds(p, rows, stride=2), :] for p in range(2)]
    back_left = jnp.concatenate(by_row, axis=0)
    fore_left = jnp.concatenate(by_row, axis=1)
    back_high, back_low = halves(back_left)
    fore_high, fore_low = halves(fore_left)
    fore = jnp.concatenate([fore_high, fore_high, fore_low], axis=0)
    back = jnp.concatenate([back_high, back_high, back_low], axis=1)

    basis = out_ref[layer]
    empty = jnp.zeros((p_out, p_out), jnp.bfloat16)

    def twice(a):
        return jnp.concatenate(
            [jnp.concatenate([a, empty], axis=1), jnp.concatenate([empty, a], axis=1)], axis=0
        )

    right_high, right_low = halves(basis)
    turned_high, turned_low = halves(basis.T)
    fore_right = jnp.concatenate([twice(right_high), twice(right_low)], axis=1)
    back_high, back_low = twice(turned_high), twice(turned_low)
    back_right = jnp.concatenate(
        [
            jnp.concatenate([back_high, back_low], axis=1),
            jnp.concatenate([back_high, jnp.zeros_like(back_low)], axis=1),
        ],
        axis=0,
    )
    return scale, fore, back, fore_right, back_right


def precond_layer(layer, factors, lines_ref, block_ref, wide_ref, tall_ref):
    scale, fore, back, fore_right, back_right = factors
    q_rows = block_ref.shape[0]
    width = wide_ref.shape[0] * LANES // q_rows
    layers = block_ref.shape[1] // width
    rows = width // LANES
    pitch = lines_ref.shape[0] // q_rows
    p_in = scale.shape[0]
    p_out = width // p_in
    left = lax.broadcasted_iota(jnp.int32, (1, LANES), 1) < p_out

    stacked = jnp.concatenate(
        [lines_ref[pl.ds(layers * j + layer, q_rows, stride=pitch), :] for j in range(rows)], axis=0
    ).astype(jnp.bfloat16)
    both = mxu(stacked, fore_right)
    wide_ref[...] = both[:, :LANES] + both[:, LANES:]
    by_query = jnp.concatenate([wide_ref[pl.ds(q, rows, stride=q_rows), :] for q in range(q_rows)], axis=1)
    high, low = halves(by_query)
    both = mxu(fore, jnp.concatenate([high, low, high], axis=0), TN)
    every = jnp.concatenate([left] * q_rows, axis=1)
    rotated = jnp.where(every, both[:p_in], both[p_in:])
    rotated = jnp.concatenate(
        [
            part + pltpu.roll(part, p_out, 1)
            for part in (rotated[:, q * LANES : (q + 1) * LANES] for q in range(q_rows))
        ],
        axis=1,
    )
    scaled = rotated * jnp.concatenate([scale] * q_rows, axis=1)
    high, low = halves(scaled)
    both = mxu(back, jnp.concatenate([high, low, high], axis=0))
    mixed = jnp.where(every, both[:rows], both[rows:])
    stacked = jnp.concatenate([mixed[:, q * LANES : (q + 1) * LANES] for q in range(q_rows)], axis=0)
    both = mxu(jnp.concatenate(halves(stacked), axis=1), back_right)
    tall_ref[...] = both[:, :LANES] + both[:, LANES:]
    for j in range(rows):
        block = tall_ref[pl.ds(j, q_rows, stride=rows), :]
        column = layer * width + j * LANES
        block_ref[:, column : column + LANES] = block.astype(jnp.bfloat16)


def by_lines(array):
    rows, layers, width = array.shape
    array = array.reshape(rows, layers, width // LANES, LANES)
    return array.transpose(0, 2, 1, 3).reshape(rows, -1, LANES)


def block_scratch(q_rows, layers, width):
    lines = layers * width // LANES
    return [pltpu.VMEM((q_rows * (lines + 8), LANES), jnp.float32)] + [
        pltpu.VMEM((layers, q_rows * width // LANES, LANES), jnp.float32)
    ] * 2


def precondition(queries, basis_in, basis_out, eigvals):
    q_rows = queries.shape[0]
    layers, width = eigvals.shape
    p_in, rows = basis_in.shape[1], width // LANES
    operands = [in_hbm(a) for a in (queries, basis_in, basis_out, eigvals)]
    shapes = [(p_in, LANES), (3 * rows, 2 * p_in), (2 * rows, 3 * p_in), (LANES, 2 * LANES), (2 * LANES, 2 * LANES)]
    types = [jnp.float32] + [jnp.bfloat16] * 4
    block, *factors = pl.pallas_call(
        functools.partial(fetched, len(operands), precond_kernel),
        out_shape=[jax.ShapeDtypeStruct((q_rows, layers * width), jnp.bfloat16)]
        + [jax.ShapeDtypeStruct((layers, *shape), dtype) for shape, dtype in zip(shapes, types)],
        in_specs=[pl.BlockSpec(memory_space=pltpu.HBM)] * len(operands),
        out_specs=[VMEM] * 6,
        scratch_shapes=block_scratch(q_rows, layers, width)
        + [pltpu.VMEM((layers, 2 * rows, LANES), jnp.float32)]
        + [pltpu.VMEM(a.shape, a.dtype) for a in operands]
        + [pltpu.SemaphoreType.DMA((len(operands),))],
        compiler_params=pltpu.CompilerParams(vmem_limit_bytes=16 * MIB),
        cost_estimate=pl.CostEstimate(flops=10**9, bytes_accessed=4 * MIB, transcendentals=0),
        name="precond",
    )(*operands)
    return block, factors


def precondition_more(queries, factors):
    q_rows, lines, _ = queries.shape
    layers = factors[0].shape[0]
    operands = [queries, *factors]
    return pl.pallas_call(
        later_kernel,
        out_shape=jax.ShapeDtypeStruct((q_rows, lines * LANES), jnp.bfloat16),
        in_specs=[VMEM] * len(operands),
        out_specs=VMEM,
        scratch_shapes=block_scratch(q_rows, layers, lines * LANES // layers),
        compiler_params=pltpu.CompilerParams(vmem_limit_bytes=16 * MIB),
        cost_estimate=pl.CostEstimate(flops=10**9, bytes_accessed=4 * MIB, transcendentals=0),
        name="precond",
    )(*operands)


def fetched(n, body, *refs):
    operands, others = refs[:n], refs[n:]
    others, here, sems = others[: -n - 1], others[-n - 1 : -1], others[-1]
    copies = [pltpu.make_async_copy(a, b, sems.at[i]) for i, (a, b) in enumerate(zip(operands, here))]
    for copy in copies:
        copy.start()
    for copy in copies:
        copy.wait()
    body(*here, *others)


def split_kernel(layers, t_ref, slabs_ref, here_ref, wide_ref, sems):
    rows, chunks = BLOCK, sems.shape[0]
    lines = t_ref.shape[1]
    pitch = wide_ref.shape[0] // rows
    chunk = t_ref.shape[0] // chunks
    copies = [
        pltpu.make_async_copy(
            t_ref.at[pl.ds(i * chunk, chunk)], here_ref.at[pl.ds(i * chunk, chunk)], sems.at[i]
        )
        for i in range(chunks)
    ]
    for copy in copies:
        copy.start()
    for i in range(chunks):
        copies[i].wait()

        @pl.loop(i * chunk // rows, (i + 1) * chunk // rows)
        def _(block):
            at = pl.multiple_of(block * rows, rows)
            for row in range(rows):
                wide_ref[row * pitch : row * pitch + lines, :] = here_ref[at + row].astype(jnp.float32)
            for line in range(lines):
                slab = (line % layers) * (lines // layers) + line // layers
                slabs_ref[slab, pl.ds(at, rows), :] = wide_ref[pl.ds(line, rows, stride=pitch), :].astype(jnp.bfloat16)


def split_layers(train_grads):
    tr_rows, layers, width = train_grads.shape
    lines = layers * width // LANES
    return pl.pallas_call(
        functools.partial(split_kernel, layers),
        out_shape=jax.ShapeDtypeStruct((lines, tr_rows, LANES), jnp.bfloat16),
        in_specs=[pl.BlockSpec(memory_space=pltpu.HBM)],
        out_specs=VMEM,
        scratch_shapes=[
            pltpu.VMEM((tr_rows, lines, LANES), jnp.bfloat16),
            pltpu.VMEM((BLOCK * (lines + 8), LANES), jnp.float32),
            pltpu.SemaphoreType.DMA((8,)),
        ],
        compiler_params=pltpu.CompilerParams(vmem_limit_bytes=20 * MIB),
        cost_estimate=pl.CostEstimate(flops=10**9, bytes_accessed=16 * MIB, transcendentals=0),
        name="split",
    )(in_hbm(by_lines(train_grads)))


def score_kernel(masks, slabs_ref, *refs):
    blocks, out_ref = refs[:-1], refs[-1]
    slabs = slabs_ref.shape[0]
    q_rows = out_ref.shape[1] // len(masks)
    n_query = out_ref.shape[1]
    step = min(slabs, 8)
    total = None
    for at in range(0, slabs, step):
        train = jnp.concatenate([slabs_ref[at + i] for i in range(step)], axis=1)
        columns = slice(at * LANES, (at + step) * LANES)
        block = jnp.concatenate([ref[:, columns] for ref in blocks], axis=0)
        term = mxu(train, block, NT)
        total = term if total is None else total + term

    me, g = lax.axis_index("train"), lax.axis_index("group")
    row = lax.broadcasted_iota(jnp.int32, (q_rows, n_query), 0)
    query = lax.broadcasted_iota(jnp.int32, (q_rows, n_query), 1)
    order = []
    for mask in masks:
        c0, c1 = (jnp.where(g == 0, mask[0][c], mask[1][c]) for c in range(CORES))
        source = me ^ jnp.where(me % CORES == 0, c0, c1)
        order.append(jnp.where(query == source * q_rows + row, 1.0, 0.0))
    order = jnp.concatenate(order, axis=0).astype(jnp.bfloat16)
    high, low = halves(total)
    lowest = (total - high.astype(jnp.float32) - low.astype(jnp.float32)).astype(jnp.bfloat16)
    out_ref[...] = mxu(high, order) + mxu(low, order) + mxu(lowest, order)


def came_masks(came):
    xors = came ^ np.arange(came.shape[1])[None]
    masks = [[int(xors[g, c]) for c in range(CORES)] for g in range(GROUPS)]
    assert all((xors[g, c::CORES] == masks[g][c]).all() for g in range(GROUPS) for c in range(CORES))
    return masks


def per_device(n_train, train_grads, query_grads, basis_in, basis_out, eigvals):
    zs = n_train // (XS * CORES)
    rest = basis_in, basis_out, eigvals
    queries = by_lines(query_grads)
    places = [np.tile(np.arange(n_train), (GROUPS, 1))]
    far = [Blocks(queries, places).hop(far_z(pair)) for pair in range(1, zs // 2)]
    block, factors = precondition(queries, *rest)
    own = Blocks(block, places)
    q_rows, width = own.array.shape
    n_query = n_train * q_rows
    cut = 5 * width // 8
    at_x = own.hop(over_x)
    twin = own.hop(over_core)
    train_grads, own = after(train_grads, own)
    slabs = split_layers(train_grads)
    slabs, own = after(slabs, own)
    at_z = own.hop(over_z)
    parts = [own, twin, at_x, at_z]
    for pair, one in enumerate(far):
        slabs, one = after(slabs, one)
        one = Blocks(precondition_more(one.array, factors), one.came)
        by_x, by_group = one.hop(over_x), one.hop(over_group)
        parts.append(one)
        if pair == 0:
            one.array, at_x = after(one.array, at_x)
            at_xz = at_x.hop(over_z)
            stacked = stack(at_x, one)
            stacked.array, by_x = after(stacked.array, by_x)
            parts += [at_xz, stacked.hop(over_core)]
        else:
            parts.append(one.hop(over_core))
        parts += [by_x, by_group, stack(by_x, by_group).hop(over_core)]
        half = by_x.columns(0, cut).hop(over_group)
        if pair == 0:
            half.array, near, near_x = after(half.array, at_z, at_xz)
            parts.append(stack(near, near_x).hop(over_core))
        corner = beside(half, by_group.columns(cut, width).hop(over_x))
        parts += [corner, corner.hop(over_core)]

    tr_rows = train_grads.shape[0]
    operands = [slabs] + [a.array for a in parts]
    partial_scores = pl.pallas_call(
        functools.partial(score_kernel, [came_masks(came) for a in parts for came in a.came]),
        out_shape=jax.ShapeDtypeStruct((tr_rows, n_query), jnp.float32),
        in_specs=[VMEM] * len(operands),
        out_specs=VMEM,
        compiler_params=pltpu.CompilerParams(vmem_limit_bytes=32 * MIB),
        cost_estimate=pl.CostEstimate(
            flops=2 * tr_rows * n_query * width, bytes_accessed=2 * width * (tr_rows + n_query), transcendentals=0
        ),
        name="scores",
    )(*operands)
    return lax.psum_scatter(partial_scores, "layer", scatter_dimension=1, tiled=True)


def solution(mesh):
    return jax.shard_map(
        functools.partial(per_device, mesh.shape["train"]),
        mesh=mesh,
        in_specs=(
            P(("group", "train"), "layer", None),
            P("train", "layer", None),
            P("layer", None, None),
            P("layer", None, None),
            P("layer", None),
        ),
        out_specs=P(("group", "train"), "layer"),
        check_vma=False,
    )
```

```python
import functools

import jax
import jax.numpy as jnp
import numpy as np
from jax import lax
from jax.experimental import pallas as pl
from jax.experimental.pallas import tpu as pltpu
from jax.sharding import PartitionSpec as P

CORES = 2
XS = 2
GROUPS = 2
LANES = 128
BLOCK = 16
MIB = 1024 * 1024
VMEM = pl.BlockSpec(memory_space=pltpu.VMEM)
NN = (((1,), (0,)), ((), ()))
NT = (((1,), (1,)), ((), ()))
TN = (((0,), (0,)), ((), ()))


def mxu(a, b, dims=NN):
    return lax.dot_general(a, b, dims, preferred_element_type=jnp.float32)


def halves(a):
    high = a.astype(jnp.bfloat16)
    return high, (a - high.astype(jnp.float32)).astype(jnp.bfloat16)


def in_hbm(array):
    return pltpu.with_memory_space_constraint(array, pltpu.HBM)


class Blocks:
    def __init__(self, array, came):
        self.array, self.came = array, came

    def hop(self, turn):
        groups, n_train = self.came[0].shape
        perm, came = [], [np.zeros_like(a) for a in self.came]
        for g in range(groups):
            for t in range(n_train):
                z, x, c = t // (XS * CORES), t // CORES % XS, t % CORES
                to_g, z, x, c = turn(g, z, x, c)
                to_t = (z * XS + x) * CORES + c
                perm.append((g * n_train + t, to_g * n_train + to_t))
                for here, there in zip(self.came, came):
                    there[to_g, to_t] = here[g, t]
        return Blocks(lax.ppermute(self.array, ("group", "train"), perm), came)

    def columns(self, start, stop):
        return Blocks(self.array[:, start:stop], self.came)


def stack(*parts):
    return Blocks(jnp.concatenate([a.array for a in parts], axis=0), sum((a.came for a in parts), []))


def beside(left, right):
    assert all((a == b).all() for a, b in zip(left.came, right.came))
    return Blocks(jnp.concatenate([left.array, right.array], axis=1), left.came)


def after(kernel_result, *parts):
    arrays, kernel_result = lax.optimization_barrier(([a.array for a in parts], kernel_result))
    return kernel_result, *(Blocks(array, a.came) for array, a in zip(arrays, parts))


def over_core(g, z, x, c):
    return g, z, x, c ^ 1


def over_x(g, z, x, c):
    return g, z, x ^ 1, c


def over_z(g, z, x, c):
    return g, z ^ 1, x, c


def far_z(pair):
    return lambda g, z, x, c: (g, z ^ (2 * pair + (g == c)), x, c)


def over_group(g, z, x, c):
    return g ^ 1, z, x, c


def spread_lines(q_ref, lines_ref):
    q_rows, lines, _ = q_ref.shape
    pitch = lines_ref.shape[0] // q_rows
    for q in range(q_rows):
        lines_ref[q * pitch : q * pitch + lines, :] = q_ref[q].astype(jnp.float32)


def precond_kernel(q_ref, in_ref, out_ref, eig_ref, block_ref, *refs):
    made, (lines_ref, wide_ref, tall_ref, even_ref) = refs[:-4], refs[-4:]
    spread_lines(q_ref, lines_ref)
    for layer in range(in_ref.shape[0]):
        factors = prepare_layer(layer, in_ref, out_ref, eig_ref, even_ref.at[layer])
        for ref, factor in zip(made, factors):
            ref[layer] = factor
        precond_layer(layer, factors, lines_ref, block_ref, wide_ref.at[layer], tall_ref.at[layer])


def later_kernel(q_ref, *refs):
    made, (block_ref, lines_ref, wide_ref, tall_ref) = refs[:-4], refs[-4:]
    spread_lines(q_ref, lines_ref)
    for layer in range(wide_ref.shape[0]):
        factors = [ref[layer] for ref in made]
        precond_layer(layer, factors, lines_ref, block_ref, wide_ref.at[layer], tall_ref.at[layer])


def prepare_layer(layer, in_ref, out_ref, eig_ref, even_ref):
    width = eig_ref.shape[1]
    rows = width // LANES
    p_out = out_ref.shape[2]
    left = lax.broadcasted_iota(jnp.int32, (1, LANES), 1) < p_out

    eig = eig_ref[layer : layer + 1, :]
    damping = 0.1 / width * jnp.sum(eig, axis=1, keepdims=True)
    for j in range(rows):
        pair = eig[:, j * LANES : (j + 1) * LANES]
        turned = pltpu.roll(pair, p_out, 1)
        even_ref[2 * j : 2 * j + 1, :] = jnp.where(left, pair, turned)
        even_ref[2 * j + 1 : 2 * j + 2, :] = jnp.where(left, turned, pair)
    scale = 1.0 / (even_ref[...] + damping)

    by_row = [in_ref[layer, pl.ds(p, rows, stride=2), :] for p in range(2)]
    back_left = jnp.concatenate(by_row, axis=0)
    fore_left = jnp.concatenate(by_row, axis=1)
    back_high, back_low = halves(back_left)
    fore_high, fore_low = halves(fore_left)
    fore = jnp.concatenate([fore_high, fore_high, fore_low], axis=0)
    back = jnp.concatenate([back_high, back_high, back_low], axis=1)

    basis = out_ref[layer]
    empty = jnp.zeros((p_out, p_out), jnp.bfloat16)

    def twice(a):
        return jnp.concatenate(
            [jnp.concatenate([a, empty], axis=1), jnp.concatenate([empty, a], axis=1)], axis=0
        )

    right_high, right_low = halves(basis)
    turned_high, turned_low = halves(basis.T)
    fore_right = jnp.concatenate([twice(right_high), twice(right_low)], axis=1)
    back_high, back_low = twice(turned_high), twice(turned_low)
    back_right = jnp.concatenate(
        [
            jnp.concatenate([back_high, back_low], axis=1),
            jnp.concatenate([back_high, jnp.zeros_like(back_low)], axis=1),
        ],
        axis=0,
    )
    return scale, fore, back, fore_right, back_right


def precond_layer(layer, factors, lines_ref, block_ref, wide_ref, tall_ref):
    scale, fore, back, fore_right, back_right = factors
    q_rows = block_ref.shape[0]
    width = wide_ref.shape[0] * LANES // q_rows
    layers = block_ref.shape[1] // width
    rows = width // LANES
    pitch = lines_ref.shape[0] // q_rows
    p_in = scale.shape[0]
    p_out = width // p_in
    left = lax.broadcasted_iota(jnp.int32, (1, LANES), 1) < p_out

    stacked = jnp.concatenate(
        [lines_ref[pl.ds(layers * j + layer, q_rows, stride=pitch), :] for j in range(rows)], axis=0
    ).astype(jnp.bfloat16)
    both = mxu(stacked, fore_right)
    wide_ref[...] = both[:, :LANES] + both[:, LANES:]
    by_query = jnp.concatenate([wide_ref[pl.ds(q, rows, stride=q_rows), :] for q in range(q_rows)], axis=1)
    high, low = halves(by_query)
    both = mxu(fore, jnp.concatenate([high, low, high], axis=0), TN)
    every = jnp.concatenate([left] * q_rows, axis=1)
    rotated = jnp.where(every, both[:p_in], both[p_in:])
    rotated = jnp.concatenate(
        [
            part + pltpu.roll(part, p_out, 1)
            for part in (rotated[:, q * LANES : (q + 1) * LANES] for q in range(q_rows))
        ],
        axis=1,
    )
    scaled = rotated * jnp.concatenate([scale] * q_rows, axis=1)
    high, low = halves(scaled)
    both = mxu(back, jnp.concatenate([high, low, high], axis=0))
    mixed = jnp.where(every, both[:rows], both[rows:])
    stacked = jnp.concatenate([mixed[:, q * LANES : (q + 1) * LANES] for q in range(q_rows)], axis=0)
    both = mxu(jnp.concatenate(halves(stacked), axis=1), back_right)
    tall_ref[...] = both[:, :LANES] + both[:, LANES:]
    for j in range(rows):
        block = tall_ref[pl.ds(j, q_rows, stride=rows), :]
        column = layer * width + j * LANES
        block_ref[:, column : column + LANES] = block.astype(jnp.bfloat16)


def by_lines(array):
    rows, layers, width = array.shape
    array = array.reshape(rows, layers, width // LANES, LANES)
    return array.transpose(0, 2, 1, 3).reshape(rows, -1, LANES)


def block_scratch(q_rows, layers, width):
    lines = layers * width // LANES
    return [pltpu.VMEM((q_rows * (lines + 8), LANES), jnp.float32)] + [
        pltpu.VMEM((layers, q_rows * width // LANES, LANES), jnp.float32)
    ] * 2


def precondition(queries, basis_in, basis_out, eigvals):
    q_rows = queries.shape[0]
    layers, width = eigvals.shape
    p_in, rows = basis_in.shape[1], width // LANES
    operands = [in_hbm(a) for a in (queries, basis_in, basis_out, eigvals)]
    shapes = [(p_in, LANES), (3 * rows, 2 * p_in), (2 * rows, 3 * p_in), (LANES, 2 * LANES), (2 * LANES, 2 * LANES)]
    types = [jnp.float32] + [jnp.bfloat16] * 4
    block, *factors = pl.pallas_call(
        functools.partial(fetched, len(operands), precond_kernel),
        out_shape=[jax.ShapeDtypeStruct((q_rows, layers * width), jnp.bfloat16)]
        + [jax.ShapeDtypeStruct((layers, *shape), dtype) for shape, dtype in zip(shapes, types)],
        in_specs=[pl.BlockSpec(memory_space=pltpu.HBM)] * len(operands),
        out_specs=[VMEM] * 6,
        scratch_shapes=block_scratch(q_rows, layers, width)
        + [pltpu.VMEM((layers, 2 * rows, LANES), jnp.float32)]
        + [pltpu.VMEM(a.shape, a.dtype) for a in operands]
        + [pltpu.SemaphoreType.DMA((len(operands),))],
        compiler_params=pltpu.CompilerParams(vmem_limit_bytes=16 * MIB),
        cost_estimate=pl.CostEstimate(flops=10**9, bytes_accessed=4 * MIB, transcendentals=0),
        name="precond",
    )(*operands)
    return block, factors


def precondition_more(queries, factors):
    q_rows, lines, _ = queries.shape
    layers = factors[0].shape[0]
    operands = [queries, *factors]
    return pl.pallas_call(
        later_kernel,
        out_shape=jax.ShapeDtypeStruct((q_rows, lines * LANES), jnp.bfloat16),
        in_specs=[VMEM] * len(operands),
        out_specs=VMEM,
        scratch_shapes=block_scratch(q_rows, layers, lines * LANES // layers),
        compiler_params=pltpu.CompilerParams(vmem_limit_bytes=16 * MIB),
        cost_estimate=pl.CostEstimate(flops=10**9, bytes_accessed=4 * MIB, transcendentals=0),
        name="precond",
    )(*operands)


def fetched(n, body, *refs):
    operands, others = refs[:n], refs[n:]
    others, here, sems = others[: -n - 1], others[-n - 1 : -1], others[-1]
    copies = [pltpu.make_async_copy(a, b, sems.at[i]) for i, (a, b) in enumerate(zip(operands, here))]
    for copy in copies:
        copy.start()
    for copy in copies:
        copy.wait()
    body(*here, *others)


def split_kernel(layers, t_ref, slabs_ref, here_ref, wide_ref, sems):
    rows, chunks = BLOCK, sems.shape[0]
    lines = t_ref.shape[1]
    pitch = wide_ref.shape[0] // rows
    chunk = t_ref.shape[0] // chunks
    copies = [
        pltpu.make_async_copy(
            t_ref.at[pl.ds(i * chunk, chunk)], here_ref.at[pl.ds(i * chunk, chunk)], sems.at[i]
        )
        for i in range(chunks)
    ]
    for copy in copies:
        copy.start()
    for i in range(chunks):
        copies[i].wait()

        @pl.loop(i * chunk // rows, (i + 1) * chunk // rows)
        def _(block):
            at = pl.multiple_of(block * rows, rows)
            for row in range(rows):
                wide_ref[row * pitch : row * pitch + lines, :] = here_ref[at + row].astype(jnp.float32)
            for line in range(lines):
                slab = (line % layers) * (lines // layers) + line // layers
                slabs_ref[slab, pl.ds(at, rows), :] = wide_ref[pl.ds(line, rows, stride=pitch), :].astype(jnp.bfloat16)


def split_layers(train_grads):
    tr_rows, layers, width = train_grads.shape
    lines = layers * width // LANES
    return pl.pallas_call(
        functools.partial(split_kernel, layers),
        out_shape=jax.ShapeDtypeStruct((lines, tr_rows, LANES), jnp.bfloat16),
        in_specs=[pl.BlockSpec(memory_space=pltpu.HBM)],
        out_specs=VMEM,
        scratch_shapes=[
            pltpu.VMEM((tr_rows, lines, LANES), jnp.bfloat16),
            pltpu.VMEM((BLOCK * (lines + 8), LANES), jnp.float32),
            pltpu.SemaphoreType.DMA((8,)),
        ],
        compiler_params=pltpu.CompilerParams(vmem_limit_bytes=20 * MIB),
        cost_estimate=pl.CostEstimate(flops=10**9, bytes_accessed=16 * MIB, transcendentals=0),
        name="split",
    )(in_hbm(by_lines(train_grads)))


def score_kernel(masks, slabs_ref, *refs):
    blocks, out_ref = refs[:-1], refs[-1]
    slabs = slabs_ref.shape[0]
    q_rows = out_ref.shape[1] // len(masks)
    n_query = out_ref.shape[1]
    step = min(slabs, 32)
    total = None
    for at in range(0, slabs, step):
        train = jnp.concatenate([slabs_ref[at + i] for i in range(step)], axis=1)
        columns = slice(at * LANES, (at + step) * LANES)
        block = jnp.concatenate([ref[:, columns] for ref in blocks], axis=0)
        term = mxu(train, block, NT)
        total = term if total is None else total + term

    me, g = lax.axis_index("train"), lax.axis_index("group")
    row = lax.broadcasted_iota(jnp.int32, (q_rows, n_query), 0)
    query = lax.broadcasted_iota(jnp.int32, (q_rows, n_query), 1)
    order = []
    for mask in masks:
        c0, c1 = (jnp.where(g == 0, mask[0][c], mask[1][c]) for c in range(CORES))
        source = me ^ jnp.where(me % CORES == 0, c0, c1)
        order.append(jnp.where(query == source * q_rows + row, 1.0, 0.0))
    order = jnp.concatenate(order, axis=0).astype(jnp.bfloat16)
    high, low = halves(total)
    lowest = (total - high.astype(jnp.float32) - low.astype(jnp.float32)).astype(jnp.bfloat16)
    out_ref[...] = mxu(high, order) + mxu(low, order) + mxu(lowest, order)


def came_masks(came):
    xors = came ^ np.arange(came.shape[1])[None]
    masks = [[int(xors[g, c]) for c in range(CORES)] for g in range(GROUPS)]
    assert all((xors[g, c::CORES] == masks[g][c]).all() for g in range(GROUPS) for c in range(CORES))
    return masks


def per_device(n_train, train_grads, query_grads, basis_in, basis_out, eigvals):
    zs = n_train // (XS * CORES)
    rest = basis_in, basis_out, eigvals
    queries = by_lines(query_grads)
    places = [np.tile(np.arange(n_train), (GROUPS, 1))]
    far = [Blocks(queries, places).hop(far_z(pair)) for pair in range(1, zs // 2)]
    block, factors = precondition(queries, *rest)
    own = Blocks(block, places)
    q_rows, width = own.array.shape
    n_query = n_train * q_rows
    cut = 5 * width // 8
    at_x = own.hop(over_x)
    twin = own.hop(over_core)
    train_grads, own = after(train_grads, own)
    slabs = split_layers(train_grads)
    slabs, own = after(slabs, own)
    at_z = own.hop(over_z)
    parts = [own, twin, at_x, at_z]
    for pair, one in enumerate(far):
        slabs, one = after(slabs, one)
        one = Blocks(precondition_more(one.array, factors), one.came)
        by_x, by_group = one.hop(over_x), one.hop(over_group)
        parts.append(one)
        if pair == 0:
            one.array, at_x = after(one.array, at_x)
            at_xz = at_x.hop(over_z)
            stacked = stack(at_x, one)
            stacked.array, by_x = after(stacked.array, by_x)
            parts += [at_xz, stacked.hop(over_core)]
        else:
            parts.append(one.hop(over_core))
        parts += [by_x, by_group, stack(by_x, by_group).hop(over_core)]
        half = by_x.columns(0, cut).hop(over_group)
        if pair == 0:
            half.array, near, near_x = after(half.array, at_z, at_xz)
            parts.append(stack(near, near_x).hop(over_core))
        corner = beside(half, by_group.columns(cut, width).hop(over_x))
        parts += [corner, corner.hop(over_core)]

    tr_rows = train_grads.shape[0]
    operands = [slabs] + [a.array for a in parts]
    partial_scores = pl.pallas_call(
        functools.partial(score_kernel, [came_masks(came) for a in parts for came in a.came]),
        out_shape=jax.ShapeDtypeStruct((tr_rows, n_query), jnp.float32),
        in_specs=[VMEM] * len(operands),
        out_specs=VMEM,
        compiler_params=pltpu.CompilerParams(vmem_limit_bytes=32 * MIB),
        cost_estimate=pl.CostEstimate(
            flops=2 * tr_rows * n_query * width, bytes_accessed=2 * width * (tr_rows + n_query), transcendentals=0
        ),
        name="scores",
    )(*operands)
    return lax.psum_scatter(partial_scores, "layer", scatter_dimension=1, tiled=True)


def solution(mesh):
    return jax.shard_map(
        functools.partial(per_device, mesh.shape["train"]),
        mesh=mesh,
        in_specs=(
            P(("group", "train"), "layer", None),
            P("train", "layer", None),
            P("layer", None, None),
            P("layer", None, None),
            P("layer", None),
        ),
        out_specs=P(("group", "train"), "layer"),
        check_vma=False,
    )
```
